128 devices in a mesh: lat: 4 (over z), lon: 32 (over x, y, core).
Axes of the slice: x: 4, y: 4, z: 4, core: 2. Of those that a mesh axis runs over, the one named last changes fastest.
Arguments:
- obs_values: bfloat16 [524288, 128], P(('lat', 'lon')), may hold values from -6 to 6
- obs_cells: int32 [524288], P(('lat', 'lon')), may hold values from 0 to 2047
- obs_subcell: int32 [524288], P(('lat', 'lon')), may hold values from 0 to 63
- slot_counts: int32 [128, 128], P(('lat', 'lon')), may hold values from 1 to 32, as said below
- sharpness: float32 [256], replicated, may hold values from 0.3 to 30
- embed_weight: bfloat16 [128, 256], replicated, may hold values from -0.5 to 0.5
- conv_weight: bfloat16 [2, 3, 3, 256, 256], replicated, may hold values from -0.125 to 0.125
- cotangent: bfloat16 [64, 4096, 256], P('lat', 'lon'), may hold values from -6 to 6
Outputs:
- encoded: bfloat16 [64, 4096, 256], P('lat', 'lon')
- value_grads: bfloat16 [524288, 128], P(('lat', 'lon'))
- conv_grads: float32 [2, 3, 3, 256, 256], replicated
- embed_grads: float32 [128, 256], replicated
The draws below stay inside these ranges and needn't reach their ends.
Inputs may be any that keep to these rules, and one draw needn't show every extreme that they name: `slot_counts`: every source device fills all 32 slots for some destination tile; densities differ by tile.
All inputs are finite; a program needn't handle non-finite values.
Results may differ from the reference program's by a relative error of at most 0.009.
Values may be sent and summed in bfloat16 or wider, within the bound.
A program may use at most 128 MiB of HBM per device.

```python
import math
import jax
import jax.numpy as jnp
from jax import lax

C = 256
VALS = 128
TLAT = 16
TLON = 128
CAP = 32
SUBCELL = 8
NLAT = 64
NLON = 4096
OBS_ALL = 524288
N_LON = 32
DEVICES = 128


def draw_slot_counts(key, part):
    key = jax.random.fold_in(key, 7)
    key_level, key_drop, key_full = jax.random.split(key, 3)
    level = jnp.left_shift(jnp.int32(1), jax.random.randint(key_level, (1, DEVICES), 0, 3))
    base_count = CAP * level // 4
    dropped = jax.random.randint(key_drop, (DEVICES, DEVICES), 0, max(CAP // 4, 1))
    counts = jnp.maximum(base_count - dropped, 1)
    full_dest = jax.random.randint(key_full, (DEVICES, 1), 0, DEVICES)
    column = jnp.arange(DEVICES, dtype=jnp.int32)[None, :]
    counts = jnp.where(column == full_dest, CAP, counts)
    return counts.astype(jnp.int32)


def place_ends(array, key, low, high):
    longest = array.shape.index(max(array.shape))
    spots = []
    for shift in (0, 1):
        where = [jax.random.randint(jax.random.fold_in(key, axis), (), 0, length) for axis, length in enumerate(array.shape)]
        where[longest] = (where[longest] + shift) % array.shape[longest]
        spots.append(tuple(where))
    return array.at[spots[0]].set(low).at[spots[1]].set(high)


def level_of(rng, shape, shards, least, largest):
    gain, own = 1.0, jax.random.fold_in(rng, 6)
    for position, shards_of in shards:
        draws = jnp.exp(jax.random.uniform(jax.random.fold_in(own, position), (shards_of,), jnp.float32, least / len(shards), largest / len(shards)))
        gain = gain * jnp.repeat(draws, shape[position] // shards_of).reshape([-1 if axis == position else 1 for axis in range(len(shape))])
    return gain


def scatter_about(stream_key, shape, deviation, bound, cuts=(), kind=jnp.bfloat16):
    entries = deviation * jax.random.normal(stream_key, shape, jnp.float32)
    if cuts:
        entries = entries * level_of(stream_key, shape, cuts, -0.22, 0.18)
    return jnp.clip(entries, -bound, bound).astype(kind)


def setup_inputs(seed: int = 0) -> dict:
    arg_keys = jax.random.split(jax.random.key(seed), 9)
    obs_values = scatter_about(arg_keys[0], (OBS_ALL, VALS), 1.0, 6.0, ((0, 128),))
    obs_cells = place_ends(jax.random.randint(arg_keys[1], (OBS_ALL,), 0, TLAT * TLON), jax.random.fold_in(arg_keys[1], 1), 0, (TLAT * TLON) - 1).astype(jnp.int32)
    obs_subcell = place_ends(jax.random.randint(arg_keys[2], (OBS_ALL,), 0, SUBCELL * SUBCELL), jax.random.fold_in(arg_keys[2], 1), 0, (SUBCELL * SUBCELL) - 1).astype(jnp.int32)
    slot_counts = draw_slot_counts(jax.random.fold_in(arg_keys[8], 71), 0)
    sharpness = jnp.clip(jnp.exp(jax.random.uniform(arg_keys[4], (C,), jnp.float32, math.log(0.3), math.log(30.0))), 0.3, 30.0)
    embed_weight = scatter_about(arg_keys[5], (VALS, C), VALS ** -0.5, 0.5)
    conv_weight = scatter_about(arg_keys[6], (2, 3, 3, C, C), (9 * C) ** -0.5, 0.125)
    cotangent = scatter_about(arg_keys[7], (NLAT, NLON, C), 1.0, 6.0, ((0, 4), (1, 32)))
    return {"obs_values": obs_values, "obs_cells": obs_cells, "obs_subcell": obs_subcell, "slot_counts": slot_counts, "sharpness": sharpness, "embed_weight": embed_weight, "conv_weight": conv_weight, "cotangent": cotangent}


def widen_grid(field):
    field = jnp.concatenate([field[:, -1:], field, field[:, :1]], axis=1)
    return jnp.pad(field, ((1, 1), (0, 0), (0, 0)))

def apply_conv(padded, kernel):
    return lax.conv_general_dilated(padded.astype(jnp.float32)[None], kernel.astype(jnp.float32), (1, 1), 'VALID', dimension_numbers=('NHWC', 'HWIO', 'NHWC'), precision=lax.Precision.HIGHEST)[0]

def kernel_grad(padded, grad):
    height, breadth = (grad.shape[0], grad.shape[1])
    blocks = []
    for row_off in range(3):
        for col_off in range(3):
            window = padded[row_off:row_off + height, col_off:col_off + breadth].astype(jnp.float32)
            blocks.append(jnp.einsum('hwc,hwo->co', window, grad.astype(jnp.float32), precision=lax.Precision.HIGHEST))
    return jnp.stack(blocks).reshape(3, 3, padded.shape[2], grad.shape[2])

def flip_kernel(kernel):
    return jnp.flip(kernel, (0, 1)).transpose(0, 1, 3, 2)

def silu_slope(field):
    value = field.astype(jnp.float32)
    sig = jax.nn.sigmoid(value)
    return sig * (1.0 + value * (1.0 - sig))

def gauss_weight(sub_ids, live_mask, sharpness):
    off_row = ((sub_ids // SUBCELL).astype(jnp.float32) + 0.5) / SUBCELL - 0.5
    off_col = ((sub_ids % SUBCELL).astype(jnp.float32) + 0.5) / SUBCELL - 0.5
    radius = off_row * off_row + off_col * off_col
    return jnp.exp(-radius[:, None] * sharpness[None, :]) * live_mask.astype(jnp.float32)[:, None]

def reference(obs_values, obs_cells, obs_subcell, slot_counts, sharpness, embed_weight, conv_weight, cotangent):
    channels = cotangent.shape[2]
    val_width = obs_values.shape[1]
    cell_count = NLAT * NLON
    per_source = DEVICES * CAP
    values_all = obs_values.reshape(DEVICES, per_source, val_width)
    cells_all = obs_cells.reshape(DEVICES, DEVICES, CAP)
    subs_all = obs_subcell.reshape(DEVICES, per_source)
    dest = jnp.arange(DEVICES, dtype=jnp.int32)[:, None]
    slot_index = jnp.arange(CAP, dtype=jnp.int32)[None, :]

    def source_rows(counts, cell_ids, sub_ids):
        live_mask = (slot_index < counts[:, None]).astype(jnp.int32).reshape(per_source)
        lat_pos = dest // N_LON * TLAT + cell_ids // TLON
        lon_pos = dest % N_LON * TLON + cell_ids % TLON
        targets = (lat_pos * NLON + lon_pos).reshape(per_source).astype(jnp.int32)
        return (targets, gauss_weight(sub_ids, live_mask, sharpness))

    def place(carry, inputs):
        placed, density = carry
        vals, counts, cell_ids, sub_ids = inputs
        targets, weight = source_rows(counts, cell_ids, sub_ids)
        embedding = jnp.dot(vals, embed_weight, preferred_element_type=jnp.float32)
        return ((placed.at[targets].add(embedding * weight), density.at[targets].add(weight)), None)
    zeros = jnp.zeros((cell_count, channels), jnp.float32)
    inputs = (values_all, slot_counts, cells_all, subs_all)
    (placed, density), _ = lax.scan(place, (zeros, zeros), inputs)
    base_grid = (placed / (density + 1.0)).astype(jnp.bfloat16).reshape(NLAT, NLON, channels)
    act_zero = jax.nn.silu(base_grid.astype(jnp.float32)).astype(jnp.bfloat16)
    pad_zero = widen_grid(act_zero)
    middle = (base_grid.astype(jnp.float32) + apply_conv(pad_zero, conv_weight[0])).astype(jnp.bfloat16)
    act_one = jax.nn.silu(middle.astype(jnp.float32)).astype(jnp.bfloat16)
    pad_one = widen_grid(act_one)
    encoded = (middle.astype(jnp.float32) + apply_conv(pad_one, conv_weight[1])).astype(jnp.bfloat16)
    outer = kernel_grad(pad_one, cotangent)
    back_one = apply_conv(widen_grid(cotangent), flip_kernel(conv_weight[1]))
    grad_mid = (cotangent.astype(jnp.float32) + back_one * silu_slope(middle)).astype(jnp.bfloat16)
    inner = kernel_grad(pad_zero, grad_mid)
    back_zero = apply_conv(widen_grid(grad_mid), flip_kernel(conv_weight[0]))
    grad_base = grad_mid.astype(jnp.float32) + back_zero * silu_slope(base_grid)
    grad_placed = grad_base.reshape(cell_count, channels) / (density + 1.0)

    def retrace(carry, inputs):
        vals, counts, cell_ids, sub_ids = inputs
        targets, weight = source_rows(counts, cell_ids, sub_ids)
        grad_embed = (weight * grad_placed[targets]).astype(jnp.bfloat16)
        grad_vals = lax.dot_general(grad_embed, embed_weight, (((1,), (1,)), ((), ())), preferred_element_type=jnp.float32).astype(jnp.bfloat16)
        carry = carry + lax.dot_general(vals, grad_embed, (((0,), (0,)), ((), ())), preferred_element_type=jnp.float32)
        return (carry, grad_vals)
    embed_sum, value_grads = lax.scan(retrace, jnp.zeros((val_width, channels), jnp.float32), inputs)
    grad_scale = 1.0 / math.sqrt(NLAT * NLON)
    conv_grads = jnp.stack([inner, outer]) * grad_scale
    return (encoded, value_grads.reshape(DEVICES * per_source, val_width), conv_grads, embed_sum * grad_scale)
```

```python
import jax
import jax.numpy as jnp
from jax import lax
from jax.experimental import pallas as pl
from jax.experimental.pallas import tpu as pltpu
from jax.sharding import PartitionSpec as P

F32 = jnp.float32
BF16 = jnp.bfloat16
N_LAT, N_LON = 4, 32
DEVICES = N_LAT * N_LON
CAP, VALS, CH = 32, 128, 256
ROWS, COLS = 16, 128
CELLS = ROWS * COLS
OBS = DEVICES * CAP
GROUP = 32 * CAP
PART, HALF, QUARTER, SHARD = 1536, 768, 192, 48
NT = (((1,), (1,)), ((), ()))
TN = (((0,), (0,)), ((), ()))


def dot(a, b):
    return jnp.dot(a, b, preferred_element_type=F32)


def iota(shape, axis):
    return lax.broadcasted_iota(jnp.int32, shape, axis)


def sigmoid(x):
    return 1.0 / (1.0 + jnp.exp(-x))


def remote(src, dst, send, recv, lat, lon):
    return pltpu.make_async_remote_copy(
        src_ref=src,
        dst_ref=dst,
        send_sem=send,
        recv_sem=recv,
        device_id=(lat, lon),
        device_id_type=pl.DeviceIdType.MESH,
    )


def await_bytes(ref, sem):
    pltpu.make_async_copy(ref, ref, sem).wait()


def loop(low, high, body):
    def step(i, carry):
        body(i)
        return carry

    lax.fori_loop(low, high, step, 0)


def aligned(start, size, unit):
    return pl.ds(pl.multiple_of(start, unit), size)


def kernel(
    obs_in, meta_in, sharp, embed_w, conv_in, cot_in,
    enc_out, vg_out, grads_out, embed_out,
    vals, queue, relay, meta_z, meta_x, meta, tmeta, colb, rowb, weight, ew, rk, colhot, rowl, placed, counts, inv,
    cot, conv_w, conv_t, embed_t, back, base, act_zero, mid, act_one, gmid, gp, act_t, zero_t,
    x3_act, x3_cot, x3_mid, hrow, hcol, strip, stripf,
    vg, grads, total, p0, s1, p1, s2, p2, s3, p3, esum, pe, qe, etotal, enc,
    local_sem, pair_send, pair_recv, a2a_send, a2a_recv, meta_send, meta_recv, vg_send, vg_recv,
    halo_send, halo_recv, ar_send, ar_recv, em_send, em_recv,
):
    lat = lax.axis_index("lat")
    lon = lax.axis_index("lon")
    me = lat * N_LON + lon
    xi, yi, ci = lax.div(lon, 8), lax.rem(lax.div(lon, 2), 4), lax.rem(lon, 2)

    chip = lat * 16 + xi * 4 + yi
    yc = lax.rem(lon, 8)
    other_core = lon + 1 - 2 * ci

    def offset(j):
        g, dx, dy = lax.div(j, 16), lax.rem(lax.div(j, 4), 4), lax.rem(j, 4)
        return dx, dy, lax.rem(g + 8 - dx - dy, 4)

    cot_copy = pltpu.make_async_copy(cot_in, cot, local_sem.at[0])
    cot_copy.start()
    pair_own = pltpu.make_async_copy(obs_in.at[:, ci], queue.at[:, ci], local_sem.at[4])
    pair_own.start()
    pair_other = remote(
        obs_in.at[:, 1 - ci], queue.at[:, ci], pair_send.at[0], pair_recv.at[0], lat, other_core
    )
    pair_other.start()

    def meta_copies(stage):
        copies = []
        for d in range(1, 8 if stage == 2 else 4):
            if stage == 0:
                c = lax.rem(lat + d, 4)
                src, dst, target = meta_in.at[c], meta_z.at[lat], (c, lon)
            elif stage == 1:
                c = lax.rem(xi + d, 4)
                src, dst, target = meta_z.at[:, c], meta_x.at[xi], (lat, c * 8 + yc)
            else:
                c = lax.rem(yc + d, 8)
                src, dst, target = meta_x.at[:, :, c], meta.at[yc], (lat, xi * 8 + c)
            copies.append(remote(src, dst, meta_send.at[stage], meta_recv.at[stage], *target))
        own = (
            (meta_in.at[lat], meta_z.at[lat]),
            (meta_z.at[:, xi], meta_x.at[xi]),
            (meta_x.at[:, :, yc], meta.at[yc]),
        )[stage]
        copies.append(pltpu.make_async_copy(*own, meta_recv.at[stage]))
        return copies

    def meta_start(stage):
        for copy in meta_copies(stage):
            copy.start()

    def meta_wait(stage):
        await_bytes((meta_z, meta_x, meta)[stage], meta_recv.at[stage])

    def meta_sent(stage):
        await_bytes((meta_z, meta_x, meta)[stage].at[pl.ds(0, (3, 3, 7)[stage])], meta_send.at[stage])

    meta_start(0)
    conv_copy = pltpu.make_async_copy(conv_in, conv_w, local_sem.at[1])
    conv_copy.start()

    def send_slot(j):
        dx, dy, dz = offset(j)
        tx, ty, tz = lax.rem(xi + dx, 4), lax.rem(yi + dy, 4), lax.rem(lat + dz, 4)
        g = lax.div(j, 16)
        remote(
            queue.at[tz * 16 + tx * 4 + ty], vals.at[j], a2a_send.at[g], a2a_recv.at[g],
            tz, tx * 8 + ty * 2 + ci,
        ).start()

    north, south = lax.rem(lat + 3, N_LAT), lax.rem(lat + 1, N_LAT)
    west, east = lax.rem(lon + N_LON - 1, N_LON), lax.rem(lon + 1, N_LON)

    def halo_copies(src, k):
        pieces = [
            (src.at[ROWS - 1], hrow.at[k, 0], south, lon),
            (src.at[0], hrow.at[k, 1], north, lon),
        ]
        for side, column, target in ((0, 1, east), (1, 0, west)):
            for turn, tlat in enumerate((lat, south, north)):
                pieces.append((strip.at[k, column], hcol.at[k, side, turn], tlat, target))
        return [
            remote(s, d, halo_send.at[k, i], halo_recv.at[k, i], a, b)
            for i, (s, d, a, b) in enumerate(pieces)
        ]

    def halo_start(src, k):
        for r in range(ROWS):
            stripf[0, r : r + 1, :] = src[r, 0:16, :].astype(F32)[0:1, :]
            stripf[1, r : r + 1, :] = src[r, COLS - 16 : COLS, :].astype(F32)[15:16, :]
        strip[k, 0] = stripf[0].astype(BF16)
        strip[k, 1] = stripf[1].astype(BF16)
        for copy in halo_copies(src, k):
            copy.start()

    def widen(src, x3):
        def body(r):
            row = src[r].astype(F32)
            x3[r + 1, :, 0:CH] = pltpu.roll(row, 1, 0).astype(BF16)
            x3[r + 1, :, CH : 2 * CH] = src[r]
            x3[r + 1, :, 2 * CH : 3 * CH] = pltpu.roll(row, COLS - 1, 0).astype(BF16)

        loop(0, ROWS, body)

    def halo_finish(src, k, x3):
        for copy in halo_copies(src, k):
            copy.wait()
        first = iota((16, CH), 0) == 0
        last = iota((16, CH), 0) == 15
        left = hcol[k, 0, 0].astype(F32)
        right = hcol[k, 1, 0].astype(F32)
        for r in range(ROWS):
            low = x3[r + 1, 0:16, 0:CH].astype(F32)
            x3[r + 1, 0:16, 0:CH] = jnp.where(first, left[r : r + 1, :], low).astype(BF16)
            high = x3[r + 1, COLS - 16 : COLS, 2 * CH : 3 * CH].astype(F32)
            x3[r + 1, COLS - 16 : COLS, 2 * CH : 3 * CH] = jnp.where(
                last, right[r : r + 1, :], high
            ).astype(BF16)
        spot = iota((COLS, CH), 0)
        for side, r, turn, pick, valid in (
            (0, 0, 1, ROWS - 1, lat > 0),
            (1, ROWS + 1, 2, 0, lat < N_LAT - 1),
        ):
            keep = jnp.where(valid, 1.0, 0.0).astype(F32)
            row = hrow[k, side].astype(F32) * keep
            lcorner = hcol[k, 0, turn].astype(F32)[pick : pick + 1, :] * keep
            rcorner = hcol[k, 1, turn].astype(F32)[pick : pick + 1, :] * keep
            x3[r, :, 0:CH] = jnp.where(spot == 0, lcorner, pltpu.roll(row, 1, 0)).astype(BF16)
            x3[r, :, CH : 2 * CH] = row.astype(BF16)
            x3[r, :, 2 * CH : 3 * CH] = jnp.where(
                spot == COLS - 1, rcorner, pltpu.roll(row, COLS - 1, 0)
            ).astype(BF16)

    def conv(x3, w, k, finish, low=0, high=4):
        def body(b):
            acc = jnp.zeros((4 * COLS, CH), F32)
            for p in range(3):
                acc += dot(x3[pl.ds(4 * b + p, 4)].reshape(4 * COLS, 3 * CH), w[k, p])
            finish(pl.ds(4 * b, 4), acc)

        loop(low, high, body)

    def tile4(x):
        return x.reshape(4 * COLS, CH)

    def grid4(x):
        return x.reshape(4, COLS, CH)

    def turn_weights(k):
        for p in range(3):
            for q in range(3):
                block = conv_w[k, 2 - p, (2 - q) * CH : (3 - q) * CH, :]
                conv_t[k, p, q * CH : (q + 1) * CH, :] = block.T

    def turn_act(act, act_t):
        for r in range(ROWS):
            act_t[:, r * COLS : (r + 1) * COLS] = act[r].T

    cot_copy.wait()
    halo_start(cot, 0)
    meta_wait(0)
    meta_start(1)
    pair_own.wait()
    pair_other.wait()
    pltpu.make_async_copy(queue.at[chip], vals.at[0], a2a_recv.at[0]).start()
    loop(1, 64, send_slot)
    widen(cot, x3_cot)
    meta_wait(1)
    meta_start(2)
    conv_copy.wait()
    turn_weights(1)
    embed_t[...] = embed_w[...].T
    halo_finish(cot, 0, x3_cot)

    def keep_back(rows, acc):
        back[rows] = grid4(acc)

    conv(x3_cot, conv_t, 1, keep_back)
    meta_wait(2)

    placed[...] = jnp.zeros_like(placed)
    counts[...] = jnp.zeros_like(counts)
    slot_mask = jnp.where(
        lax.rem(iota((CAP, 128), 1), 32) == iota((CAP, 128), 0), 1.0, 0.0
    ).astype(F32)
    spread = jnp.where(
        lax.div(iota((128, 512), 0), 32) == lax.div(iota((128, 512), 1), 128), 1.0, 0.0
    ).astype(BF16)
    lane, line = iota((COLS + 16, 128), 1), iota((COLS + 16, 128), 0)
    pick = jnp.where(lax.div(lane, 32) == jnp.where(line < COLS, 0, 3), 1.0, 0.0).astype(BF16)
    decay = sharp[...] * (-1.0 / 256.0)

    for g in range(4):
        def stretch(s, g=g):
            dx, dy, dz = offset(g * 16 + lax.div(s, 2))
            sx, sy, sz = lax.rem(xi + 4 - dx, 4), lax.rem(yi + 4 - dy, 4), lax.rem(lat + 4 - dz, 4)
            source = meta[sy * 2 + lax.rem(s, 2), sx, sz]
            line = jnp.broadcast_to(source, (CAP, 128)) * slot_mask
            tmeta[aligned(s * CAP, CAP, CAP), :] = line.astype(BF16)

        loop(0, 32, stretch)
        await_bytes(vals.at[pl.ds(g * 16, 16)], a2a_recv.at[g])

        def embed_block(b, g=g):
            at = aligned(b * 256, 256, 256)
            of = aligned(g * GROUP + b * 256, 256, 256)
            wide = dot(tmeta[at, :], spread)
            colb[of, :] = wide[:, 0:128].astype(BF16)
            rowb[of, :] = wide[:, 384:512].astype(BF16)
            rk_of = jnp.concatenate([wide[:, 128:256]] * 2, axis=1)
            radius = jnp.concatenate([wide[:, 256:384]] * 2, axis=1)
            rk[at, :] = jnp.where(
                rk_of == iota((256, 256), 1).astype(F32), 1.0, 0.0
            ).astype(BF16)
            w = jnp.exp(radius * decay)
            weight[of, :] = w
            ew[at, :] = (dot(vals[pl.ds(g * 16 + 4 * b, 4)].reshape(256, VALS), embed_w[...]) * w).astype(BF16)

        loop(0, 4, embed_block)
        both = lax.dot_general(pick, tmeta[...], NT, preferred_element_type=F32)
        colhot[...] = jnp.where(
            both[0:COLS] == iota((COLS, GROUP), 0).astype(F32), 1.0, 0.0
        ).astype(BF16)
        rowl[...] = both[COLS : COLS + 16]
        counts[...] += dot(colhot[...], rk[...])

        def place(pair):
            hot = colhot[...].reshape(8, 16, GROUP)
            halves = []
            for h in range(2):
                r = (2 * pair + h).astype(F32)
                mask = jnp.where(rowl[...] == r, 1.0, 0.0).astype(BF16)
                halves.append((hot * mask[None]).reshape(COLS, GROUP))
            at = aligned(pair * 256, 256, 256)
            placed[at, :] += dot(jnp.concatenate(halves, axis=0), ew[...])

        loop(0, 8, place)

    tally = counts[...].astype(BF16)
    kind = lax.rem(iota((256, CH), 0), 16)
    half_u, half_v = 2 * lax.div(kind, 4) + 1, 2 * lax.rem(kind, 4) + 1
    table = jnp.exp((half_u * half_u + half_v * half_v).astype(F32) * decay)
    table_hi = table.astype(BF16)
    table_lo = (table - table_hi.astype(F32)).astype(BF16)

    def base_row(r):
        own = lax.div(iota((256, CH), 0), 16) == r
        hi = jnp.where(own, table_hi.astype(F32), 0.0).astype(BF16)
        lo = jnp.where(own, table_lo.astype(F32), 0.0).astype(BF16)
        recip = 1.0 / (dot(tally, hi) + dot(tally, lo) + 1.0)
        inv[r] = recip
        value = (placed[aligned(r * COLS, COLS, COLS), :] * recip).astype(BF16)
        base[r] = value
        x = value.astype(F32)
        act_zero[r] = (x * sigmoid(x)).astype(BF16)

    loop(0, ROWS, base_row)
    halo_start(act_zero, 1)
    widen(act_zero, x3_act)
    turn_weights(0)
    turn_act(act_zero, zero_t)
    halo_finish(act_zero, 1, x3_act)

    def keep_mid(rows, acc):
        value = (tile4(base[rows]).astype(F32) + acc).astype(BF16)
        mid[rows] = grid4(value)
        x = value.astype(F32)
        s = sigmoid(x)
        act_one[rows] = grid4((x * s).astype(BF16))
        slope = s * (1.0 + x * (1.0 - s))
        grad = tile4(cot[rows]).astype(F32) + tile4(back[rows]) * slope
        gmid[rows] = grid4(grad.astype(BF16))

    conv(x3_act, conv_w, 0, keep_mid)
    halo_start(gmid, 2)
    halo_start(act_one, 3)

    def kernel_grad(act_t, x3, k):
        def body(p):
            block = dot(act_t[...], x3[pl.ds(2 - p, ROWS)].reshape(CELLS, 3 * CH))
            for q in range(3):
                at = aligned((k * 9 + 3 * p + q) * CH, CH, CH)
                grads[at, :] = block[:, (2 - q) * CH : (3 - q) * CH].astype(BF16)

        loop(0, 3, body)

    turn_act(act_one, act_t)
    kernel_grad(act_t, x3_cot, 1)
    widen(gmid, x3_mid)
    halo_finish(gmid, 2, x3_mid)
    kernel_grad(zero_t, x3_mid, 0)

    coords = {"x": xi, "y": yi, "z": lat}
    orders = (("x", "y", "z"), ("y", "z", "x"), ("z", "x", "y"))

    def along(axis, c):
        cx, cy, cz = [c if axis == n else coords[n] for n in ("x", "y", "z")]
        return cz, cx * 8 + cy * 2 + ci

    def turned(axis, d):
        return lax.rem(coords[axis] + d, 4)

    def part_copies(stage):
        copies = []
        for a, order in enumerate(orders):
            own = a * PART + ci * HALF
            sems = lambda d: (ar_send.at[stage, a, d], ar_recv.at[stage, a, d])
            quarter = own + coords[order[0]] * QUARTER
            shard = quarter + coords[order[1]] * SHARD
            if stage == 0:
                src = grads.at[aligned(a * PART + (1 - ci) * HALF, HALF, 16)]
                copies.append(remote(src, p0.at[a], *sems(0), lat, other_core))
            elif stage == 6:
                piece = total.at[aligned(own, HALF, 16)]
                copies.append(remote(piece, piece, *sems(0), lat, other_core))
            else:
                axis = order[{1: 0, 2: 1, 3: 2, 4: 1, 5: 0}[stage]]
                for d in (1, 3, 2):
                    c = turned(axis, d)
                    if stage == 1:
                        src, dst = s1.at[a, aligned(c * QUARTER, QUARTER, 16)], p1.at[a, d - 1]
                    elif stage == 2:
                        src, dst = s2.at[a, aligned(c * SHARD, SHARD, 16)], p2.at[a, d - 1]
                    elif stage == 3:
                        src, dst = s3.at[a], p3.at[a, coords[axis]]
                    elif stage == 4:
                        src = dst = total.at[aligned(shard, SHARD, 16)]
                    else:
                        src = dst = total.at[aligned(quarter, QUARTER, 16)]
                    copies.append(remote(src, dst, *sems(d - 1), *along(axis, c)))
        return copies

    def ar_start(stage):
        for copy in part_copies(stage):
            copy.start()

    def ar_finish(stage):
        for copy in part_copies(stage):
            copy.wait()
        for a, order in enumerate(orders):
            own = a * PART + ci * HALF
            if stage == 0:

                def body(b, a=a, own=own):
                    here = grads[aligned(own + b * QUARTER, QUARTER, 16), :].astype(F32)
                    at = aligned(b * QUARTER, QUARTER, 16)
                    s1[a, at, :] = (here + p0[a, at, :].astype(F32)).astype(BF16)

                loop(0, 4, body)
            elif stage in (1, 2):
                size = QUARTER if stage == 1 else SHARD
                src, came, dst = (s1, p1, s2) if stage == 1 else (s2, p2, s3)
                here = src[a, aligned(coords[order[stage - 1]] * size, size, 16), :].astype(F32)
                for d in range(3):
                    here += came[a, d].astype(F32)
                dst[a] = here.astype(BF16)
            elif stage == 3:
                p3[a, coords[order[2]]] = s3[a]
                whole = p3[a, 0].astype(F32)
                for d in range(1, 4):
                    whole += p3[a, d].astype(F32)
                quarter = own + coords[order[0]] * QUARTER
                at = aligned(quarter + coords[order[1]] * SHARD, SHARD, 16)
                total[at, :] = whole.astype(BF16)

    ar_start(0)

    def keep_gp(rows, acc):
        x = tile4(base[rows]).astype(F32)
        s = sigmoid(x)
        grad = tile4(gmid[rows]).astype(F32) + acc * (s * (1.0 + x * (1.0 - s)))
        gp[aligned(rows.start * COLS, 4 * COLS, 4 * COLS), :] = (
            grad * tile4(inv[rows])
        ).astype(BF16)

    conv(x3_mid, conv_t, 0, keep_gp)
    ar_finish(0)
    ar_start(1)

    esum[...] = jnp.zeros_like(esum)

    def vg_copy(j):
        dx, dy, dz = offset(j)
        sx, sy, sz = lax.rem(xi + 4 - dx, 4), lax.rem(yi + 4 - dy, 4), lax.rem(lat + 4 - dz, 4)
        return remote(vg.at[j], relay.at[chip], vg_send, vg_recv, sz, sx * 8 + sy * 2 + ci)

    def gather(b):
        at = aligned(b * 256, 256, 256)
        hot = jnp.where(
            colb[at, :].astype(F32) == iota((256, COLS), 1).astype(F32), 1.0, 0.0
        ).astype(BF16)
        row_of = rowb[at, :]
        pieces = [
            jnp.where(row_of == jnp.array(r, BF16), hot, jnp.zeros_like(hot)) for r in range(ROWS)
        ]
        found = dot(jnp.concatenate(pieces, axis=1), gp[...])
        grad = (found * weight[at, :]).astype(BF16)
        vg[pl.ds(4 * b, 4)] = dot(grad, embed_t[...]).astype(BF16).reshape(4, 2, CAP, VALS)
        own = vals[pl.ds(4 * b, 4)].reshape(256, VALS)
        esum[...] += lax.dot_general(own, grad, TN, preferred_element_type=F32)

    gather(0)
    pltpu.make_async_copy(vg.at[0], relay.at[chip], vg_recv).start()
    for j in range(1, 4):
        vg_copy(j).start()

    def gather_send(b):
        gather(b)
        for s in range(4):
            vg_copy(b * 4 + s).start()

    loop(1, 6, gather_send)
    ar_finish(1)
    ar_start(2)
    loop(6, 9, gather_send)
    ar_finish(2)
    ar_start(3)
    loop(9, 12, gather_send)
    ar_finish(3)
    ar_start(4)
    loop(12, 16, gather_send)
    ar_finish(4)
    ar_start(5)

    member = yc
    column = xi * 4 + lat

    def embed_copies(stage):
        copies = []
        for d in range(1, 16 if stage == 1 else 8):
            if stage == 1:
                c = lax.rem(column + d, 16)
                tlat, tlon = lax.rem(c, 4), lax.div(c, 4) * 8 + member
                src, dst = esum.at[aligned(member * 16, 16, 16)], qe.at[column]
            else:
                m = lax.rem(member + d, 8)
                tlat, tlon = lat, xi * 8 + m
                if stage == 0:
                    src, dst = esum.at[aligned(m * 16, 16, 16)], pe.at[d - 1]
                else:
                    src = dst = etotal.at[aligned(member * 16, 16, 16)]
            copies.append(remote(src, dst, em_send.at[stage, d - 1], em_recv.at[stage, d - 1], tlat, tlon))
        return copies

    def embed_start(stage):
        for copy in embed_copies(stage):
            copy.start()

    def embed_wait(stage):
        for copy in embed_copies(stage):
            copy.wait()

    embed_start(0)
    widen(act_one, x3_act)
    halo_finish(act_one, 3, x3_act)

    def keep_enc(rows, acc):
        enc[rows] = grid4((tile4(mid[rows]).astype(F32) + acc).astype(BF16))

    conv(x3_act, conv_w, 1, keep_enc, 0, 2)
    embed_wait(0)
    own_rows = aligned(member * 16, 16, 16)
    mine = esum[own_rows, :]
    for d in range(7):
        mine += pe[d]
    esum[own_rows, :] = mine
    embed_start(1)
    conv(x3_act, conv_w, 1, keep_enc, 2, 4)
    enc_copy = pltpu.make_async_copy(enc, enc_out, local_sem.at[2])
    enc_copy.start()
    embed_wait(1)
    qe[column] = esum[own_rows, :]
    whole = qe[0]
    for d in range(1, 16):
        whole += qe[d]
    etotal[own_rows, :] = whole
    embed_start(2)
    ar_finish(5)
    ar_start(6)
    await_bytes(relay, vg_recv)
    vg_own = pltpu.make_async_copy(relay.at[:, ci], vg_out.at[:, ci], local_sem.at[5])
    vg_own.start()
    vg_other = remote(
        relay.at[:, 1 - ci], vg_out.at[:, ci], pair_send.at[1], pair_recv.at[1], lat, other_core
    )
    vg_other.start()
    ar_finish(6)
    grads_copy = pltpu.make_async_copy(total, grads_out, local_sem.at[3])
    grads_copy.start()
    embed_wait(2)
    embed_out[...] = etotal[...] * (1.0 / 512.0)
    for g in range(4):
        await_bytes(vals.at[pl.ds(0, 15 if g == 0 else 16)], a2a_send.at[g])
    for stage in range(3):
        meta_sent(stage)
    await_bytes(vg.at[pl.ds(0, 63)], vg_send)
    vg_own.wait()
    vg_other.wait()
    enc_copy.wait()
    grads_copy.wait()


def scaled(grads_ref, out_ref):
    out_ref[...] = grads_ref[...].astype(F32) * (1.0 / 512.0)


def on_device(
    obs_values, obs_cells, obs_subcell, slot_counts, sharpness, embed_weight, conv_weight, cotangent
):
    cells = obs_cells.reshape(DEVICES, 1, CAP)
    subs = obs_subcell.reshape(DEVICES, 1, CAP)
    spread = (DEVICES, 4, CAP)
    live = lax.broadcasted_iota(jnp.int32, spread, 2) < slot_counts.reshape(DEVICES, 1, 1)
    field = lax.broadcasted_iota(jnp.int32, spread, 1)
    i, j = subs >> 3, subs & 7
    u = jnp.where(i >= 4, i - 4, 3 - i)
    v = jnp.where(j >= 4, j - 4, 3 - j)
    row = cells >> 7
    radius = (2 * u + 1) * (2 * u + 1) + (2 * v + 1) * (2 * v + 1)
    column = jnp.where(live, cells & 127, 255)
    rest = jnp.where(field == 1, row * 16 + u * 4 + v, jnp.where(field == 2, radius, row))
    meta = jnp.where(field == 0, column, rest).astype(F32)
    anywhere = pl.BlockSpec(memory_space=pl.ANY)
    vmem = pl.BlockSpec(memory_space=pltpu.VMEM)
    grid = (ROWS, COLS, CH)
    wide = (ROWS + 2, COLS, 3 * CH)
    dma = pltpu.SemaphoreType.DMA
    scratch = [
        pltpu.VMEM((64, 2, CAP, VALS), BF16),
        pltpu.VMEM((64, 2, CAP, VALS), BF16),
        pltpu.VMEM((64, 2, CAP, VALS), BF16),
        pltpu.VMEM((4, 4, 8, 1, 128), F32),
        pltpu.VMEM((4, 4, 8, 1, 128), F32),
        pltpu.VMEM((8, 4, 4, 1, 128), F32),
        pltpu.VMEM((GROUP, 128), BF16),
        pltpu.VMEM((OBS, 128), BF16),
        pltpu.VMEM((OBS, 128), BF16),
        pltpu.VMEM((OBS, CH), F32),
        pltpu.VMEM((GROUP, CH), BF16),
        pltpu.VMEM((GROUP, 256), BF16),
        pltpu.VMEM((COLS, GROUP), BF16),
        pltpu.VMEM((16, GROUP), F32),
        pltpu.VMEM((CELLS, CH), F32),
        pltpu.VMEM((COLS, 256), F32),
        pltpu.VMEM(grid, F32),
        pltpu.VMEM(grid, BF16),
        pltpu.VMEM((2, 3, 3 * CH, CH), BF16),
        pltpu.VMEM((2, 3, 3 * CH, CH), BF16),
        pltpu.VMEM((CH, VALS), BF16),
        pltpu.VMEM(grid, F32),
        pltpu.VMEM(grid, BF16),
        pltpu.VMEM(grid, BF16),
        pltpu.VMEM(grid, BF16),
        pltpu.VMEM(grid, BF16),
        pltpu.VMEM(grid, BF16),
        pltpu.VMEM((CELLS, CH), BF16),
        pltpu.VMEM((CH, CELLS), BF16),
        pltpu.VMEM((CH, CELLS), BF16),
        pltpu.VMEM(wide, BF16),
        pltpu.VMEM(wide, BF16),
        pltpu.VMEM(wide, BF16),
        pltpu.VMEM((4, 2, COLS, CH), BF16),
        pltpu.VMEM((4, 2, 3, 16, CH), BF16),
        pltpu.VMEM((4, 2, 16, CH), BF16),
        pltpu.VMEM((2, 16, CH), F32),
        pltpu.VMEM((64, 2, CAP, VALS), BF16),
        pltpu.VMEM((3 * PART, CH), BF16),
        pltpu.VMEM((3 * PART, CH), BF16),
        pltpu.VMEM((3, HALF, CH), BF16),
        pltpu.VMEM((3, HALF, CH), BF16),
        pltpu.VMEM((3, 3, QUARTER, CH), BF16),
        pltpu.VMEM((3, QUARTER, CH), BF16),
        pltpu.VMEM((3, 3, SHARD, CH), BF16),
        pltpu.VMEM((3, SHARD, CH), BF16),
        pltpu.VMEM((3, 4, SHARD, CH), BF16),
        pltpu.VMEM((VALS, CH), F32),
        pltpu.VMEM((7, 16, CH), F32),
        pltpu.VMEM((16, 16, CH), F32),
        pltpu.VMEM((VALS, CH), F32),
        pltpu.VMEM(grid, BF16),
        dma((6,)),
        dma((2,)),
        dma((2,)),
        dma((4,)),
        dma((4,)),
        dma((3,)),
        dma((3,)),
        dma,
        dma,
        dma((4, 8)),
        dma((4, 8)),
        dma((7, 3, 3)),
        dma((7, 3, 3)),
        dma((3, 15)),
        dma((3, 15)),
    ]
    encoded, value_grads, grads, embed_total = pl.pallas_call(
        kernel,
        out_shape=(
            jax.ShapeDtypeStruct(grid, BF16),
            jax.ShapeDtypeStruct((64, 2, CAP, VALS), BF16),
            jax.ShapeDtypeStruct((3 * PART, CH), BF16),
            jax.ShapeDtypeStruct((VALS, CH), F32),
        ),
        in_specs=[anywhere, anywhere, vmem, vmem, anywhere, anywhere],
        out_specs=(anywhere, anywhere, anywhere, vmem),
        scratch_shapes=scratch,
        compiler_params=pltpu.CompilerParams(
            has_side_effects=True, vmem_limit_bytes=60 * 1024 * 1024
        ),
        cost_estimate=pl.CostEstimate(
            flops=30_000_000_000, bytes_accessed=20_000_000, transcendentals=4_000_000
        ),
    )(
        obs_values.reshape(64, 2, CAP, VALS),
        meta.reshape(4, 4, 8, 1, 128),
        sharpness.reshape(1, CH),
        embed_weight,
        conv_weight.reshape(2, 3, 3 * CH, CH),
        cotangent,
    )
    conv_grads = pl.pallas_call(
        scaled,
        grid=(6,),
        out_shape=jax.ShapeDtypeStruct((3 * PART, CH), F32),
        in_specs=[pl.BlockSpec((HALF, CH), lambda i: (i, 0))],
        out_specs=pl.BlockSpec((HALF, CH), lambda i: (i, 0)),
    )(grads)
    return (
        encoded,
        value_grads.reshape(OBS, VALS),
        conv_grads.reshape(2, 3, 3, CH, CH),
        embed_total,
    )


def solution(mesh):
    placed = (
        P(("lat", "lon"), None),
        P(("lat", "lon")),
        P(("lat", "lon")),
        P(("lat", "lon"), None),
        P(),
        P(),
        P(),
        P("lat", "lon", None),
    )
    return jax.shard_map(
        on_device,
        mesh=mesh,
        in_specs=placed,
        out_specs=(P("lat", "lon", None), P(("lat", "lon"), None), P(), P()),
        check_vma=False,
    )
```

```python
import jax
import jax.numpy as jnp
from jax import lax
from jax.experimental import pallas as pl
from jax.experimental.pallas import tpu as pltpu
from jax.sharding import PartitionSpec as P

F32 = jnp.float32
BF16 = jnp.bfloat16
N_LAT, N_LON = 4, 32
DEVICES = N_LAT * N_LON
CAP, VALS, CH = 32, 128, 256
ROWS, COLS = 16, 128
CELLS = ROWS * COLS
OBS = DEVICES * CAP
GROUP = 32 * CAP
PART, HALF, QUARTER, SHARD = 1536, 768, 192, 48
NT = (((1,), (1,)), ((), ()))
TN = (((0,), (0,)), ((), ()))


def dot(a, b):
    return jnp.dot(a, b, preferred_element_type=F32)


def iota(shape, axis):
    return lax.broadcasted_iota(jnp.int32, shape, axis)


def sigmoid(x):
    return 1.0 / (1.0 + jnp.exp(-x))


def remote(src, dst, send, recv, lat, lon):
    return pltpu.make_async_remote_copy(
        src_ref=src,
        dst_ref=dst,
        send_sem=send,
        recv_sem=recv,
        device_id=(lat, lon),
        device_id_type=pl.DeviceIdType.MESH,
    )


def await_bytes(ref, sem):
    pltpu.make_async_copy(ref, ref, sem).wait()


def loop(low, high, body):
    def step(i, carry):
        body(i)
        return carry

    lax.fori_loop(low, high, step, 0)


def aligned(start, size, unit):
    return pl.ds(pl.multiple_of(start, unit), size)


def kernel(
    obs_in, meta_in, sharp, embed_w, conv_in, cot_in,
    enc_out, vg_out, grads_out, embed_out,
    vals, queue, relay, meta_z, meta_x, meta, tmeta, colb, rowb, weight, ew, rk, colhot, rowl, placed, counts, inv,
    cot, conv_w, conv_t, embed_t, back, base, act_zero, mid, act_one, gmid, gp, act_t, zero_t,
    x3_act, x3_cot, x3_mid, hrow, hcol, strip, stripf,
    vg, grads, total, p0, s1, p1, s2, p2, s3, p3, esum, pe, qe, etotal, enc,
    local_sem, pair_send, pair_recv, a2a_send, a2a_recv, meta_send, meta_recv, vg_send, vg_recv,
    halo_send, halo_recv, ar_send, ar_recv, em_send, em_recv,
):
    lat = lax.axis_index("lat")
    lon = lax.axis_index("lon")
    me = lat * N_LON + lon
    xi, yi, ci = lax.div(lon, 8), lax.rem(lax.div(lon, 2), 4), lax.rem(lon, 2)

    chip = lat * 16 + xi * 4 + yi
    yc = lax.rem(lon, 8)
    other_core = lon + 1 - 2 * ci

    def offset(j):
        g, dx, dy = lax.div(j, 16), lax.rem(lax.div(j, 4), 4), lax.rem(j, 4)
        return dx, dy, lax.rem(g + 8 - dx - dy, 4)

    cot_copy = pltpu.make_async_copy(cot_in, cot, local_sem.at[0])
    cot_copy.start()
    pair_own = pltpu.make_async_copy(obs_in.at[:, ci], queue.at[:, ci], local_sem.at[4])
    pair_own.start()
    pair_other = remote(
        obs_in.at[:, 1 - ci], queue.at[:, ci], pair_send.at[0], pair_recv.at[0], lat, other_core
    )
    pair_other.start()

    def meta_copies(stage):
        copies = []
        for d in range(1, 8 if stage == 2 else 4):
            if stage == 0:
                c = lax.rem(lat + d, 4)
                src, dst, target = meta_in.at[c], meta_z.at[lat], (c, lon)
            elif stage == 1:
                c = lax.rem(xi + d, 4)
                src, dst, target = meta_z.at[:, c], meta_x.at[xi], (lat, c * 8 + yc)
            else:
                c = lax.rem(yc + d, 8)
                src, dst, target = meta_x.at[:, :, c], meta.at[yc], (lat, xi * 8 + c)
            copies.append(remote(src, dst, meta_send.at[stage], meta_recv.at[stage], *target))
        own = (
            (meta_in.at[lat], meta_z.at[lat]),
            (meta_z.at[:, xi], meta_x.at[xi]),
            (meta_x.at[:, :, yc], meta.at[yc]),
        )[stage]
        copies.append(pltpu.make_async_copy(*own, meta_recv.at[stage]))
        return copies

    def meta_start(stage):
        for copy in meta_copies(stage):
            copy.start()

    def meta_wait(stage):
        await_bytes((meta_z, meta_x, meta)[stage], meta_recv.at[stage])

    def meta_sent(stage):
        await_bytes((meta_z, meta_x, meta)[stage].at[pl.ds(0, (3, 3, 7)[stage])], meta_send.at[stage])

    meta_start(0)
    conv_copy = pltpu.make_async_copy(conv_in, conv_w, local_sem.at[1])
    conv_copy.start()

    def send_slot(j):
        dx, dy, dz = offset(j)
        tx, ty, tz = lax.rem(xi + dx, 4), lax.rem(yi + dy, 4), lax.rem(lat + dz, 4)
        g = lax.div(j, 16)
        remote(
            queue.at[tz * 16 + tx * 4 + ty], vals.at[j], a2a_send.at[g], a2a_recv.at[g],
            tz, tx * 8 + ty * 2 + ci,
        ).start()

    north, south = lax.rem(lat + 3, N_LAT), lax.rem(lat + 1, N_LAT)
    west, east = lax.rem(lon + N_LON - 1, N_LON), lax.rem(lon + 1, N_LON)

    def halo_copies(src, k):
        pieces = [
            (src.at[ROWS - 1], hrow.at[k, 0], south, lon),
            (src.at[0], hrow.at[k, 1], north, lon),
        ]
        for side, column, target in ((0, 1, east), (1, 0, west)):
            for turn, tlat in enumerate((lat, south, north)):
                pieces.append((strip.at[k, column], hcol.at[k, side, turn], tlat, target))
        return [
            remote(s, d, halo_send.at[k, i], halo_recv.at[k, i], a, b)
            for i, (s, d, a, b) in enumerate(pieces)
        ]

    def halo_start(src, k):
        for r in range(ROWS):
            stripf[0, r : r + 1, :] = src[r, 0:16, :].astype(F32)[0:1, :]
            stripf[1, r : r + 1, :] = src[r, COLS - 16 : COLS, :].astype(F32)[15:16, :]
        strip[k, 0] = stripf[0].astype(BF16)
        strip[k, 1] = stripf[1].astype(BF16)
        for copy in halo_copies(src, k):
            copy.start()

    def widen(src, x3):
        def body(b):
            for i in range(4):
                r = 4 * b + i
                row = src[r].astype(F32)
                x3[r + 1, :, 0:CH] = pltpu.roll(row, 1, 0).astype(BF16)
                x3[r + 1, :, CH : 2 * CH] = src[r]
                x3[r + 1, :, 2 * CH : 3 * CH] = pltpu.roll(row, COLS - 1, 0).astype(BF16)

        loop(0, ROWS // 4, body)

    def halo_finish(src, k, x3):
        for copy in halo_copies(src, k):
            copy.wait()
        first = iota((16, CH), 0) == 0
        last = iota((16, CH), 0) == 15
        left = hcol[k, 0, 0].astype(F32)
        right = hcol[k, 1, 0].astype(F32)
        for r in range(ROWS):
            low = x3[r + 1, 0:16, 0:CH].astype(F32)
            x3[r + 1, 0:16, 0:CH] = jnp.where(first, left[r : r + 1, :], low).astype(BF16)
            high = x3[r + 1, COLS - 16 : COLS, 2 * CH : 3 * CH].astype(F32)
            x3[r + 1, COLS - 16 : COLS, 2 * CH : 3 * CH] = jnp.where(
                last, right[r : r + 1, :], high
            ).astype(BF16)
        spot = iota((COLS, CH), 0)
        for side, r, turn, pick, valid in (
            (0, 0, 1, ROWS - 1, lat > 0),
            (1, ROWS + 1, 2, 0, lat < N_LAT - 1),
        ):
            keep = jnp.where(valid, 1.0, 0.0).astype(F32)
            row = hrow[k, side].astype(F32) * keep
            lcorner = hcol[k, 0, turn].astype(F32)[pick : pick + 1, :] * keep
            rcorner = hcol[k, 1, turn].astype(F32)[pick : pick + 1, :] * keep
            x3[r, :, 0:CH] = jnp.where(spot == 0, lcorner, pltpu.roll(row, 1, 0)).astype(BF16)
            x3[r, :, CH : 2 * CH] = row.astype(BF16)
            x3[r, :, 2 * CH : 3 * CH] = jnp.where(
                spot == COLS - 1, rcorner, pltpu.roll(row, COLS - 1, 0)
            ).astype(BF16)

    def conv(x3, w, k, finish, low=0, high=4):
        taps = w[k].reshape(9 * CH, CH)
        for b in range(low, high):
            near = [x3[4 * b + p : 4 * b + p + 4].reshape(4 * COLS, 3 * CH) for p in range(3)]
            finish(slice(4 * b, 4 * b + 4), dot(jnp.concatenate(near, axis=1), taps))

    def tile4(x):
        return x.reshape(4 * COLS, CH)

    def grid4(x):
        return x.reshape(4, COLS, CH)

    def turn_weights(k):
        for p in range(3):
            for q in range(3):
                block = conv_w[k, 2 - p, (2 - q) * CH : (3 - q) * CH, :]
                conv_t[k, p, q * CH : (q + 1) * CH, :] = block.T

    def turn_act(act, act_t):
        for r in range(ROWS):
            act_t[:, r * COLS : (r + 1) * COLS] = act[r].T

    cot_copy.wait()
    halo_start(cot, 0)
    meta_wait(0)
    meta_start(1)
    pair_own.wait()
    pair_other.wait()
    pltpu.make_async_copy(queue.at[chip], vals.at[0], a2a_recv.at[0]).start()
    loop(1, 64, send_slot)
    widen(cot, x3_cot)
    meta_wait(1)
    meta_start(2)
    conv_copy.wait()
    turn_weights(1)
    embed_t[...] = embed_w[...].T
    halo_finish(cot, 0, x3_cot)

    def keep_back(rows, acc):
        back[rows] = grid4(acc)

    conv(x3_cot, conv_t, 1, keep_back)
    meta_wait(2)

    placed[...] = jnp.zeros_like(placed)
    counts[...] = jnp.zeros_like(counts)
    slot_mask = jnp.where(
        lax.rem(iota((CAP, 128), 1), 32) == iota((CAP, 128), 0), 1.0, 0.0
    ).astype(F32)
    spread = jnp.where(
        lax.div(iota((128, 512), 0), 32) == lax.div(iota((128, 512), 1), 128), 1.0, 0.0
    ).astype(BF16)
    lane, line = iota((COLS + 16, 128), 1), iota((COLS + 16, 128), 0)
    pick = jnp.where(lax.div(lane, 32) == jnp.where(line < COLS, 0, 3), 1.0, 0.0).astype(BF16)
    decay = sharp[...] * (-1.0 / 256.0)

    for g in range(4):
        def stretch(b, g=g):
            for i in range(8):
                s = 8 * b + i
                dx, dy, dz = offset(g * 16 + 4 * b + i // 2)
                sx, sy = lax.rem(xi + 4 - dx, 4), lax.rem(yi + 4 - dy, 4)
                source = meta[sy * 2 + i % 2, sx, lax.rem(lat + 4 - dz, 4)]
                line = jnp.broadcast_to(source, (CAP, 128)) * slot_mask
                tmeta[aligned(s * CAP, CAP, CAP), :] = line.astype(BF16)

        loop(0, 4, stretch)
        await_bytes(vals.at[pl.ds(g * 16, 16)], a2a_recv.at[g])

        for b in range(4):
            at = slice(b * 256, b * 256 + 256)
            of = slice(g * GROUP + b * 256, g * GROUP + b * 256 + 256)
            wide = dot(tmeta[at, :], spread)
            colb[of, :] = wide[:, 0:128].astype(BF16)
            rowb[of, :] = wide[:, 384:512].astype(BF16)
            rk_of = jnp.concatenate([wide[:, 128:256]] * 2, axis=1)
            radius = jnp.concatenate([wide[:, 256:384]] * 2, axis=1)
            rk[at, :] = jnp.where(
                rk_of == iota((256, 256), 1).astype(F32), 1.0, 0.0
            ).astype(BF16)
            w = jnp.exp(radius * decay)
            weight[of, :] = w
            ew[at, :] = (dot(vals[g * 16 + 4 * b : g * 16 + 4 * b + 4].reshape(256, VALS), embed_w[...]) * w).astype(BF16)

        both = lax.dot_general(pick, tmeta[...], NT, preferred_element_type=F32)
        colhot[...] = jnp.where(
            both[0:COLS] == iota((COLS, GROUP), 0).astype(F32), 1.0, 0.0
        ).astype(BF16)
        rowl[...] = both[COLS : COLS + 16]
        counts[...] += dot(colhot[...], rk[...])

        hot = colhot[...].reshape(8, 16, GROUP)
        for b in range(4):
            rows = []
            for r in range(4 * b, 4 * b + 4):
                mask = jnp.where(rowl[...] == float(r), 1.0, 0.0).astype(BF16)
                rows.append((hot * mask[None]).reshape(COLS, GROUP))
            at = slice(b * 512, b * 512 + 512)
            placed[at, :] += dot(jnp.concatenate(rows, axis=0), ew[...])

    kind = lax.rem(iota((256, CH), 0), 16)
    half_u, half_v = 2 * lax.div(kind, 4) + 1, 2 * lax.rem(kind, 4) + 1
    table = jnp.exp((half_u * half_u + half_v * half_v).astype(F32) * decay)
    table_hi = table.astype(BF16)
    table_lo = (table - table_hi.astype(F32)).astype(BF16)
    tables = jnp.concatenate([table_hi, table_lo], axis=0)
    row_of_lane = lax.div(iota((COLS, 256), 1), 16)
    for b in range(4):
        rows = []
        for r in range(4 * b, 4 * b + 4):
            rows.append(jnp.where(row_of_lane == r, counts[...], 0.0).astype(BF16))
        tally = jnp.concatenate(rows, axis=0)
        recip = 1.0 / (dot(jnp.concatenate([tally, tally], axis=1), tables) + 1.0)
        at = slice(4 * b, 4 * b + 4)
        inv[at] = grid4(recip)
        value = (placed[b * 512 : b * 512 + 512, :] * recip).astype(BF16)
        base[at] = grid4(value)
        x = value.astype(F32)
        act_zero[at] = grid4((x * sigmoid(x)).astype(BF16))

    halo_start(act_zero, 1)
    widen(act_zero, x3_act)
    turn_weights(0)
    turn_act(act_zero, zero_t)
    halo_finish(act_zero, 1, x3_act)

    def keep_mid(rows, acc):
        value = (tile4(base[rows]).astype(F32) + acc).astype(BF16)
        mid[rows] = grid4(value)
        x = value.astype(F32)
        s = sigmoid(x)
        act_one[rows] = grid4((x * s).astype(BF16))
        slope = s * (1.0 + x * (1.0 - s))
        grad = tile4(cot[rows]).astype(F32) + tile4(back[rows]) * slope
        gmid[rows] = grid4(grad.astype(BF16))

    conv(x3_act, conv_w, 0, keep_mid)
    halo_start(gmid, 2)
    halo_start(act_one, 3)

    def kernel_grad(act_t, x3, k):
        for p in range(3):
            block = dot(act_t[...], x3[2 - p : 2 - p + ROWS].reshape(CELLS, 3 * CH))
            for q in range(3):
                at = (k * 9 + 3 * p + q) * CH
                grads[at : at + CH, :] = block[:, (2 - q) * CH : (3 - q) * CH].astype(BF16)

    turn_act(act_one, act_t)
    kernel_grad(act_t, x3_cot, 1)
    widen(gmid, x3_mid)
    halo_finish(gmid, 2, x3_mid)
    kernel_grad(zero_t, x3_mid, 0)

    coords = {"x": xi, "y": yi, "z": lat}
    orders = (("x", "y", "z"), ("y", "z", "x"), ("z", "x", "y"))

    def along(axis, c):
        cx, cy, cz = [c if axis == n else coords[n] for n in ("x", "y", "z")]
        return cz, cx * 8 + cy * 2 + ci

    def turned(axis, d):
        return lax.rem(coords[axis] + d, 4)

    def part_copies(stage):
        copies = []
        for a, order in enumerate(orders):
            own = a * PART + ci * HALF
            sems = lambda d: (ar_send.at[stage, a, d], ar_recv.at[stage, a, d])
            quarter = own + coords[order[0]] * QUARTER
            shard = quarter + coords[order[1]] * SHARD
            if stage == 0:
                src = grads.at[aligned(a * PART + (1 - ci) * HALF, HALF, 16)]
                copies.append(remote(src, p0.at[a], *sems(0), lat, other_core))
            elif stage == 6:
                piece = total.at[aligned(own, HALF, 16)]
                copies.append(remote(piece, piece, *sems(0), lat, other_core))
            else:
                axis = order[{1: 0, 2: 1, 3: 2, 4: 1, 5: 0}[stage]]
                for d in (1, 3, 2):
                    c = turned(axis, d)
                    if stage == 1:
                        src, dst = s1.at[a, aligned(c * QUARTER, QUARTER, 16)], p1.at[a, d - 1]
                    elif stage == 2:
                        src, dst = s2.at[a, aligned(c * SHARD, SHARD, 16)], p2.at[a, d - 1]
                    elif stage == 3:
                        src, dst = s3.at[a], p3.at[a, coords[axis]]
                    elif stage == 4:
                        src = dst = total.at[aligned(shard, SHARD, 16)]
                    else:
                        src = dst = total.at[aligned(quarter, QUARTER, 16)]
                    copies.append(remote(src, dst, *sems(d - 1), *along(axis, c)))
        return copies

    def ar_start(stage):
        for copy in part_copies(stage):
            copy.start()

    def ar_finish(stage):
        for copy in part_copies(stage):
            copy.wait()
        for a, order in enumerate(orders):
            own = a * PART + ci * HALF
            if stage == 0:

                def body(b, a=a, own=own):
                    here = grads[aligned(own + b * QUARTER, QUARTER, 16), :].astype(F32)
                    at = aligned(b * QUARTER, QUARTER, 16)
                    s1[a, at, :] = (here + p0[a, at, :].astype(F32)).astype(BF16)

                loop(0, 4, body)
            elif stage in (1, 2):
                size = QUARTER if stage == 1 else SHARD
                src, came, dst = (s1, p1, s2) if stage == 1 else (s2, p2, s3)
                here = src[a, aligned(coords[order[stage - 1]] * size, size, 16), :].astype(F32)
                for d in range(3):
                    here += came[a, d].astype(F32)
                dst[a] = here.astype(BF16)
            elif stage == 3:
                p3[a, coords[order[2]]] = s3[a]
                whole = p3[a, 0].astype(F32)
                for d in range(1, 4):
                    whole += p3[a, d].astype(F32)
                quarter = own + coords[order[0]] * QUARTER
                at = aligned(quarter + coords[order[1]] * SHARD, SHARD, 16)
                total[at, :] = whole.astype(BF16)

    ar_start(0)

    def keep_gp(rows, acc):
        x = tile4(base[rows]).astype(F32)
        s = sigmoid(x)
        grad = tile4(gmid[rows]).astype(F32) + acc * (s * (1.0 + x * (1.0 - s)))
        gp[rows.start * COLS : rows.stop * COLS, :] = (
            grad * tile4(inv[rows])
        ).astype(BF16)

    conv(x3_mid, conv_t, 0, keep_gp)
    ar_finish(0)
    ar_start(1)

    esum[...] = jnp.zeros_like(esum)

    def vg_copy(j):
        dx, dy, dz = offset(j)
        sx, sy, sz = lax.rem(xi + 4 - dx, 4), lax.rem(yi + 4 - dy, 4), lax.rem(lat + 4 - dz, 4)
        return remote(vg.at[j], relay.at[chip], vg_send, vg_recv, sz, sx * 8 + sy * 2 + ci)

    def gather(b):
        at = slice(b * 512, b * 512 + 512)
        chips = slice(b * 8, b * 8 + 8)
        hot = jnp.where(
            colb[at, :].astype(F32) == iota((512, COLS), 1).astype(F32), 1.0, 0.0
        ).astype(BF16)
        row_of = rowb[at, :]
        pieces = [
            jnp.where(row_of == jnp.array(r, BF16), hot, jnp.zeros_like(hot)) for r in range(ROWS)
        ]
        found = dot(jnp.concatenate(pieces, axis=1), gp[...])
        grad = (found * weight[at, :]).astype(BF16)
        vg[chips] = dot(grad, embed_t[...]).astype(BF16).reshape(8, 2, CAP, VALS)
        own = vals[chips].reshape(512, VALS)
        esum[...] += lax.dot_general(own, grad, TN, preferred_element_type=F32)
        for j in range(8 * b, 8 * b + 8):
            if j == 0:
                pltpu.make_async_copy(vg.at[0], relay.at[chip], vg_recv).start()
            else:
                vg_copy(j).start()

    gather(0)
    gather(1)
    gather(2)
    ar_finish(1)
    ar_start(2)
    gather(3)
    ar_finish(2)
    ar_start(3)
    gather(4)
    gather(5)
    ar_finish(3)
    ar_start(4)
    gather(6)
    gather(7)
    ar_finish(4)
    ar_start(5)

    member = yc
    column = xi * 4 + lat

    def embed_copies(stage):
        copies = []
        for d in range(1, 16 if stage == 1 else 8):
            if stage == 1:
                c = lax.rem(column + d, 16)
                tlat, tlon = lax.rem(c, 4), lax.div(c, 4) * 8 + member
                src, dst = esum.at[aligned(member * 16, 16, 16)], qe.at[column]
            else:
                m = lax.rem(member + d, 8)
                tlat, tlon = lat, xi * 8 + m
                if stage == 0:
                    src, dst = esum.at[aligned(m * 16, 16, 16)], pe.at[d - 1]
                else:
                    src = dst = etotal.at[aligned(member * 16, 16, 16)]
            copies.append(remote(src, dst, em_send.at[stage, d - 1], em_recv.at[stage, d - 1], tlat, tlon))
        return copies

    def embed_start(stage):
        for copy in embed_copies(stage):
            copy.start()

    def embed_wait(stage):
        for copy in embed_copies(stage):
            copy.wait()

    embed_start(0)
    widen(act_one, x3_act)
    halo_finish(act_one, 3, x3_act)

    def keep_enc(rows, acc):
        enc[rows] = grid4((tile4(mid[rows]).astype(F32) + acc).astype(BF16))

    conv(x3_act, conv_w, 1, keep_enc, 0, 2)
    embed_wait(0)
    own_rows = aligned(member * 16, 16, 16)
    mine = esum[own_rows, :]
    for d in range(7):
        mine += pe[d]
    esum[own_rows, :] = mine
    embed_start(1)
    conv(x3_act, conv_w, 1, keep_enc, 2, 4)
    enc_copy = pltpu.make_async_copy(enc, enc_out, local_sem.at[2])
    enc_copy.start()
    embed_wait(1)
    qe[column] = esum[own_rows, :]
    whole = qe[0]
    for d in range(1, 16):
        whole += qe[d]
    etotal[own_rows, :] = whole
    embed_start(2)
    ar_finish(5)
    ar_start(6)
    await_bytes(relay, vg_recv)
    vg_own = pltpu.make_async_copy(relay.at[:, ci], vg_out.at[:, ci], local_sem.at[5])
    vg_own.start()
    vg_other = remote(
        relay.at[:, 1 - ci], vg_out.at[:, ci], pair_send.at[1], pair_recv.at[1], lat, other_core
    )
    vg_other.start()
    ar_finish(6)
    grads_copy = pltpu.make_async_copy(total, grads_out, local_sem.at[3])
    grads_copy.start()
    embed_wait(2)
    embed_out[...] = etotal[...] * (1.0 / 512.0)
    for g in range(4):
        await_bytes(vals.at[pl.ds(0, 15 if g == 0 else 16)], a2a_send.at[g])
    for stage in range(3):
        meta_sent(stage)
    await_bytes(vg.at[pl.ds(0, 63)], vg_send)
    vg_own.wait()
    vg_other.wait()
    enc_copy.wait()
    grads_copy.wait()


def on_device(
    obs_values, obs_cells, obs_subcell, slot_counts, sharpness, embed_weight, conv_weight, cotangent
):
    cells = obs_cells.reshape(DEVICES, CAP)
    subs = obs_subcell.reshape(DEVICES, CAP)
    live = lax.broadcasted_iota(jnp.int32, (DEVICES, CAP), 1) < slot_counts.reshape(DEVICES, 1)
    i, j = subs >> 3, subs & 7
    u = jnp.where(i >= 4, i - 4, 3 - i)
    v = jnp.where(j >= 4, j - 4, 3 - j)
    row = cells >> 7
    radius = (2 * u + 1) * (2 * u + 1) + (2 * v + 1) * (2 * v + 1)
    column = jnp.where(live, cells & 127, 255)
    meta = jnp.concatenate([column, row * 16 + u * 4 + v, radius, row], axis=1).astype(F32)
    anywhere = pl.BlockSpec(memory_space=pl.ANY)
    vmem = pl.BlockSpec(memory_space=pltpu.VMEM)
    grid = (ROWS, COLS, CH)
    wide = (ROWS + 2, COLS, 3 * CH)
    dma = pltpu.SemaphoreType.DMA
    scratch = [
        pltpu.VMEM((64, 2, CAP, VALS), BF16),
        pltpu.VMEM((64, 2, CAP, VALS), BF16),
        pltpu.VMEM((64, 2, CAP, VALS), BF16),
        pltpu.VMEM((4, 4, 8, 1, 128), F32),
        pltpu.VMEM((4, 4, 8, 1, 128), F32),
        pltpu.VMEM((8, 4, 4, 1, 128), F32),
        pltpu.VMEM((GROUP, 128), BF16),
        pltpu.VMEM((OBS, 128), BF16),
        pltpu.VMEM((OBS, 128), BF16),
        pltpu.VMEM((OBS, CH), F32),
        pltpu.VMEM((GROUP, CH), BF16),
        pltpu.VMEM((GROUP, 256), BF16),
        pltpu.VMEM((COLS, GROUP), BF16),
        pltpu.VMEM((16, GROUP), F32),
        pltpu.VMEM((CELLS, CH), F32),
        pltpu.VMEM((COLS, 256), F32),
        pltpu.VMEM(grid, F32),
        pltpu.VMEM(grid, BF16),
        pltpu.VMEM((2, 3, 3 * CH, CH), BF16),
        pltpu.VMEM((2, 3, 3 * CH, CH), BF16),
        pltpu.VMEM((CH, VALS), BF16),
        pltpu.VMEM(grid, F32),
        pltpu.VMEM(grid, BF16),
        pltpu.VMEM(grid, BF16),
        pltpu.VMEM(grid, BF16),
        pltpu.VMEM(grid, BF16),
        pltpu.VMEM(grid, BF16),
        pltpu.VMEM((CELLS, CH), BF16),
        pltpu.VMEM((CH, CELLS), BF16),
        pltpu.VMEM((CH, CELLS), BF16),
        pltpu.VMEM(wide, BF16),
        pltpu.VMEM(wide, BF16),
        pltpu.VMEM(wide, BF16),
        pltpu.VMEM((4, 2, COLS, CH), BF16),
        pltpu.VMEM((4, 2, 3, 16, CH), BF16),
        pltpu.VMEM((4, 2, 16, CH), BF16),
        pltpu.VMEM((2, 16, CH), F32),
        pltpu.VMEM((64, 2, CAP, VALS), BF16),
        pltpu.VMEM((3 * PART, CH), BF16),
        pltpu.VMEM((3 * PART, CH), BF16),
        pltpu.VMEM((3, HALF, CH), BF16),
        pltpu.VMEM((3, HALF, CH), BF16),
        pltpu.VMEM((3, 3, QUARTER, CH), BF16),
        pltpu.VMEM((3, QUARTER, CH), BF16),
        pltpu.VMEM((3, 3, SHARD, CH), BF16),
        pltpu.VMEM((3, SHARD, CH), BF16),
        pltpu.VMEM((3, 4, SHARD, CH), BF16),
        pltpu.VMEM((VALS, CH), F32),
        pltpu.VMEM((7, 16, CH), F32),
        pltpu.VMEM((16, 16, CH), F32),
        pltpu.VMEM((VALS, CH), F32),
        pltpu.VMEM(grid, BF16),
        dma((6,)),
        dma((2,)),
        dma((2,)),
        dma((4,)),
        dma((4,)),
        dma((3,)),
        dma((3,)),
        dma,
        dma,
        dma((4, 8)),
        dma((4, 8)),
        dma((7, 3, 3)),
        dma((7, 3, 3)),
        dma((3, 15)),
        dma((3, 15)),
    ]
    encoded, value_grads, grads, embed_total = pl.pallas_call(
        kernel,
        out_shape=(
            jax.ShapeDtypeStruct(grid, BF16),
            jax.ShapeDtypeStruct((64, 2, CAP, VALS), BF16),
            jax.ShapeDtypeStruct((3 * PART, CH), BF16),
            jax.ShapeDtypeStruct((VALS, CH), F32),
        ),
        in_specs=[anywhere, anywhere, vmem, vmem, anywhere, anywhere],
        out_specs=(anywhere, anywhere, anywhere, vmem),
        scratch_shapes=scratch,
        compiler_params=pltpu.CompilerParams(
            has_side_effects=True, vmem_limit_bytes=60 * 1024 * 1024
        ),
        cost_estimate=pl.CostEstimate(
            flops=30_000_000_000, bytes_accessed=20_000_000, transcendentals=4_000_000
        ),
    )(
        obs_values.reshape(64, 2, CAP, VALS),
        meta.reshape(4, 4, 8, 1, 128),
        sharpness.reshape(1, CH),
        embed_weight,
        conv_weight.reshape(2, 3, 3 * CH, CH),
        cotangent,
    )
    conv_grads = grads.astype(F32) * (1.0 / 512.0)
    return (
        encoded,
        value_grads.reshape(OBS, VALS),
        conv_grads.reshape(2, 3, 3, CH, CH),
        embed_total,
    )


def solution(mesh):
    placed = (
        P(("lat", "lon"), None),
        P(("lat", "lon")),
        P(("lat", "lon")),
        P(("lat", "lon"), None),
        P(),
        P(),
        P(),
        P("lat", "lon", None),
    )
    return jax.shard_map(
        on_device,
        mesh=mesh,
        in_specs=placed,
        out_specs=(P("lat", "lon", None), P(("lat", "lon"), None), P(), P()),
        check_vma=False,
    )
```

```python
import jax
import jax.numpy as jnp
from jax import lax
from jax.experimental import pallas as pl
from jax.experimental.pallas import tpu as pltpu
from jax.sharding import PartitionSpec as P

F32 = jnp.float32
BF16 = jnp.bfloat16
N_LAT, N_LON = 4, 32
DEVICES = N_LAT * N_LON
CAP, VALS, CH = 32, 128, 256
ROWS, COLS = 16, 128
CELLS = ROWS * COLS
OBS = DEVICES * CAP
GROUP = 32 * CAP
PART, HALF, QUARTER, SHARD = 1536, 768, 192, 48
NT = (((1,), (1,)), ((), ()))
TN = (((0,), (0,)), ((), ()))


def dot(a, b):
    return jnp.dot(a, b, preferred_element_type=F32)


def iota(shape, axis):
    return lax.broadcasted_iota(jnp.int32, shape, axis)


def sigmoid(x):
    return 0.5 + 0.5 * jnp.tanh(0.5 * x)


def remote(src, dst, send, recv, lat, lon):
    return pltpu.make_async_remote_copy(
        src_ref=src,
        dst_ref=dst,
        send_sem=send,
        recv_sem=recv,
        device_id=(lat, lon),
        device_id_type=pl.DeviceIdType.MESH,
    )


def await_bytes(ref, sem):
    pltpu.make_async_copy(ref, ref, sem).wait()


def loop(low, high, body):
    def step(i, carry):
        body(i)
        return carry

    lax.fori_loop(low, high, step, 0)


def aligned(start, size, unit):
    return pl.ds(pl.multiple_of(start, unit), size)


def kernel(
    obs_in, cells, subs, live_counts, sharp, embed_w, conv_in, cot_in,
    enc_out, vg_out, grads_out, embed_out,
    vals, queue, relay, meta_own, meta_z, meta_x, meta, tmeta, colb, rowb, weight, ew, rk, colhot, rowl, placed, counts, inv,
    cot, conv_w, embed_t, back, bend, base, act_zero, mid, act_one, gmid, gp, act_t, zero_t,
    x3_act, x3_cot, x3_mid, hrow, hcol, strip, stripf,
    vg, grads, total, p0, s1, p1, s2, p2, s3, p3, esum, pe, qe, etotal, enc,
    local_sem, pair_send, pair_recv, a2a_send, a2a_recv, meta_send, meta_recv, vg_send, vg_recv,
    halo_send, halo_recv, ar_send, ar_recv, em_send, em_recv,
):
    lat = lax.axis_index("lat")
    lon = lax.axis_index("lon")
    me = lat * N_LON + lon
    xi, yi, ci = lax.div(lon, 8), lax.rem(lax.div(lon, 2), 4), lax.rem(lon, 2)

    chip = lat * 16 + xi * 4 + yi
    yc = lax.rem(lon, 8)
    other_core = lon + 1 - 2 * ci

    def offset(j):
        g, dx, dy = lax.div(j, 16), lax.rem(lax.div(j, 4), 4), lax.rem(j, 4)
        return dx, dy, lax.rem(g + 8 - dx - dy, 4)

    barrier = pltpu.get_barrier_semaphore()

    cot_copy = pltpu.make_async_copy(cot_in, cot, local_sem.at[0])
    cot_copy.start()
    pair_own = pltpu.make_async_copy(obs_in.at[:, ci], queue.at[:, ci], local_sem.at[4])
    pair_own.start()
    pair_other = remote(
        obs_in.at[:, 1 - ci], queue.at[:, ci], pair_send.at[0], pair_recv.at[0], lat, other_core
    )

    def greet(j):
        tlat, tlon = lax.rem(lat + lax.div(j, N_LON), N_LAT), lax.rem(lon + lax.rem(j, N_LON), N_LON)
        pl.semaphore_signal(
            barrier, inc=1, device_id=(tlat, tlon), device_id_type=pl.DeviceIdType.MESH
        )

    loop(1, DEVICES, greet)

    def meta_copies(stage):
        copies = []
        for d in range(1, 8 if stage == 2 else 4):
            if stage == 0:
                c = lax.rem(lat + d, 4)
                src, dst, target = meta_own.at[:, pl.ds(c * 8, 8)], meta_z.at[lat], (c, lon)
            elif stage == 1:
                c = lax.rem(xi + d, 4)
                src, dst = meta_z.at[:, :, pl.ds(c * 2, 2)], meta_x.at[xi]
                target = (lat, c * 8 + yc)
            else:
                c = lax.rem(yc + d, 8)
                src, dst = meta_x.at[:, :, lax.rem(c, 4), lax.div(c, 4)], meta.at[yc]
                target = (lat, xi * 8 + c)
            copies.append(remote(src, dst, meta_send.at[stage], meta_recv.at[stage], *target))
        own = (
            (meta_own.at[:, pl.ds(lat * 8, 8)], meta_z.at[lat]),
            (meta_z.at[:, :, pl.ds(xi * 2, 2)], meta_x.at[xi]),
            (meta_x.at[:, :, lax.rem(yc, 4), lax.div(yc, 4)], meta.at[yc]),
        )[stage]
        copies.append(pltpu.make_async_copy(*own, meta_recv.at[stage]))
        return copies

    def meta_start(stage):
        for copy in meta_copies(stage):
            copy.start()

    def meta_wait(stage):
        await_bytes((meta_z, meta_x, meta)[stage], meta_recv.at[stage])

    def meta_sent(stage):
        await_bytes((meta_z, meta_x, meta)[stage].at[pl.ds(0, (3, 3, 7)[stage])], meta_send.at[stage])

    line, lane = iota((32, 128), 0), iota((32, 128), 1)
    own_four = jnp.where(lax.div(lane, 4) == line, live_counts[...].astype(F32), 0.0).astype(BF16)
    to_slots = jnp.where(
        lax.rem(iota((128, 128), 0), 4) == lax.div(iota((128, 128), 1), 32), 1.0, 0.0
    ).astype(BF16)
    live = lax.rem(lane, 32).astype(F32) < dot(own_four, to_slots)
    cell, sub = cells[...], subs[...]
    u, v = sub >> 3, sub & 7
    u = jnp.where(u >= 4, u - 4, 3 - u)
    v = jnp.where(v >= 4, v - 4, 3 - v)
    row = cell >> 7
    fields = [
        jnp.where(live, (cell & 127).astype(F32), 255.0),
        (row * 16 + u * 4 + v).astype(F32),
        ((2 * u + 1) * (2 * u + 1) + (2 * v + 1) * (2 * v + 1)).astype(F32),
        row.astype(F32),
    ]
    for i in range(4):
        mixed = jnp.zeros((32, 128), F32)
        for f in range(4):
            shift = (f - i) * 32 % 128
            turned_field = pltpu.roll(fields[f], shift, 1) if shift else fields[f]
            mixed = jnp.where(lax.div(lane, 32) == f, turned_field, mixed)
        for r in range(32):
            meta_own[i, r] = mixed[r : r + 1, :]

    conv_copy = pltpu.make_async_copy(conv_in, conv_w, local_sem.at[1])
    conv_copy.start()

    def send_slot(j):
        dx, dy, dz = offset(j)
        tx, ty, tz = lax.rem(xi + dx, 4), lax.rem(yi + dy, 4), lax.rem(lat + dz, 4)
        g = lax.div(j, 16)
        remote(
            queue.at[tz * 16 + tx * 4 + ty], vals.at[j], a2a_send.at[g], a2a_recv.at[g],
            tz, tx * 8 + ty * 2 + ci,
        ).start()

    north, south = lax.rem(lat + 3, N_LAT), lax.rem(lat + 1, N_LAT)
    west, east = lax.rem(lon + N_LON - 1, N_LON), lax.rem(lon + 1, N_LON)

    def halo_copies(src, k):
        pieces = [
            (src.at[ROWS - 1], hrow.at[k, 0], south, lon),
            (src.at[0], hrow.at[k, 1], north, lon),
        ]
        for side, column, target in ((0, 1, east), (1, 0, west)):
            for turn, tlat in enumerate((lat, south, north)):
                pieces.append((strip.at[k, column], hcol.at[k, side, turn], tlat, target))
        return [
            remote(s, d, halo_send.at[k, i], halo_recv.at[k, i], a, b)
            for i, (s, d, a, b) in enumerate(pieces)
        ]

    def halo_pack(src, k):
        for r in range(ROWS):
            stripf[0, r : r + 1, :] = src[r, 0:16, :].astype(F32)[0:1, :]
            stripf[1, r : r + 1, :] = src[r, COLS - 16 : COLS, :].astype(F32)[15:16, :]
        strip[k, 0] = stripf[0].astype(BF16)
        strip[k, 1] = stripf[1].astype(BF16)

    def halo_start(src, k):
        for copy in halo_copies(src, k):
            copy.start()

    def widen(src, x3, low=0, high=4):
        def body(b):
            for i in range(4):
                r = 4 * b + i
                row = src[r].astype(F32)
                x3[r + 1, :, 0:CH] = pltpu.roll(row, 1, 0).astype(BF16)
                x3[r + 1, :, CH : 2 * CH] = src[r]
                x3[r + 1, :, 2 * CH : 3 * CH] = pltpu.roll(row, COLS - 1, 0).astype(BF16)

        loop(low, high, body)

    def halo_finish(src, k, x3):
        for copy in halo_copies(src, k):
            copy.wait()
        first = iota((16, CH), 0) == 0
        last = iota((16, CH), 0) == 15
        left = hcol[k, 0, 0].astype(F32)
        right = hcol[k, 1, 0].astype(F32)
        for r in range(ROWS):
            low = x3[r + 1, 0:16, 0:CH].astype(F32)
            x3[r + 1, 0:16, 0:CH] = jnp.where(first, left[r : r + 1, :], low).astype(BF16)
            high = x3[r + 1, COLS - 16 : COLS, 2 * CH : 3 * CH].astype(F32)
            x3[r + 1, COLS - 16 : COLS, 2 * CH : 3 * CH] = jnp.where(
                last, right[r : r + 1, :], high
            ).astype(BF16)
        spot = iota((COLS, CH), 0)
        for side, r, turn, pick, valid in (
            (0, 0, 1, ROWS - 1, lat > 0),
            (1, ROWS + 1, 2, 0, lat < N_LAT - 1),
        ):
            keep = jnp.where(valid, 1.0, 0.0).astype(F32)
            row = hrow[k, side].astype(F32) * keep
            lcorner = hcol[k, 0, turn].astype(F32)[pick : pick + 1, :] * keep
            rcorner = hcol[k, 1, turn].astype(F32)[pick : pick + 1, :] * keep
            x3[r, :, 0:CH] = jnp.where(spot == 0, lcorner, pltpu.roll(row, 1, 0)).astype(BF16)
            x3[r, :, CH : 2 * CH] = row.astype(BF16)
            x3[r, :, 2 * CH : 3 * CH] = jnp.where(
                spot == COLS - 1, rcorner, pltpu.roll(row, COLS - 1, 0)
            ).astype(BF16)

    def conv(x3, k, finish, flip=False, low=0, high=4):
        if flip:
            taps = [
                conv_w[k, 2 - p, (2 - q) * CH : (3 - q) * CH, :] for p in range(3) for q in range(3)
            ]
            taps = jnp.concatenate(taps, axis=1)
        else:
            taps = conv_w[k].reshape(9 * CH, CH)
        for b in range(low, high):
            near = [x3[4 * b + p : 4 * b + p + 4].reshape(4 * COLS, 3 * CH) for p in range(3)]
            near = jnp.concatenate(near, axis=1)
            if flip:
                acc = lax.dot_general(near, taps, NT, preferred_element_type=F32)
            else:
                acc = dot(near, taps)
            finish(slice(4 * b, 4 * b + 4), acc)

    def tile4(x):
        return x.reshape(4 * COLS, CH)

    def grid4(x):
        return x.reshape(4, COLS, CH)

    def turn_act(act, act_t):
        for r in range(ROWS):
            act_t[:, r * COLS : (r + 1) * COLS] = act[r].T

    cot_copy.wait()
    halo_pack(cot, 0)
    pl.semaphore_wait(barrier, DEVICES - 1)
    pair_other.start()
    meta_start(0)
    halo_start(cot, 0)
    widen(cot, x3_cot, 0, 2)
    meta_wait(0)
    meta_start(1)
    widen(cot, x3_cot, 2, 4)
    meta_wait(1)
    meta_start(2)
    pair_own.wait()
    pair_other.wait()
    pltpu.make_async_copy(queue.at[chip], vals.at[0], a2a_recv.at[0]).start()
    loop(1, 64, send_slot)
    conv_copy.wait()
    embed_t[...] = embed_w[...].T
    halo_finish(cot, 0, x3_cot)

    def keep_back(rows, acc):
        back[rows] = grid4(acc)

    conv(x3_cot, 1, keep_back, flip=True)
    meta_wait(2)

    placed[...] = jnp.zeros_like(placed)
    counts[...] = jnp.zeros_like(counts)
    slot_mask = jnp.where(
        lax.rem(iota((CAP, 128), 1), 32) == iota((CAP, 128), 0), 1.0, 0.0
    ).astype(F32)
    spread = jnp.where(
        lax.div(iota((128, 512), 0), 32) == lax.div(iota((128, 512), 1), 128), 1.0, 0.0
    ).astype(BF16)
    lane, line = iota((COLS + 16, 128), 1), iota((COLS + 16, 128), 0)
    pick = jnp.where(lax.div(lane, 32) == jnp.where(line < COLS, 0, 3), 1.0, 0.0).astype(BF16)
    decay = sharp[...] * (-1.0 / 256.0)

    for g in range(4):
        def stretch(b, g=g):
            for i in range(8):
                s = 8 * b + i
                dx, dy, dz = offset(g * 16 + 4 * b + i // 2)
                sx, sy = lax.rem(xi + 4 - dx, 4), lax.rem(yi + 4 - dy, 4)
                source = meta[sy * 2 + i % 2, sx, lax.rem(lat + 4 - dz, 4)]
                line = jnp.broadcast_to(source, (CAP, 128)) * slot_mask
                tmeta[aligned(s * CAP, CAP, CAP), :] = line.astype(BF16)

        loop(0, 4, stretch)
        await_bytes(vals.at[pl.ds(g * 16, 16)], a2a_recv.at[g])

        for b in range(4):
            at = slice(b * 256, b * 256 + 256)
            of = slice(g * GROUP + b * 256, g * GROUP + b * 256 + 256)
            wide = dot(tmeta[at, :], spread)
            colb[of, :] = wide[:, 0:128].astype(BF16)
            rowb[of, :] = wide[:, 384:512].astype(BF16)
            rk_of = jnp.concatenate([wide[:, 128:256]] * 2, axis=1)
            radius = jnp.concatenate([wide[:, 256:384]] * 2, axis=1)
            rk[at, :] = jnp.where(
                rk_of == iota((256, 256), 1).astype(F32), 1.0, 0.0
            ).astype(BF16)
            w = jnp.exp(radius * decay)
            weight[of, :] = w
            ew[at, :] = (dot(vals[g * 16 + 4 * b : g * 16 + 4 * b + 4].reshape(256, VALS), embed_w[...]) * w).astype(BF16)

        both = lax.dot_general(pick, tmeta[...], NT, preferred_element_type=F32)
        colhot[...] = jnp.where(
            both[0:COLS] == iota((COLS, GROUP), 0).astype(F32), 1.0, 0.0
        ).astype(BF16)
        rowl[...] = both[COLS : COLS + 16]
        counts[...] += dot(colhot[...], rk[...])

        hot = colhot[...].reshape(8, 16, GROUP)
        for b in range(4):
            rows = []
            for r in range(4 * b, 4 * b + 4):
                mask = jnp.where(rowl[...] == float(r), 1.0, 0.0).astype(BF16)
                rows.append((hot * mask[None]).reshape(COLS, GROUP))
            at = slice(b * 512, b * 512 + 512)
            placed[at, :] += dot(jnp.concatenate(rows, axis=0), ew[...])

    kind = lax.rem(iota((256, CH), 0), 16)
    half_u, half_v = 2 * lax.div(kind, 4) + 1, 2 * lax.rem(kind, 4) + 1
    table = jnp.exp((half_u * half_u + half_v * half_v).astype(F32) * decay)
    table_hi = table.astype(BF16)
    table_lo = (table - table_hi.astype(F32)).astype(BF16)
    tables = jnp.concatenate([table_hi, table_lo], axis=0)
    row_of_lane = lax.div(iota((COLS, 256), 1), 16)
    for b in range(4):
        rows = []
        for r in range(4 * b, 4 * b + 4):
            rows.append(jnp.where(row_of_lane == r, counts[...], 0.0).astype(BF16))
        tally = jnp.concatenate(rows, axis=0)
        recip = 1.0 / (dot(jnp.concatenate([tally, tally], axis=1), tables) + 1.0)
        at = slice(4 * b, 4 * b + 4)
        inv[at] = grid4(recip)
        value = (placed[b * 512 : b * 512 + 512, :] * recip).astype(BF16)
        base[at] = grid4(value)
        x = value.astype(F32)
        s = sigmoid(x)
        act_zero[at] = grid4((x * s).astype(BF16))
        bend[at] = grid4(s * (1.0 + x * (1.0 - s)))

    halo_pack(act_zero, 1)
    halo_start(act_zero, 1)
    widen(act_zero, x3_act)
    turn_act(act_zero, zero_t)
    halo_finish(act_zero, 1, x3_act)

    def keep_mid(rows, acc):
        value = (tile4(base[rows]).astype(F32) + acc).astype(BF16)
        mid[rows] = grid4(value)
        x = value.astype(F32)
        s = sigmoid(x)
        act_one[rows] = grid4((x * s).astype(BF16))
        slope = s * (1.0 + x * (1.0 - s))
        grad = tile4(cot[rows]).astype(F32) + tile4(back[rows]) * slope
        gmid[rows] = grid4(grad.astype(BF16))

    conv(x3_act, 0, keep_mid)
    halo_pack(gmid, 2)
    halo_start(gmid, 2)
    halo_pack(act_one, 3)
    halo_start(act_one, 3)

    def kernel_grad(act_t, x3, k):
        for p in range(3):
            block = dot(act_t[...], x3[2 - p : 2 - p + ROWS].reshape(CELLS, 3 * CH))
            for q in range(3):
                for h in range(2):
                    at, lanes = (6 * p + 2 * q + h) * CH, (2 - q) * CH + h * 128
                    grads[k, at : at + CH, :] = block[:, lanes : lanes + 128].astype(BF16)

    coords = {"x": xi, "y": yi, "z": lat}
    orders = (("x", "y", "z"), ("y", "z", "x"), ("z", "x", "y"))

    def along(axis, c):
        cx, cy, cz = [c if axis == n else coords[n] for n in ("x", "y", "z")]
        return cz, cx * 8 + cy * 2 + ci

    def turned(axis, d):
        return lax.rem(coords[axis] + d, 4)

    def part_copies(k, stage):
        copies = []
        for a, order in enumerate(orders):
            own = a * PART + ci * HALF
            sems = lambda d: (ar_send.at[k, stage, a, d], ar_recv.at[k, stage, a, d])
            quarter = own + coords[order[0]] * QUARTER
            shard = quarter + coords[order[1]] * SHARD
            if stage == 0:
                src = grads.at[k, aligned(a * PART + (1 - ci) * HALF, HALF, 16)]
                copies.append(remote(src, p0.at[k, a], *sems(0), lat, other_core))
            elif stage == 6:
                piece = total.at[k, aligned(own, HALF, 16)]
                copies.append(remote(piece, piece, *sems(0), lat, other_core))
            else:
                axis = order[{1: 0, 2: 1, 3: 2, 4: 1, 5: 0}[stage]]
                for d in (1, 3, 2):
                    c = turned(axis, d)
                    if stage == 1:
                        src = s1.at[k, a, aligned(c * QUARTER, QUARTER, 16)]
                        dst = p1.at[k, a, d - 1]
                    elif stage == 2:
                        src = s2.at[k, a, aligned(c * SHARD, SHARD, 16)]
                        dst = p2.at[k, a, d - 1]
                    elif stage == 3:
                        src, dst = s3.at[k, a], p3.at[k, a, coords[axis]]
                    elif stage == 4:
                        src = dst = total.at[k, aligned(shard, SHARD, 16)]
                    else:
                        src = dst = total.at[k, aligned(quarter, QUARTER, 16)]
                    copies.append(remote(src, dst, *sems(d - 1), *along(axis, c)))
        return copies

    def ar_start(k, stage):
        for copy in part_copies(k, stage):
            copy.start()

    def ar_finish(k, stage):
        for copy in part_copies(k, stage):
            copy.wait()
        for a, order in enumerate(orders):
            own = a * PART + ci * HALF
            if stage == 0:
                here = grads[k, aligned(own, HALF, 16), :].astype(F32)
                s1[k, a] = (here + p0[k, a].astype(F32)).astype(BF16)
            elif stage in (1, 2):
                size = QUARTER if stage == 1 else SHARD
                src, came, dst = (s1, p1, s2) if stage == 1 else (s2, p2, s3)
                at = aligned(coords[order[stage - 1]] * size, size, 16)
                here = src[k, a, at, :].astype(F32)
                for d in range(3):
                    here += came[k, a, d].astype(F32)
                dst[k, a] = here.astype(BF16)
            elif stage == 3:
                p3[k, a, coords[order[2]]] = s3[k, a]
                whole = p3[k, a, 0].astype(F32)
                for d in range(1, 4):
                    whole += p3[k, a, d].astype(F32)
                quarter = own + coords[order[0]] * QUARTER
                at = aligned(quarter + coords[order[1]] * SHARD, SHARD, 16)
                total[k, at, :] = whole.astype(BF16)

    def ar_step(k, stage):
        ar_finish(k, stage)
        ar_start(k, stage + 1)

    def ar_leave(k):
        return pltpu.make_async_copy(total.at[k], grads_out.at[k], local_sem.at[3 if k else 6])

    turn_act(act_one, act_t)
    kernel_grad(act_t, x3_cot, 1)
    ar_start(1, 0)
    widen(gmid, x3_mid)
    halo_finish(gmid, 2, x3_mid)
    ar_step(1, 0)
    kernel_grad(zero_t, x3_mid, 0)
    ar_start(0, 0)

    def keep_gp(rows, acc):
        grad = tile4(gmid[rows]).astype(F32) + acc * tile4(bend[rows])
        gp[rows.start * COLS : rows.stop * COLS, :] = (
            grad * tile4(inv[rows])
        ).astype(BF16)

    conv(x3_mid, 0, keep_gp, flip=True, low=0, high=2)
    ar_step(1, 1)
    ar_step(0, 0)
    conv(x3_mid, 0, keep_gp, flip=True, low=2, high=4)

    esum[...] = jnp.zeros_like(esum)

    def vg_copy(j):
        dx, dy, dz = offset(j)
        sx, sy, sz = lax.rem(xi + 4 - dx, 4), lax.rem(yi + 4 - dy, 4), lax.rem(lat + 4 - dz, 4)
        return remote(vg.at[j], relay.at[chip], vg_send, vg_recv, sz, sx * 8 + sy * 2 + ci)

    def gather(b):
        at = slice(b * 512, b * 512 + 512)
        chips = slice(b * 8, b * 8 + 8)
        hot = jnp.where(
            colb[at, :].astype(F32) == iota((512, COLS), 1).astype(F32), 1.0, 0.0
        ).astype(BF16)
        row_of = rowb[at, :]
        pieces = [
            jnp.where(row_of == jnp.array(r, BF16), hot, jnp.zeros_like(hot)) for r in range(ROWS)
        ]
        found = dot(jnp.concatenate(pieces, axis=1), gp[...])
        grad = (found * weight[at, :]).astype(BF16)
        vg[chips] = dot(grad, embed_t[...]).astype(BF16).reshape(8, 2, CAP, VALS)
        own = vals[chips].reshape(512, VALS)
        esum[...] += lax.dot_general(own, grad, TN, preferred_element_type=F32)
        for j in range(8 * b, 8 * b + 8):
            if j == 0:
                pltpu.make_async_copy(vg.at[0], relay.at[chip], vg_recv).start()
            else:
                vg_copy(j).start()

    gather(0)
    gather(1)
    ar_step(1, 2)
    gather(2)
    ar_step(0, 1)
    gather(3)
    ar_step(1, 3)
    gather(4)
    ar_step(0, 2)
    gather(5)
    ar_step(1, 4)
    gather(6)
    ar_step(0, 3)
    gather(7)
    ar_step(0, 4)

    member = yc
    column = xi * 4 + lat

    def embed_copies(stage):
        copies = []
        for d in range(1, 16 if stage == 1 else 8):
            if stage == 1:
                c = lax.rem(column + d, 16)
                tlat, tlon = lax.rem(c, 4), lax.div(c, 4) * 8 + member
                src, dst = esum.at[aligned(member * 16, 16, 16)], qe.at[column]
            else:
                m = lax.rem(member + d, 8)
                tlat, tlon = lat, xi * 8 + m
                if stage == 0:
                    src, dst = esum.at[aligned(m * 16, 16, 16)], pe.at[d - 1]
                else:
                    src = dst = etotal.at[aligned(member * 16, 16, 16)]
            copies.append(remote(src, dst, em_send.at[stage, d - 1], em_recv.at[stage, d - 1], tlat, tlon))
        return copies

    def embed_start(stage):
        for copy in embed_copies(stage):
            copy.start()

    def embed_wait(stage):
        for copy in embed_copies(stage):
            copy.wait()

    embed_start(0)
    widen(act_one, x3_act)
    halo_finish(act_one, 3, x3_act)
    ar_step(1, 5)

    def keep_enc(rows, acc):
        enc[rows] = grid4((tile4(mid[rows]).astype(F32) + acc).astype(BF16))

    conv(x3_act, 1, keep_enc, low=0, high=2)
    embed_wait(0)
    own_rows = aligned(member * 16, 16, 16)
    mine = esum[own_rows, :]
    for d in range(7):
        mine += pe[d]
    esum[own_rows, :] = mine
    embed_start(1)
    ar_step(0, 5)
    ar_finish(1, 6)
    ar_leave(1).start()
    conv(x3_act, 1, keep_enc, low=2, high=4)
    enc_copy = pltpu.make_async_copy(enc, enc_out, local_sem.at[2])
    enc_copy.start()
    embed_wait(1)
    qe[column] = esum[own_rows, :]
    whole = qe[0]
    for d in range(1, 16):
        whole += qe[d]
    etotal[own_rows, :] = whole
    embed_start(2)
    await_bytes(relay, vg_recv)
    vg_own = pltpu.make_async_copy(relay.at[:, ci], vg_out.at[:, ci], local_sem.at[5])
    vg_own.start()
    vg_other = remote(
        relay.at[:, 1 - ci], vg_out.at[:, ci], pair_send.at[1], pair_recv.at[1], lat, other_core
    )
    vg_other.start()
    ar_finish(0, 6)
    ar_leave(0).start()
    embed_wait(2)
    embed_out[...] = etotal[...] * (1.0 / 512.0)
    for g in range(4):
        await_bytes(vals.at[pl.ds(0, 15 if g == 0 else 16)], a2a_send.at[g])
    for stage in range(3):
        meta_sent(stage)
    await_bytes(vg.at[pl.ds(0, 63)], vg_send)
    vg_own.wait()
    vg_other.wait()
    enc_copy.wait()
    ar_leave(1).wait()
    ar_leave(0).wait()


def hand_over(
    enc_in, vg_in, grads_in, embed_in, enc_out, vg_out, grads_out, embed_out,
    enc, vg, embed, narrow, wide, in_sem, out_sem,
):
    steps = []
    for i in range(18):
        src, dst = slice(i % 9 * 2 * CH, (i % 9 + 1) * 2 * CH), slice(i * CH, i * CH + CH)
        k = i // 9
        steps.append(
            (grads_in.at[k, src], narrow.at[k, src], wide.at[dst], grads_out.at[dst], (k, src, dst))
        )
    for i in range(2):
        at = slice(i * 8, i * 8 + 8)
        steps.append((enc_in.at[at], enc.at[at], enc.at[at], enc_out.at[at], None))
        at = slice(i * 32, i * 32 + 32)
        steps.append((vg_in.at[at], vg.at[at], vg.at[at], vg_out.at[at], None))
    steps.append((embed_in, embed, embed, embed_out, None))
    moves = [
        pltpu.make_async_copy(step[0], step[1], in_sem.at[i]) for i, step in enumerate(steps)
    ]
    for move in moves:
        move.start()
    results = []
    for i, (_, _, src, dst, at) in enumerate(steps):
        moves[i].wait()
        if at is not None:
            k, rows, to = at
            for h in range(2):
                half = slice(rows.start + h * CH, rows.start + h * CH + CH)
                wide[to, h * 128 : h * 128 + 128] = narrow[k, half, :].astype(F32) * (1.0 / 512.0)
        results.append(pltpu.make_async_copy(src, dst, out_sem.at[i]))
        results[i].start()
    for copy in results:
        copy.wait()


def on_device(
    obs_values, obs_cells, obs_subcell, slot_counts, sharpness, embed_weight, conv_weight, cotangent
):
    anywhere = pl.BlockSpec(memory_space=pl.ANY)
    vmem = pl.BlockSpec(memory_space=pltpu.VMEM)
    grid = (ROWS, COLS, CH)
    wide = (ROWS + 2, COLS, 3 * CH)
    dma = pltpu.SemaphoreType.DMA
    scratch = [
        pltpu.VMEM((64, 2, CAP, VALS), BF16),
        pltpu.VMEM((64, 2, CAP, VALS), BF16),
        pltpu.VMEM((64, 2, CAP, VALS), BF16),
        pltpu.VMEM((4, 32, 1, 128), F32),
        pltpu.VMEM((4, 4, 8, 1, 128), F32),
        pltpu.VMEM((4, 4, 4, 2, 1, 128), F32),
        pltpu.VMEM((8, 4, 4, 1, 128), F32),
        pltpu.VMEM((GROUP, 128), BF16),
        pltpu.VMEM((OBS, 128), BF16),
        pltpu.VMEM((OBS, 128), BF16),
        pltpu.VMEM((OBS, CH), F32),
        pltpu.VMEM((GROUP, CH), BF16),
        pltpu.VMEM((GROUP, 256), BF16),
        pltpu.VMEM((COLS, GROUP), BF16),
        pltpu.VMEM((16, GROUP), F32),
        pltpu.VMEM((CELLS, CH), F32),
        pltpu.VMEM((COLS, 256), F32),
        pltpu.VMEM(grid, F32),
        pltpu.VMEM(grid, BF16),
        pltpu.VMEM((2, 3, 3 * CH, CH), BF16),
        pltpu.VMEM((CH, VALS), BF16),
        pltpu.VMEM(grid, F32),
        pltpu.VMEM(grid, F32),
        pltpu.VMEM(grid, BF16),
        pltpu.VMEM(grid, BF16),
        pltpu.VMEM(grid, BF16),
        pltpu.VMEM(grid, BF16),
        pltpu.VMEM(grid, BF16),
        pltpu.VMEM((CELLS, CH), BF16),
        pltpu.VMEM((CH, CELLS), BF16),
        pltpu.VMEM((CH, CELLS), BF16),
        pltpu.VMEM(wide, BF16),
        pltpu.VMEM(wide, BF16),
        pltpu.VMEM(wide, BF16),
        pltpu.VMEM((4, 2, COLS, CH), BF16),
        pltpu.VMEM((4, 2, 3, 16, CH), BF16),
        pltpu.VMEM((4, 2, 16, CH), BF16),
        pltpu.VMEM((2, 16, CH), F32),
        pltpu.VMEM((64, 2, CAP, VALS), BF16),
        pltpu.VMEM((2, 3 * PART, 128), BF16),
        pltpu.VMEM((2, 3 * PART, 128), BF16),
        pltpu.VMEM((2, 3, HALF, 128), BF16),
        pltpu.VMEM((2, 3, HALF, 128), BF16),
        pltpu.VMEM((2, 3, 3, QUARTER, 128), BF16),
        pltpu.VMEM((2, 3, QUARTER, 128), BF16),
        pltpu.VMEM((2, 3, 3, SHARD, 128), BF16),
        pltpu.VMEM((2, 3, SHARD, 128), BF16),
        pltpu.VMEM((2, 3, 4, SHARD, 128), BF16),
        pltpu.VMEM((VALS, CH), F32),
        pltpu.VMEM((7, 16, CH), F32),
        pltpu.VMEM((16, 16, CH), F32),
        pltpu.VMEM((VALS, CH), F32),
        pltpu.VMEM(grid, BF16),
        dma((7,)),
        dma((2,)),
        dma((2,)),
        dma((4,)),
        dma((4,)),
        dma((3,)),
        dma((3,)),
        dma,
        dma,
        dma((4, 8)),
        dma((4, 8)),
        dma((2, 7, 3, 3)),
        dma((2, 7, 3, 3)),
        dma((3, 15)),
        dma((3, 15)),
    ]
    encoded, value_grads, grads, embed_total = pl.pallas_call(
        kernel,
        out_shape=(
            jax.ShapeDtypeStruct(grid, BF16),
            jax.ShapeDtypeStruct((64, 2, CAP, VALS), BF16),
            jax.ShapeDtypeStruct((2, 3 * PART, 128), BF16),
            jax.ShapeDtypeStruct((VALS, CH), F32),
        ),
        in_specs=[anywhere, vmem, vmem, vmem, vmem, vmem, anywhere, anywhere],
        out_specs=(anywhere, anywhere, anywhere, vmem),
        scratch_shapes=scratch,
        compiler_params=pltpu.CompilerParams(
            collective_id=0, has_side_effects=True, vmem_limit_bytes=60 * 1024 * 1024
        ),
        cost_estimate=pl.CostEstimate(
            flops=30_000_000_000, bytes_accessed=20_000_000, transcendentals=4_000_000
        ),
    )(
        obs_values.reshape(64, 2, CAP, VALS),
        obs_cells.reshape(32, 128),
        obs_subcell.reshape(32, 128),
        slot_counts,
        sharpness.reshape(1, CH),
        embed_weight,
        conv_weight.reshape(2, 3, 3 * CH, CH),
        cotangent,
    )
    encoded, value_grads, conv_grads, embed_grads = pl.pallas_call(
        hand_over,
        out_shape=(
            jax.ShapeDtypeStruct(grid, BF16),
            jax.ShapeDtypeStruct((64, 2, CAP, VALS), BF16),
            jax.ShapeDtypeStruct((3 * PART, CH), F32),
            jax.ShapeDtypeStruct((VALS, CH), F32),
        ),
        in_specs=[anywhere] * 4,
        out_specs=(anywhere,) * 4,
        scratch_shapes=[
            pltpu.VMEM(grid, BF16),
            pltpu.VMEM((64, 2, CAP, VALS), BF16),
            pltpu.VMEM((VALS, CH), F32),
            pltpu.VMEM((2, 3 * PART, 128), BF16),
            pltpu.VMEM((3 * PART, CH), F32),
            dma((23,)),
            dma((23,)),
        ],
        compiler_params=pltpu.CompilerParams(vmem_limit_bytes=60 * 1024 * 1024),
    )(encoded, value_grads, grads, embed_total)
    return (
        encoded,
        value_grads.reshape(OBS, VALS),
        conv_grads.reshape(2, 3, 3, CH, CH),
        embed_grads,
    )


def solution(mesh):
    placed = (
        P(("lat", "lon"), None),
        P(("lat", "lon")),
        P(("lat", "lon")),
        P(("lat", "lon"), None),
        P(),
        P(),
        P(),
        P("lat", "lon", None),
    )
    return jax.shard_map(
        on_device,
        mesh=mesh,
        in_specs=placed,
        out_specs=(P("lat", "lon", None), P(("lat", "lon"), None), P(), P()),
        check_vma=False,
    )
```

```python
import jax
import jax.numpy as jnp
from jax import lax
from jax.experimental import pallas as pl
from jax.experimental.pallas import tpu as pltpu
from jax.sharding import PartitionSpec as P

F32 = jnp.float32
BF16 = jnp.bfloat16
N_LAT, N_LON = 4, 32
DEVICES = N_LAT * N_LON
CAP, VALS, CH = 32, 128, 256
ROWS, COLS = 16, 128
CELLS = ROWS * COLS
OBS = DEVICES * CAP
GROUP = 32 * CAP
PART, HALF, QUARTER, SHARD = 1536, 768, 192, 48
NT = (((1,), (1,)), ((), ()))
TN = (((0,), (0,)), ((), ()))


def dot(a, b):
    return jnp.dot(a, b, preferred_element_type=F32)


def iota(shape, axis):
    return lax.broadcasted_iota(jnp.int32, shape, axis)


def sigmoid(x):
    return 0.5 + 0.5 * jnp.tanh(0.5 * x)


def remote(src, dst, send, recv, lat, lon):
    return pltpu.make_async_remote_copy(
        src_ref=src,
        dst_ref=dst,
        send_sem=send,
        recv_sem=recv,
        device_id=(lat, lon),
        device_id_type=pl.DeviceIdType.MESH,
    )


def await_bytes(ref, sem):
    pltpu.make_async_copy(ref, ref, sem).wait()


def loop(low, high, body):
    def step(i, carry):
        body(i)
        return carry

    lax.fori_loop(low, high, step, 0)


def aligned(start, size, unit):
    return pl.ds(pl.multiple_of(start, unit), size)


def kernel(
    obs_in, cells, subs, live_counts, sharp, embed_w, conv_in, cot_in,
    enc_out, vg_out, grads_out, embed_out,
    vals, queue, relay, meta_own, meta_z, meta_x, meta, tmeta, colb, rowb, weight, ew, rk, colhot, rowl, placed, counts, inv,
    cot, conv_w, embed_t, back, bend, base, act_zero, mid, act_one, gmid, gp, act_t, zero_t,
    x3_act, x3_cot, x3_mid, hrow, hcol, strip, stripf,
    vg, grads, total, p0, s1, p1, s2, p2, s3, p3, esum, pe, qe, etotal, enc,
    local_sem, pair_send, pair_recv, a2a_send, a2a_recv, meta_send, meta_recv, vg_send, vg_recv,
    halo_send, halo_recv, ar_send, ar_recv, em_send, em_recv,
):
    lat = lax.axis_index("lat")
    lon = lax.axis_index("lon")
    me = lat * N_LON + lon
    xi, yi, ci = lax.div(lon, 8), lax.rem(lax.div(lon, 2), 4), lax.rem(lon, 2)

    chip = lat * 16 + xi * 4 + yi
    yc = lax.rem(lon, 8)
    other_core = lon + 1 - 2 * ci

    def offset(j):
        g, dx, dy = lax.div(j, 16), lax.rem(lax.div(j, 4), 4), lax.rem(j, 4)
        return dx, dy, lax.rem(g + 8 - dx - dy, 4)

    barrier = pltpu.get_barrier_semaphore()

    cot_copy = pltpu.make_async_copy(cot_in, cot, local_sem.at[0])
    cot_copy.start()
    pair_own = pltpu.make_async_copy(obs_in.at[:, ci], queue.at[:, ci], local_sem.at[4])
    pair_own.start()
    pair_other = remote(
        obs_in.at[:, 1 - ci], queue.at[:, ci], pair_send.at[0], pair_recv.at[0], lat, other_core
    )

    def greet(j):
        tlat, tlon = lax.rem(lat + lax.div(j, N_LON), N_LAT), lax.rem(lon + lax.rem(j, N_LON), N_LON)
        pl.semaphore_signal(
            barrier, inc=1, device_id=(tlat, tlon), device_id_type=pl.DeviceIdType.MESH
        )

    loop(1, DEVICES, greet)

    def meta_copies(stage):
        copies = []
        for d in range(1, 8 if stage == 2 else 4):
            if stage == 0:
                c = lax.rem(lat + d, 4)
                src, dst, target = meta_own.at[:, pl.ds(c * 8, 8)], meta_z.at[lat], (c, lon)
            elif stage == 1:
                c = lax.rem(xi + d, 4)
                src, dst = meta_z.at[:, :, pl.ds(c * 2, 2)], meta_x.at[xi]
                target = (lat, c * 8 + yc)
            else:
                c = lax.rem(yc + d, 8)
                src, dst = meta_x.at[:, :, lax.rem(c, 4), lax.div(c, 4)], meta.at[yc]
                target = (lat, xi * 8 + c)
            copies.append(remote(src, dst, meta_send.at[stage], meta_recv.at[stage], *target))
        own = (
            (meta_own.at[:, pl.ds(lat * 8, 8)], meta_z.at[lat]),
            (meta_z.at[:, :, pl.ds(xi * 2, 2)], meta_x.at[xi]),
            (meta_x.at[:, :, lax.rem(yc, 4), lax.div(yc, 4)], meta.at[yc]),
        )[stage]
        copies.append(pltpu.make_async_copy(*own, meta_recv.at[stage]))
        return copies

    def meta_start(stage):
        for copy in meta_copies(stage):
            copy.start()

    def meta_wait(stage):
        await_bytes((meta_z, meta_x, meta)[stage], meta_recv.at[stage])

    def meta_sent(stage):
        await_bytes((meta_z, meta_x, meta)[stage].at[pl.ds(0, (3, 3, 7)[stage])], meta_send.at[stage])

    line, lane = iota((32, 128), 0), iota((32, 128), 1)
    own_four = jnp.where(lax.div(lane, 4) == line, live_counts[...].astype(F32), 0.0).astype(BF16)
    to_slots = jnp.where(
        lax.rem(iota((128, 128), 0), 4) == lax.div(iota((128, 128), 1), 32), 1.0, 0.0
    ).astype(BF16)
    live = lax.rem(lane, 32).astype(F32) < dot(own_four, to_slots)
    cell, sub = cells[...], subs[...]
    u, v = sub >> 3, sub & 7
    u = jnp.where(u >= 4, u - 4, 3 - u)
    v = jnp.where(v >= 4, v - 4, 3 - v)
    row = cell >> 7
    fields = [
        jnp.where(live, (cell & 127).astype(F32), 255.0),
        (row * 16 + u * 4 + v).astype(F32),
        ((2 * u + 1) * (2 * u + 1) + (2 * v + 1) * (2 * v + 1)).astype(F32),
        row.astype(F32),
    ]
    for i in range(4):
        mixed = jnp.zeros((32, 128), F32)
        for f in range(4):
            shift = (f - i) * 32 % 128
            turned_field = pltpu.roll(fields[f], shift, 1) if shift else fields[f]
            mixed = jnp.where(lax.div(lane, 32) == f, turned_field, mixed)
        for r in range(32):
            meta_own[i, r] = mixed[r : r + 1, :]

    conv_copy = pltpu.make_async_copy(conv_in, conv_w, local_sem.at[1])
    conv_copy.start()

    def send_slot(j):
        dx, dy, dz = offset(j)
        tx, ty, tz = lax.rem(xi + dx, 4), lax.rem(yi + dy, 4), lax.rem(lat + dz, 4)
        g = lax.div(j, 16)
        remote(
            queue.at[tz * 16 + tx * 4 + ty], vals.at[j], a2a_send.at[g], a2a_recv.at[g],
            tz, tx * 8 + ty * 2 + ci,
        ).start()

    north, south = lax.rem(lat + 3, N_LAT), lax.rem(lat + 1, N_LAT)
    west, east = lax.rem(lon + N_LON - 1, N_LON), lax.rem(lon + 1, N_LON)

    def halo_copies(src, k):
        pieces = [
            (src.at[ROWS - 1], hrow.at[k, 0], south, lon),
            (src.at[0], hrow.at[k, 1], north, lon),
        ]
        for side, column, target in ((0, 1, east), (1, 0, west)):
            for turn, tlat in enumerate((lat, south, north)):
                pieces.append((strip.at[k, column], hcol.at[k, side, turn], tlat, target))
        return [
            remote(s, d, halo_send.at[k, i], halo_recv.at[k, i], a, b)
            for i, (s, d, a, b) in enumerate(pieces)
        ]

    def halo_pack(src, k):
        for r in range(ROWS):
            stripf[0, r : r + 1, :] = src[r, 0:16, :].astype(F32)[0:1, :]
            stripf[1, r : r + 1, :] = src[r, COLS - 16 : COLS, :].astype(F32)[15:16, :]
        strip[k, 0] = stripf[0].astype(BF16)
        strip[k, 1] = stripf[1].astype(BF16)

    def halo_start(src, k):
        for copy in halo_copies(src, k):
            copy.start()

    def widen(src, x3, low=0, high=4):
        def body(b):
            for i in range(4):
                r = 4 * b + i
                row = src[r].astype(F32)
                x3[r + 1, :, 0:CH] = pltpu.roll(row, 1, 0).astype(BF16)
                x3[r + 1, :, CH : 2 * CH] = src[r]
                x3[r + 1, :, 2 * CH : 3 * CH] = pltpu.roll(row, COLS - 1, 0).astype(BF16)

        loop(low, high, body)

    def halo_finish(src, k, x3):
        for copy in halo_copies(src, k):
            copy.wait()
        first = iota((16, CH), 0) == 0
        last = iota((16, CH), 0) == 15
        left = hcol[k, 0, 0].astype(F32)
        right = hcol[k, 1, 0].astype(F32)
        for r in range(ROWS):
            low = x3[r + 1, 0:16, 0:CH].astype(F32)
            x3[r + 1, 0:16, 0:CH] = jnp.where(first, left[r : r + 1, :], low).astype(BF16)
            high = x3[r + 1, COLS - 16 : COLS, 2 * CH : 3 * CH].astype(F32)
            x3[r + 1, COLS - 16 : COLS, 2 * CH : 3 * CH] = jnp.where(
                last, right[r : r + 1, :], high
            ).astype(BF16)
        spot = iota((COLS, CH), 0)
        for side, r, turn, pick, valid in (
            (0, 0, 1, ROWS - 1, lat > 0),
            (1, ROWS + 1, 2, 0, lat < N_LAT - 1),
        ):
            keep = jnp.where(valid, 1.0, 0.0).astype(F32)
            row = hrow[k, side].astype(F32) * keep
            lcorner = hcol[k, 0, turn].astype(F32)[pick : pick + 1, :] * keep
            rcorner = hcol[k, 1, turn].astype(F32)[pick : pick + 1, :] * keep
            x3[r, :, 0:CH] = jnp.where(spot == 0, lcorner, pltpu.roll(row, 1, 0)).astype(BF16)
            x3[r, :, CH : 2 * CH] = row.astype(BF16)
            x3[r, :, 2 * CH : 3 * CH] = jnp.where(
                spot == COLS - 1, rcorner, pltpu.roll(row, COLS - 1, 0)
            ).astype(BF16)

    def conv(x3, k, finish, flip=False, low=0, high=4):
        def body(pair):
            for b in (2 * pair, 2 * pair + 1):
                near = [x3[pl.ds(4 * b + p, 4)].reshape(4 * COLS, 3 * CH) for p in range(3)]
                near = jnp.concatenate(near, axis=1)
                if flip:
                    taps = [
                        conv_w[k, 2 - p, (2 - q) * CH : (3 - q) * CH, :]
                        for p in range(3)
                        for q in range(3)
                    ]
                    taps = jnp.concatenate(taps, axis=1)
                    acc = lax.dot_general(near, taps, NT, preferred_element_type=F32)
                else:
                    acc = dot(near, conv_w[k].reshape(9 * CH, CH))
                finish(pl.ds(4 * b, 4), acc)

        loop(low // 2, high // 2, body)

    def tile4(x):
        return x.reshape(4 * COLS, CH)

    def grid4(x):
        return x.reshape(4, COLS, CH)

    def turn_act(act, act_t):
        for r in range(ROWS):
            act_t[:, r * COLS : (r + 1) * COLS] = act[r].T

    cot_copy.wait()
    halo_pack(cot, 0)
    pl.semaphore_wait(barrier, DEVICES - 1)
    pair_other.start()
    meta_start(0)
    halo_start(cot, 0)
    widen(cot, x3_cot, 0, 2)
    meta_wait(0)
    meta_start(1)
    widen(cot, x3_cot, 2, 4)
    meta_wait(1)
    meta_start(2)
    pair_own.wait()
    pair_other.wait()
    pltpu.make_async_copy(queue.at[chip], vals.at[0], a2a_recv.at[0]).start()
    loop(1, 64, send_slot)
    conv_copy.wait()
    embed_t[...] = embed_w[...].T
    halo_finish(cot, 0, x3_cot)

    def keep_back(rows, acc):
        back[rows] = grid4(acc)

    conv(x3_cot, 1, keep_back, flip=True)
    meta_wait(2)

    placed[...] = jnp.zeros_like(placed)
    counts[...] = jnp.zeros_like(counts)
    slot_mask = jnp.where(
        lax.rem(iota((CAP, 128), 1), 32) == iota((CAP, 128), 0), 1.0, 0.0
    ).astype(F32)
    spread = jnp.where(
        lax.div(iota((128, 512), 0), 32) == lax.div(iota((128, 512), 1), 128), 1.0, 0.0
    ).astype(BF16)
    lane, line = iota((COLS + 16, 128), 1), iota((COLS + 16, 128), 0)
    pick = jnp.where(lax.div(lane, 32) == jnp.where(line < COLS, 0, 3), 1.0, 0.0).astype(BF16)
    decay = sharp[...] * (-1.0 / 256.0)

    def place_group(g):
        def stretch(b):
            for i in range(8):
                s = 8 * b + i
                dx, dy, dz = offset(g * 16 + 4 * b + i // 2)
                sx, sy = lax.rem(xi + 4 - dx, 4), lax.rem(yi + 4 - dy, 4)
                source = meta[sy * 2 + i % 2, sx, lax.rem(lat + 4 - dz, 4)]
                line = jnp.broadcast_to(source, (CAP, 128)) * slot_mask
                tmeta[aligned(s * CAP, CAP, CAP), :] = line.astype(BF16)

        loop(0, 4, stretch)
        await_bytes(vals.at[pl.ds(g * 16, 16)], a2a_recv.at[g])

        for b in range(4):
            at = slice(b * 256, b * 256 + 256)
            of = aligned(g * GROUP + b * 256, 256, 256)
            wide = dot(tmeta[at, :], spread)
            colb[of, :] = wide[:, 0:128].astype(BF16)
            rowb[of, :] = wide[:, 384:512].astype(BF16)
            rk_of = jnp.concatenate([wide[:, 128:256]] * 2, axis=1)
            radius = jnp.concatenate([wide[:, 256:384]] * 2, axis=1)
            rk[at, :] = jnp.where(
                rk_of == iota((256, 256), 1).astype(F32), 1.0, 0.0
            ).astype(BF16)
            w = jnp.exp(radius * decay)
            weight[of, :] = w
            ew[at, :] = (dot(vals[pl.ds(g * 16 + 4 * b, 4)].reshape(256, VALS), embed_w[...]) * w).astype(BF16)

        both = lax.dot_general(pick, tmeta[...], NT, preferred_element_type=F32)
        colhot[...] = jnp.where(
            both[0:COLS] == iota((COLS, GROUP), 0).astype(F32), 1.0, 0.0
        ).astype(BF16)
        rowl[...] = both[COLS : COLS + 16]
        counts[...] += dot(colhot[...], rk[...])

        hot = colhot[...].reshape(8, 16, GROUP)
        for b in range(4):
            rows = []
            for r in range(4 * b, 4 * b + 4):
                mask = jnp.where(rowl[...] == float(r), 1.0, 0.0).astype(BF16)
                rows.append((hot * mask[None]).reshape(COLS, GROUP))
            at = slice(b * 512, b * 512 + 512)
            placed[at, :] += dot(jnp.concatenate(rows, axis=0), ew[...])

    loop(0, 4, place_group)

    kind = lax.rem(iota((256, CH), 0), 16)
    half_u, half_v = 2 * lax.div(kind, 4) + 1, 2 * lax.rem(kind, 4) + 1
    table = jnp.exp((half_u * half_u + half_v * half_v).astype(F32) * decay)
    table_hi = table.astype(BF16)
    table_lo = (table - table_hi.astype(F32)).astype(BF16)
    tables = jnp.concatenate([table_hi, table_lo], axis=0)
    row_of_lane = lax.div(iota((COLS, 256), 1), 16)
    for b in range(4):
        rows = []
        for r in range(4 * b, 4 * b + 4):
            rows.append(jnp.where(row_of_lane == r, counts[...], 0.0).astype(BF16))
        tally = jnp.concatenate(rows, axis=0)
        recip = 1.0 / (dot(jnp.concatenate([tally, tally], axis=1), tables) + 1.0)
        at = slice(4 * b, 4 * b + 4)
        inv[at] = grid4(recip)
        value = (placed[b * 512 : b * 512 + 512, :] * recip).astype(BF16)
        base[at] = grid4(value)
        x = value.astype(F32)
        s = sigmoid(x)
        act_zero[at] = grid4((x * s).astype(BF16))
        bend[at] = grid4(s * (1.0 + x * (1.0 - s)))

    halo_pack(act_zero, 1)
    halo_start(act_zero, 1)
    widen(act_zero, x3_act)
    turn_act(act_zero, zero_t)
    halo_finish(act_zero, 1, x3_act)

    def keep_mid(rows, acc):
        value = (tile4(base[rows]).astype(F32) + acc).astype(BF16)
        mid[rows] = grid4(value)
        x = value.astype(F32)
        s = sigmoid(x)
        act_one[rows] = grid4((x * s).astype(BF16))
        slope = s * (1.0 + x * (1.0 - s))
        grad = tile4(cot[rows]).astype(F32) + tile4(back[rows]) * slope
        gmid[rows] = grid4(grad.astype(BF16))

    conv(x3_act, 0, keep_mid)
    halo_pack(gmid, 2)
    halo_start(gmid, 2)
    halo_pack(act_one, 3)
    halo_start(act_one, 3)

    def kernel_grad(act_t, x3, k):
        for p in range(3):
            block = dot(act_t[...], x3[2 - p : 2 - p + ROWS].reshape(CELLS, 3 * CH))
            for q in range(3):
                for h in range(2):
                    at, lanes = (6 * p + 2 * q + h) * CH, (2 - q) * CH + h * 128
                    grads[k, at : at + CH, :] = block[:, lanes : lanes + 128].astype(BF16)

    coords = {"x": xi, "y": yi, "z": lat}
    orders = (("x", "y", "z"), ("y", "z", "x"), ("z", "x", "y"))

    def along(axis, c):
        cx, cy, cz = [c if axis == n else coords[n] for n in ("x", "y", "z")]
        return cz, cx * 8 + cy * 2 + ci

    def turned(axis, d):
        return lax.rem(coords[axis] + d, 4)

    def part_copies(k, stage):
        copies = []
        for a, order in enumerate(orders):
            own = a * PART + ci * HALF
            sems = lambda d: (ar_send.at[k, stage, a, d], ar_recv.at[k, stage, a, d])
            quarter = own + coords[order[0]] * QUARTER
            shard = quarter + coords[order[1]] * SHARD
            if stage == 0:
                src = grads.at[k, aligned(a * PART + (1 - ci) * HALF, HALF, 16)]
                copies.append(remote(src, p0.at[k, a], *sems(0), lat, other_core))
            elif stage == 6:
                piece = total.at[k, aligned(own, HALF, 16)]
                copies.append(remote(piece, piece, *sems(0), lat, other_core))
            else:
                axis = order[{1: 0, 2: 1, 3: 2, 4: 1, 5: 0}[stage]]
                for d in (1, 3, 2):
                    c = turned(axis, d)
                    if stage == 1:
                        src = s1.at[k, a, aligned(c * QUARTER, QUARTER, 16)]
                        dst = p1.at[k, a, d - 1]
                    elif stage == 2:
                        src = s2.at[k, a, aligned(c * SHARD, SHARD, 16)]
                        dst = p2.at[k, a, d - 1]
                    elif stage == 3:
                        src, dst = s3.at[k, a], p3.at[k, a, coords[axis]]
                    elif stage == 4:
                        src = dst = total.at[k, aligned(shard, SHARD, 16)]
                    else:
                        src = dst = total.at[k, aligned(quarter, QUARTER, 16)]
                    copies.append(remote(src, dst, *sems(d - 1), *along(axis, c)))
        return copies

    def ar_start(k, stage):
        for copy in part_copies(k, stage):
            copy.start()

    def ar_finish(k, stage):
        for copy in part_copies(k, stage):
            copy.wait()
        for a, order in enumerate(orders):
            own = a * PART + ci * HALF
            if stage == 0:
                here = grads[k, aligned(own, HALF, 16), :].astype(F32)
                s1[k, a] = (here + p0[k, a].astype(F32)).astype(BF16)
            elif stage in (1, 2):
                size = QUARTER if stage == 1 else SHARD
                src, came, dst = (s1, p1, s2) if stage == 1 else (s2, p2, s3)
                at = aligned(coords[order[stage - 1]] * size, size, 16)
                here = src[k, a, at, :].astype(F32)
                for d in range(3):
                    here += came[k, a, d].astype(F32)
                dst[k, a] = here.astype(BF16)
            elif stage == 3:
                p3[k, a, coords[order[2]]] = s3[k, a]
                whole = p3[k, a, 0].astype(F32)
                for d in range(1, 4):
                    whole += p3[k, a, d].astype(F32)
                quarter = own + coords[order[0]] * QUARTER
                at = aligned(quarter + coords[order[1]] * SHARD, SHARD, 16)
                total[k, at, :] = whole.astype(BF16)

    def ar_step(k, stage):
        ar_finish(k, stage)
        ar_start(k, stage + 1)

    def ar_leave(k):
        return pltpu.make_async_copy(total.at[k], grads_out.at[k], local_sem.at[3 if k else 6])

    turn_act(act_one, act_t)
    kernel_grad(act_t, x3_cot, 1)
    ar_start(1, 0)
    widen(gmid, x3_mid)
    halo_finish(gmid, 2, x3_mid)
    ar_step(1, 0)
    kernel_grad(zero_t, x3_mid, 0)
    ar_start(0, 0)

    def keep_gp(rows, acc):
        grad = tile4(gmid[rows]).astype(F32) + acc * tile4(bend[rows])
        gp[aligned(rows.start * COLS, 4 * COLS, 4 * COLS), :] = (
            grad * tile4(inv[rows])
        ).astype(BF16)

    conv(x3_mid, 0, keep_gp, flip=True, low=0, high=2)
    ar_step(1, 1)
    ar_step(0, 0)
    conv(x3_mid, 0, keep_gp, flip=True, low=2, high=4)

    esum[...] = jnp.zeros_like(esum)

    def vg_copy(j):
        dx, dy, dz = offset(j)
        sx, sy, sz = lax.rem(xi + 4 - dx, 4), lax.rem(yi + 4 - dy, 4), lax.rem(lat + 4 - dz, 4)
        return remote(vg.at[j], relay.at[chip], vg_send, vg_recv, sz, sx * 8 + sy * 2 + ci)

    def gather(b):
        at = slice(b * 512, b * 512 + 512)
        chips = slice(b * 8, b * 8 + 8)
        hot = jnp.where(
            colb[at, :].astype(F32) == iota((512, COLS), 1).astype(F32), 1.0, 0.0
        ).astype(BF16)
        row_of = rowb[at, :]
        pieces = [
            jnp.where(row_of == jnp.array(r, BF16), hot, jnp.zeros_like(hot)) for r in range(ROWS)
        ]
        found = dot(jnp.concatenate(pieces, axis=1), gp[...])
        grad = (found * weight[at, :]).astype(BF16)
        vg[chips] = dot(grad, embed_t[...]).astype(BF16).reshape(8, 2, CAP, VALS)
        own = vals[chips].reshape(512, VALS)
        esum[...] += lax.dot_general(own, grad, TN, preferred_element_type=F32)
        for j in range(8 * b, 8 * b + 8):
            if j == 0:
                pltpu.make_async_copy(vg.at[0], relay.at[chip], vg_recv).start()
            else:
                vg_copy(j).start()

    gather(0)
    gather(1)
    ar_step(1, 2)
    gather(2)
    ar_step(0, 1)
    gather(3)
    ar_step(1, 3)
    gather(4)
    ar_step(0, 2)
    gather(5)
    ar_step(1, 4)
    gather(6)
    ar_step(0, 3)
    gather(7)
    ar_step(0, 4)

    member = yc
    column = xi * 4 + lat

    def embed_copies(stage):
        copies = []
        for d in range(1, 16 if stage == 1 else 8):
            if stage == 1:
                c = lax.rem(column + d, 16)
                tlat, tlon = lax.rem(c, 4), lax.div(c, 4) * 8 + member
                src, dst = esum.at[aligned(member * 16, 16, 16)], qe.at[column]
            else:
                m = lax.rem(member + d, 8)
                tlat, tlon = lat, xi * 8 + m
                if stage == 0:
                    src, dst = esum.at[aligned(m * 16, 16, 16)], pe.at[d - 1]
                else:
                    src = dst = etotal.at[aligned(member * 16, 16, 16)]
            copies.append(remote(src, dst, em_send.at[stage, d - 1], em_recv.at[stage, d - 1], tlat, tlon))
        return copies

    def embed_start(stage):
        for copy in embed_copies(stage):
            copy.start()

    def embed_wait(stage):
        for copy in embed_copies(stage):
            copy.wait()

    embed_start(0)
    widen(act_one, x3_act)
    halo_finish(act_one, 3, x3_act)
    ar_step(1, 5)

    def keep_enc(rows, acc):
        enc[rows] = grid4((tile4(mid[rows]).astype(F32) + acc).astype(BF16))

    conv(x3_act, 1, keep_enc, low=0, high=2)
    embed_wait(0)
    own_rows = aligned(member * 16, 16, 16)
    mine = esum[own_rows, :]
    for d in range(7):
        mine += pe[d]
    esum[own_rows, :] = mine
    embed_start(1)
    ar_step(0, 5)
    ar_finish(1, 6)
    ar_leave(1).start()
    conv(x3_act, 1, keep_enc, low=2, high=4)
    enc_copy = pltpu.make_async_copy(enc, enc_out, local_sem.at[2])
    enc_copy.start()
    embed_wait(1)
    qe[column] = esum[own_rows, :]
    whole = qe[0]
    for d in range(1, 16):
        whole += qe[d]
    etotal[own_rows, :] = whole
    embed_start(2)
    await_bytes(relay, vg_recv)
    vg_own = pltpu.make_async_copy(relay.at[:, ci], vg_out.at[:, ci], local_sem.at[5])
    vg_own.start()
    vg_other = remote(
        relay.at[:, 1 - ci], vg_out.at[:, ci], pair_send.at[1], pair_recv.at[1], lat, other_core
    )
    vg_other.start()
    ar_finish(0, 6)
    ar_leave(0).start()
    embed_wait(2)
    embed_out[...] = etotal[...] * (1.0 / 512.0)
    for g in range(4):
        await_bytes(vals.at[pl.ds(0, 15 if g == 0 else 16)], a2a_send.at[g])
    for stage in range(3):
        meta_sent(stage)
    await_bytes(vg.at[pl.ds(0, 63)], vg_send)
    vg_own.wait()
    vg_other.wait()
    enc_copy.wait()
    ar_leave(1).wait()
    ar_leave(0).wait()


def hand_over(
    enc_in, vg_in, grads_in, embed_in, enc_out, vg_out, grads_out, embed_out,
    enc, vg, embed, narrow, wide, in_sem, out_sem,
):
    steps = []
    for i in range(18):
        src, dst = slice(i % 9 * 2 * CH, (i % 9 + 1) * 2 * CH), slice(i * CH, i * CH + CH)
        k = i // 9
        steps.append(
            (grads_in.at[k, src], narrow.at[k, src], wide.at[dst], grads_out.at[dst], (k, src, dst))
        )
    for i in range(2):
        at = slice(i * 8, i * 8 + 8)
        steps.append((enc_in.at[at], enc.at[at], enc.at[at], enc_out.at[at], None))
        at = slice(i * 32, i * 32 + 32)
        steps.append((vg_in.at[at], vg.at[at], vg.at[at], vg_out.at[at], None))
    steps.append((embed_in, embed, embed, embed_out, None))
    moves = [
        pltpu.make_async_copy(step[0], step[1], in_sem.at[i]) for i, step in enumerate(steps)
    ]
    for move in moves:
        move.start()
    results = []
    for i, (_, _, src, dst, at) in enumerate(steps):
        moves[i].wait()
        if at is not None:
            k, rows, to = at
            for h in range(2):
                half = slice(rows.start + h * CH, rows.start + h * CH + CH)
                wide[to, h * 128 : h * 128 + 128] = narrow[k, half, :].astype(F32) * (1.0 / 512.0)
        results.append(pltpu.make_async_copy(src, dst, out_sem.at[i]))
        results[i].start()
    for copy in results:
        copy.wait()


def on_device(
    obs_values, obs_cells, obs_subcell, slot_counts, sharpness, embed_weight, conv_weight, cotangent
):
    anywhere = pl.BlockSpec(memory_space=pl.ANY)
    vmem = pl.BlockSpec(memory_space=pltpu.VMEM)
    grid = (ROWS, COLS, CH)
    wide = (ROWS + 2, COLS, 3 * CH)
    dma = pltpu.SemaphoreType.DMA
    scratch = [
        pltpu.VMEM((64, 2, CAP, VALS), BF16),
        pltpu.VMEM((64, 2, CAP, VALS), BF16),
        pltpu.VMEM((64, 2, CAP, VALS), BF16),
        pltpu.VMEM((4, 32, 1, 128), F32),
        pltpu.VMEM((4, 4, 8, 1, 128), F32),
        pltpu.VMEM((4, 4, 4, 2, 1, 128), F32),
        pltpu.VMEM((8, 4, 4, 1, 128), F32),
        pltpu.VMEM((GROUP, 128), BF16),
        pltpu.VMEM((OBS, 128), BF16),
        pltpu.VMEM((OBS, 128), BF16),
        pltpu.VMEM((OBS, CH), F32),
        pltpu.VMEM((GROUP, CH), BF16),
        pltpu.VMEM((GROUP, 256), BF16),
        pltpu.VMEM((COLS, GROUP), BF16),
        pltpu.VMEM((16, GROUP), F32),
        pltpu.VMEM((CELLS, CH), F32),
        pltpu.VMEM((COLS, 256), F32),
        pltpu.VMEM(grid, F32),
        pltpu.VMEM(grid, BF16),
        pltpu.VMEM((2, 3, 3 * CH, CH), BF16),
        pltpu.VMEM((CH, VALS), BF16),
        pltpu.VMEM(grid, F32),
        pltpu.VMEM(grid, F32),
        pltpu.VMEM(grid, BF16),
        pltpu.VMEM(grid, BF16),
        pltpu.VMEM(grid, BF16),
        pltpu.VMEM(grid, BF16),
        pltpu.VMEM(grid, BF16),
        pltpu.VMEM((CELLS, CH), BF16),
        pltpu.VMEM((CH, CELLS), BF16),
        pltpu.VMEM((CH, CELLS), BF16),
        pltpu.VMEM(wide, BF16),
        pltpu.VMEM(wide, BF16),
        pltpu.VMEM(wide, BF16),
        pltpu.VMEM((4, 2, COLS, CH), BF16),
        pltpu.VMEM((4, 2, 3, 16, CH), BF16),
        pltpu.VMEM((4, 2, 16, CH), BF16),
        pltpu.VMEM((2, 16, CH), F32),
        pltpu.VMEM((64, 2, CAP, VALS), BF16),
        pltpu.VMEM((2, 3 * PART, 128), BF16),
        pltpu.VMEM((2, 3 * PART, 128), BF16),
        pltpu.VMEM((2, 3, HALF, 128), BF16),
        pltpu.VMEM((2, 3, HALF, 128), BF16),
        pltpu.VMEM((2, 3, 3, QUARTER, 128), BF16),
        pltpu.VMEM((2, 3, QUARTER, 128), BF16),
        pltpu.VMEM((2, 3, 3, SHARD, 128), BF16),
        pltpu.VMEM((2, 3, SHARD, 128), BF16),
        pltpu.VMEM((2, 3, 4, SHARD, 128), BF16),
        pltpu.VMEM((VALS, CH), F32),
        pltpu.VMEM((7, 16, CH), F32),
        pltpu.VMEM((16, 16, CH), F32),
        pltpu.VMEM((VALS, CH), F32),
        pltpu.VMEM(grid, BF16),
        dma((7,)),
        dma((2,)),
        dma((2,)),
        dma((4,)),
        dma((4,)),
        dma((3,)),
        dma((3,)),
        dma,
        dma,
        dma((4, 8)),
        dma((4, 8)),
        dma((2, 7, 3, 3)),
        dma((2, 7, 3, 3)),
        dma((3, 15)),
        dma((3, 15)),
    ]
    encoded, value_grads, grads, embed_total = pl.pallas_call(
        kernel,
        out_shape=(
            jax.ShapeDtypeStruct(grid, BF16),
            jax.ShapeDtypeStruct((64, 2, CAP, VALS), BF16),
            jax.ShapeDtypeStruct((2, 3 * PART, 128), BF16),
            jax.ShapeDtypeStruct((VALS, CH), F32),
        ),
        in_specs=[anywhere, vmem, vmem, vmem, vmem, vmem, anywhere, anywhere],
        out_specs=(anywhere, anywhere, anywhere, vmem),
        scratch_shapes=scratch,
        compiler_params=pltpu.CompilerParams(
            collective_id=0, has_side_effects=True, vmem_limit_bytes=60 * 1024 * 1024
        ),
        cost_estimate=pl.CostEstimate(
            flops=30_000_000_000, bytes_accessed=20_000_000, transcendentals=4_000_000
        ),
    )(
        obs_values.reshape(64, 2, CAP, VALS),
        obs_cells.reshape(32, 128),
        obs_subcell.reshape(32, 128),
        slot_counts,
        sharpness.reshape(1, CH),
        embed_weight,
        conv_weight.reshape(2, 3, 3 * CH, CH),
        cotangent,
    )
    encoded, value_grads, conv_grads, embed_grads = pl.pallas_call(
        hand_over,
        out_shape=(
            jax.ShapeDtypeStruct(grid, BF16),
            jax.ShapeDtypeStruct((64, 2, CAP, VALS), BF16),
            jax.ShapeDtypeStruct((3 * PART, CH), F32),
            jax.ShapeDtypeStruct((VALS, CH), F32),
        ),
        in_specs=[anywhere] * 4,
        out_specs=(anywhere,) * 4,
        scratch_shapes=[
            pltpu.VMEM(grid, BF16),
            pltpu.VMEM((64, 2, CAP, VALS), BF16),
            pltpu.VMEM((VALS, CH), F32),
            pltpu.VMEM((2, 3 * PART, 128), BF16),
            pltpu.VMEM((3 * PART, CH), F32),
            dma((23,)),
            dma((23,)),
        ],
        compiler_params=pltpu.CompilerParams(vmem_limit_bytes=60 * 1024 * 1024),
    )(encoded, value_grads, grads, embed_total)
    return (
        encoded,
        value_grads.reshape(OBS, VALS),
        conv_grads.reshape(2, 3, 3, CH, CH),
        embed_grads,
    )


def solution(mesh):
    placed = (
        P(("lat", "lon"), None),
        P(("lat", "lon")),
        P(("lat", "lon")),
        P(("lat", "lon"), None),
        P(),
        P(),
        P(),
        P("lat", "lon", None),
    )
    return jax.shard_map(
        on_device,
        mesh=mesh,
        in_specs=placed,
        out_specs=(P("lat", "lon", None), P(("lat", "lon"), None), P(), P()),
        check_vma=False,
    )
```

```python
import jax
import jax.numpy as jnp
from jax import lax
from jax.experimental import pallas as pl
from jax.experimental.pallas import tpu as pltpu
from jax.sharding import PartitionSpec as P

F32 = jnp.float32
BF16 = jnp.bfloat16
N_LAT, N_LON = 4, 32
DEVICES = N_LAT * N_LON
CAP, VALS, CH = 32, 128, 256
ROWS, COLS = 16, 128
CELLS = ROWS * COLS
OBS = DEVICES * CAP
GROUP = 32 * CAP
PART, HALF, QUARTER, SHARD = 1536, 768, 192, 48
NT = (((1,), (1,)), ((), ()))
TN = (((0,), (0,)), ((), ()))


def dot(a, b):
    return jnp.dot(a, b, preferred_element_type=F32)


def iota(shape, axis):
    return lax.broadcasted_iota(jnp.int32, shape, axis)


def sigmoid(x):
    return 0.5 + 0.5 * jnp.tanh(0.5 * x)


def remote(src, dst, send, recv, lat, lon):
    return pltpu.make_async_remote_copy(
        src_ref=src,
        dst_ref=dst,
        send_sem=send,
        recv_sem=recv,
        device_id=(lat, lon),
        device_id_type=pl.DeviceIdType.MESH,
    )


def await_bytes(ref, sem):
    pltpu.make_async_copy(ref, ref, sem).wait()


def loop(low, high, body):
    def step(i, carry):
        body(i)
        return carry

    lax.fori_loop(low, high, step, 0)


def aligned(start, size, unit):
    return pl.ds(pl.multiple_of(start, unit), size)


def kernel(
    obs_in, cells, subs, live_counts, sharp, embed_w, conv_in, cot_in,
    enc_out, vg_out, grads_out, embed_out,
    vals, queue, relay, meta_own, meta_z, meta_x, meta, tmeta, colb, rowb, weight, ew, rk, colhot, rowl, placed, counts, inv,
    cot, conv_w, embed_t, back, bend, pending, base, act_zero, mid, act_one, gmid, gp, act_t, zero_t,
    x3_act, x3_cot, x3_mid, hrow, hcol, strip, stripf,
    vg, grads, total, p0, s1, p1, s2, p2, s3, p3, esum, pe, qe, etotal, enc,
    local_sem, pair_send, pair_recv, a2a_send, a2a_recv, meta_send, meta_recv, vg_send, vg_recv,
    halo_send, halo_recv, ar_send, ar_recv, em_send, em_recv,
):
    lat = lax.axis_index("lat")
    lon = lax.axis_index("lon")
    me = lat * N_LON + lon
    xi, yi, ci = lax.div(lon, 8), lax.rem(lax.div(lon, 2), 4), lax.rem(lon, 2)

    chip = lat * 16 + xi * 4 + yi
    yc = lax.rem(lon, 8)
    other_core = lon + 1 - 2 * ci

    def offset(j):
        g, dx, dy = lax.div(j, 16), lax.rem(lax.div(j, 4), 4), lax.rem(j, 4)
        return dx, dy, lax.rem(g + 8 - dx - dy, 4)

    barrier = pltpu.get_barrier_semaphore()

    cot_copy = pltpu.make_async_copy(cot_in, cot, local_sem.at[0])
    cot_copy.start()
    pair_own = pltpu.make_async_copy(obs_in.at[:, ci], queue.at[:, ci], local_sem.at[4])
    pair_own.start()
    pair_other = remote(
        obs_in.at[:, 1 - ci], queue.at[:, ci], pair_send.at[0], pair_recv.at[0], lat, other_core
    )

    def greet(j):
        tlat, tlon = lax.rem(lat + lax.div(j, N_LON), N_LAT), lax.rem(lon + lax.rem(j, N_LON), N_LON)
        pl.semaphore_signal(
            barrier, inc=1, device_id=(tlat, tlon), device_id_type=pl.DeviceIdType.MESH
        )

    loop(1, DEVICES, greet)

    def meta_copies(stage):
        copies = []
        for d in range(1, 8 if stage == 2 else 4):
            if stage == 0:
                c = lax.rem(lat + d, 4)
                src, dst, target = meta_own.at[:, pl.ds(c * 8, 8)], meta_z.at[lat], (c, lon)
            elif stage == 1:
                c = lax.rem(xi + d, 4)
                src, dst = meta_z.at[:, :, pl.ds(c * 2, 2)], meta_x.at[xi]
                target = (lat, c * 8 + yc)
            else:
                c = lax.rem(yc + d, 8)
                src, dst = meta_x.at[:, :, lax.rem(c, 4), lax.div(c, 4)], meta.at[yc]
                target = (lat, xi * 8 + c)
            copies.append(remote(src, dst, meta_send.at[stage], meta_recv.at[stage], *target))
        own = (
            (meta_own.at[:, pl.ds(lat * 8, 8)], meta_z.at[lat]),
            (meta_z.at[:, :, pl.ds(xi * 2, 2)], meta_x.at[xi]),
            (meta_x.at[:, :, lax.rem(yc, 4), lax.div(yc, 4)], meta.at[yc]),
        )[stage]
        copies.append(pltpu.make_async_copy(*own, meta_recv.at[stage]))
        return copies

    def meta_start(stage):
        for copy in meta_copies(stage):
            copy.start()

    def meta_wait(stage):
        await_bytes((meta_z, meta_x, meta)[stage], meta_recv.at[stage])

    def meta_sent(stage):
        await_bytes((meta_z, meta_x, meta)[stage].at[pl.ds(0, (3, 3, 7)[stage])], meta_send.at[stage])

    line, lane = iota((32, 128), 0), iota((32, 128), 1)
    own_four = jnp.where(lax.div(lane, 4) == line, live_counts[...].astype(F32), 0.0).astype(BF16)
    to_slots = jnp.where(
        lax.rem(iota((128, 128), 0), 4) == lax.div(iota((128, 128), 1), 32), 1.0, 0.0
    ).astype(BF16)
    live = lax.rem(lane, 32).astype(F32) < dot(own_four, to_slots)
    cell, sub = cells[...], subs[...]
    u, v = sub >> 3, sub & 7
    u = jnp.where(u >= 4, u - 4, 3 - u)
    v = jnp.where(v >= 4, v - 4, 3 - v)
    row = cell >> 7
    fields = [
        jnp.where(live, (cell & 127).astype(F32), 255.0),
        (row * 16 + u * 4 + v).astype(F32),
        ((2 * u + 1) * (2 * u + 1) + (2 * v + 1) * (2 * v + 1)).astype(F32),
        row.astype(F32),
    ]
    for i in range(4):
        mixed = jnp.zeros((32, 128), F32)
        for f in range(4):
            shift = (f - i) * 32 % 128
            turned_field = pltpu.roll(fields[f], shift, 1) if shift else fields[f]
            mixed = jnp.where(lax.div(lane, 32) == f, turned_field, mixed)
        for r in range(32):
            meta_own[i, r] = mixed[r : r + 1, :]

    conv_copy = pltpu.make_async_copy(conv_in, conv_w, local_sem.at[1])
    conv_copy.start()

    def send_slot(j):
        dx, dy, dz = offset(j)
        tx, ty, tz = lax.rem(xi + dx, 4), lax.rem(yi + dy, 4), lax.rem(lat + dz, 4)
        g = lax.div(j, 16)
        remote(
            queue.at[tz * 16 + tx * 4 + ty], vals.at[j], a2a_send.at[g], a2a_recv.at[g],
            tz, tx * 8 + ty * 2 + ci,
        ).start()

    north, south = lax.rem(lat + 3, N_LAT), lax.rem(lat + 1, N_LAT)
    west, east = lax.rem(lon + N_LON - 1, N_LON), lax.rem(lon + 1, N_LON)

    def halo_copies(src, k):
        pieces = [
            (src.at[ROWS - 1], hrow.at[k, 0], south, lon),
            (src.at[0], hrow.at[k, 1], north, lon),
        ]
        for side, column, target in ((0, 1, east), (1, 0, west)):
            for turn, tlat in enumerate((lat, south, north)):
                pieces.append((strip.at[k, column], hcol.at[k, side, turn], tlat, target))
        return [
            remote(s, d, halo_send.at[k, i], halo_recv.at[k, i], a, b)
            for i, (s, d, a, b) in enumerate(pieces)
        ]

    def halo_pack(src, k):
        for r in range(ROWS):
            stripf[0, r : r + 1, :] = src[r, 0:16, :].astype(F32)[0:1, :]
            stripf[1, r : r + 1, :] = src[r, COLS - 16 : COLS, :].astype(F32)[15:16, :]
        strip[k, 0] = stripf[0].astype(BF16)
        strip[k, 1] = stripf[1].astype(BF16)

    def halo_start(src, k):
        for copy in halo_copies(src, k):
            copy.start()

    def widen(src, x3, low=0, high=4):
        def body(b):
            for i in range(4):
                r = 4 * b + i
                row = src[r].astype(F32)
                x3[r + 1, :, 0:CH] = pltpu.roll(row, 1, 0).astype(BF16)
                x3[r + 1, :, CH : 2 * CH] = src[r]
                x3[r + 1, :, 2 * CH : 3 * CH] = pltpu.roll(row, COLS - 1, 0).astype(BF16)

        loop(low, high, body)

    def halo_finish(src, k, x3):
        for copy in halo_copies(src, k):
            copy.wait()
        first = iota((16, CH), 0) == 0
        last = iota((16, CH), 0) == 15
        left = hcol[k, 0, 0].astype(F32)
        right = hcol[k, 1, 0].astype(F32)
        for r in range(ROWS):
            low = x3[r + 1, 0:16, 0:CH].astype(F32)
            x3[r + 1, 0:16, 0:CH] = jnp.where(first, left[r : r + 1, :], low).astype(BF16)
            high = x3[r + 1, COLS - 16 : COLS, 2 * CH : 3 * CH].astype(F32)
            x3[r + 1, COLS - 16 : COLS, 2 * CH : 3 * CH] = jnp.where(
                last, right[r : r + 1, :], high
            ).astype(BF16)
        spot = iota((COLS, CH), 0)
        for side, r, turn, pick, valid in (
            (0, 0, 1, ROWS - 1, lat > 0),
            (1, ROWS + 1, 2, 0, lat < N_LAT - 1),
        ):
            keep = jnp.where(valid, 1.0, 0.0).astype(F32)
            row = hrow[k, side].astype(F32) * keep
            lcorner = hcol[k, 0, turn].astype(F32)[pick : pick + 1, :] * keep
            rcorner = hcol[k, 1, turn].astype(F32)[pick : pick + 1, :] * keep
            x3[r, :, 0:CH] = jnp.where(spot == 0, lcorner, pltpu.roll(row, 1, 0)).astype(BF16)
            x3[r, :, CH : 2 * CH] = row.astype(BF16)
            x3[r, :, 2 * CH : 3 * CH] = jnp.where(
                spot == COLS - 1, rcorner, pltpu.roll(row, COLS - 1, 0)
            ).astype(BF16)

    def conv(x3, k, finish, flip=False, low=0, high=3):
        for b in range(low, high):
            near = x3[6 * b : 6 * b + 6].reshape(6 * COLS, 3 * CH)
            if flip:
                taps = [
                    jnp.concatenate(
                        [conv_w[k, 2 - p, (2 - q) * CH : (3 - q) * CH, :] for q in range(3)], axis=1
                    )
                    for p in range(3)
                ]
                taps = jnp.concatenate(taps, axis=0)
                acc = lax.dot_general(near, taps, NT, preferred_element_type=F32)
            else:
                taps = jnp.concatenate([conv_w[k, p] for p in range(3)], axis=1)
                acc = dot(near, taps)
            for j in range(6):
                r = 6 * b + j
                part = acc[j * COLS : (j + 1) * COLS]
                if r >= 2:
                    finish(r - 2, pending[r - 2] + part[:, 2 * CH : 3 * CH])
                if 1 <= r <= ROWS:
                    pending[r - 1] += part[:, CH : 2 * CH]
                if r < ROWS:
                    pending[r] = part[:, 0:CH]

    def grid4(x):
        return x.reshape(4, COLS, CH)

    def turn_act(act, act_t):
        for r in range(ROWS):
            act_t[:, r * COLS : (r + 1) * COLS] = act[r].T

    cot_copy.wait()
    halo_pack(cot, 0)
    pl.semaphore_wait(barrier, DEVICES - 1)
    pair_other.start()
    meta_start(0)
    halo_start(cot, 0)
    widen(cot, x3_cot, 0, 2)
    meta_wait(0)
    meta_start(1)
    widen(cot, x3_cot, 2, 4)
    meta_wait(1)
    meta_start(2)
    pair_own.wait()
    pair_other.wait()
    pltpu.make_async_copy(queue.at[chip], vals.at[0], a2a_recv.at[0]).start()
    loop(1, 64, send_slot)
    conv_copy.wait()
    embed_t[...] = embed_w[...].T
    halo_finish(cot, 0, x3_cot)

    def keep_back(r, acc):
        back[r] = acc

    conv(x3_cot, 1, keep_back, flip=True)
    meta_wait(2)

    placed[...] = jnp.zeros_like(placed)
    counts[...] = jnp.zeros_like(counts)
    slot_mask = jnp.where(
        lax.rem(iota((CAP, 128), 1), 32) == iota((CAP, 128), 0), 1.0, 0.0
    ).astype(F32)
    spread = jnp.where(
        lax.div(iota((128, 512), 0), 32) == lax.div(iota((128, 512), 1), 128), 1.0, 0.0
    ).astype(BF16)
    lane, line = iota((COLS + 16, 128), 1), iota((COLS + 16, 128), 0)
    pick = jnp.where(lax.div(lane, 32) == jnp.where(line < COLS, 0, 3), 1.0, 0.0).astype(BF16)
    decay = sharp[...] * (-1.0 / 256.0)

    def place_group(g):
        def stretch(b):
            for i in range(8):
                s = 8 * b + i
                dx, dy, dz = offset(g * 16 + 4 * b + i // 2)
                sx, sy = lax.rem(xi + 4 - dx, 4), lax.rem(yi + 4 - dy, 4)
                source = meta[sy * 2 + i % 2, sx, lax.rem(lat + 4 - dz, 4)]
                line = jnp.broadcast_to(source, (CAP, 128)) * slot_mask
                tmeta[aligned(s * CAP, CAP, CAP), :] = line.astype(BF16)

        loop(0, 4, stretch)
        await_bytes(vals.at[pl.ds(g * 16, 16)], a2a_recv.at[g])

        for b in range(4):
            at = slice(b * 256, b * 256 + 256)
            of = aligned(g * GROUP + b * 256, 256, 256)
            wide = dot(tmeta[at, :], spread)
            colb[of, :] = wide[:, 0:128].astype(BF16)
            rowb[of, :] = wide[:, 384:512].astype(BF16)
            rk_of = jnp.concatenate([wide[:, 128:256]] * 2, axis=1)
            radius = jnp.concatenate([wide[:, 256:384]] * 2, axis=1)
            rk[at, :] = jnp.where(
                rk_of == iota((256, 256), 1).astype(F32), 1.0, 0.0
            ).astype(BF16)
            w = jnp.exp(radius * decay)
            weight[of, :] = w
            ew[at, :] = (dot(vals[pl.ds(g * 16 + 4 * b, 4)].reshape(256, VALS), embed_w[...]) * w).astype(BF16)

        both = lax.dot_general(pick, tmeta[...], NT, preferred_element_type=F32)
        colhot[...] = jnp.where(
            both[0:COLS] == iota((COLS, GROUP), 0).astype(F32), 1.0, 0.0
        ).astype(BF16)
        rowl[...] = both[COLS : COLS + 16]
        counts[...] += dot(colhot[...], rk[...])

        hot = colhot[...].reshape(8, 16, GROUP)
        for b in range(4):
            rows = []
            for r in range(4 * b, 4 * b + 4):
                mask = jnp.where(rowl[...] == float(r), 1.0, 0.0).astype(BF16)
                rows.append((hot * mask[None]).reshape(COLS, GROUP))
            at = slice(b * 512, b * 512 + 512)
            placed[at, :] += dot(jnp.concatenate(rows, axis=0), ew[...])

    loop(0, 4, place_group)

    kind = lax.rem(iota((256, CH), 0), 16)
    half_u, half_v = 2 * lax.div(kind, 4) + 1, 2 * lax.rem(kind, 4) + 1
    table = jnp.exp((half_u * half_u + half_v * half_v).astype(F32) * decay)
    table_hi = table.astype(BF16)
    table_lo = (table - table_hi.astype(F32)).astype(BF16)
    tables = jnp.concatenate([table_hi, table_lo], axis=0)
    row_of_lane = lax.div(iota((COLS, 256), 1), 16)
    for b in range(4):
        rows = []
        for r in range(4 * b, 4 * b + 4):
            rows.append(jnp.where(row_of_lane == r, counts[...], 0.0).astype(BF16))
        tally = jnp.concatenate(rows, axis=0)
        recip = 1.0 / (dot(jnp.concatenate([tally, tally], axis=1), tables) + 1.0)
        at = slice(4 * b, 4 * b + 4)
        inv[at] = grid4(recip)
        value = (placed[b * 512 : b * 512 + 512, :] * recip).astype(BF16)
        base[at] = grid4(value)
        x = value.astype(F32)
        s = sigmoid(x)
        act_zero[at] = grid4((x * s).astype(BF16))
        bend[at] = grid4(s * (1.0 + x * (1.0 - s)))

    halo_pack(act_zero, 1)
    halo_start(act_zero, 1)
    widen(act_zero, x3_act)
    turn_act(act_zero, zero_t)
    halo_finish(act_zero, 1, x3_act)

    def keep_mid(r, acc):
        value = (base[r].astype(F32) + acc).astype(BF16)
        mid[r] = value
        x = value.astype(F32)
        s = sigmoid(x)
        act_one[r] = (x * s).astype(BF16)
        slope = s * (1.0 + x * (1.0 - s))
        gmid[r] = (cot[r].astype(F32) + back[r] * slope).astype(BF16)

    conv(x3_act, 0, keep_mid)
    halo_pack(gmid, 2)
    halo_start(gmid, 2)
    halo_pack(act_one, 3)
    halo_start(act_one, 3)

    def kernel_grad(act_t, x3, k):
        for p in range(3):
            block = dot(act_t[...], x3[2 - p : 2 - p + ROWS].reshape(CELLS, 3 * CH))
            for q in range(3):
                for h in range(2):
                    at, lanes = (6 * p + 2 * q + h) * CH, (2 - q) * CH + h * 128
                    grads[k, at : at + CH, :] = block[:, lanes : lanes + 128].astype(BF16)

    coords = {"x": xi, "y": yi, "z": lat}
    orders = (("x", "y", "z"), ("y", "z", "x"), ("z", "x", "y"))

    def along(axis, c):
        cx, cy, cz = [c if axis == n else coords[n] for n in ("x", "y", "z")]
        return cz, cx * 8 + cy * 2 + ci

    def turned(axis, d):
        return lax.rem(coords[axis] + d, 4)

    def part_copies(k, stage):
        copies = []
        for a, order in enumerate(orders):
            own = a * PART + ci * HALF
            sems = lambda d: (ar_send.at[k, stage, a, d], ar_recv.at[k, stage, a, d])
            quarter = own + coords[order[0]] * QUARTER
            shard = quarter + coords[order[1]] * SHARD
            if stage == 0:
                src = grads.at[k, aligned(a * PART + (1 - ci) * HALF, HALF, 16)]
                copies.append(remote(src, p0.at[k, a], *sems(0), lat, other_core))
            elif stage == 6:
                piece = total.at[k, aligned(own, HALF, 16)]
                copies.append(remote(piece, piece, *sems(0), lat, other_core))
            else:
                axis = order[{1: 0, 2: 1, 3: 2, 4: 1, 5: 0}[stage]]
                for d in (1, 3, 2):
                    c = turned(axis, d)
                    if stage == 1:
                        src = s1.at[k, a, aligned(c * QUARTER, QUARTER, 16)]
                        dst = p1.at[k, a, d - 1]
                    elif stage == 2:
                        src = s2.at[k, a, aligned(c * SHARD, SHARD, 16)]
                        dst = p2.at[k, a, d - 1]
                    elif stage == 3:
                        src, dst = s3.at[k, a], p3.at[k, a, coords[axis]]
                    elif stage == 4:
                        src = dst = total.at[k, aligned(shard, SHARD, 16)]
                    else:
                        src = dst = total.at[k, aligned(quarter, QUARTER, 16)]
                    copies.append(remote(src, dst, *sems(d - 1), *along(axis, c)))
        return copies

    def ar_start(k, stage):
        for copy in part_copies(k, stage):
            copy.start()

    def ar_finish(k, stage):
        for copy in part_copies(k, stage):
            copy.wait()
        for a, order in enumerate(orders):
            own = a * PART + ci * HALF
            if stage == 0:
                here = grads[k, aligned(own, HALF, 16), :].astype(F32)
                s1[k, a] = (here + p0[k, a].astype(F32)).astype(BF16)
            elif stage in (1, 2):
                size = QUARTER if stage == 1 else SHARD
                src, came, dst = (s1, p1, s2) if stage == 1 else (s2, p2, s3)
                at = aligned(coords[order[stage - 1]] * size, size, 16)
                here = src[k, a, at, :].astype(F32)
                for d in range(3):
                    here += came[k, a, d].astype(F32)
                dst[k, a] = here.astype(BF16)
            elif stage == 3:
                p3[k, a, coords[order[2]]] = s3[k, a]
                whole = p3[k, a, 0].astype(F32)
                for d in range(1, 4):
                    whole += p3[k, a, d].astype(F32)
                quarter = own + coords[order[0]] * QUARTER
                at = aligned(quarter + coords[order[1]] * SHARD, SHARD, 16)
                total[k, at, :] = whole.astype(BF16)

    def ar_step(k, stage):
        ar_finish(k, stage)
        ar_start(k, stage + 1)

    def ar_leave(k):
        return pltpu.make_async_copy(total.at[k], grads_out.at[k], local_sem.at[3 if k else 6])

    turn_act(act_one, act_t)
    kernel_grad(act_t, x3_cot, 1)
    ar_start(1, 0)
    widen(gmid, x3_mid)
    halo_finish(gmid, 2, x3_mid)
    ar_step(1, 0)
    kernel_grad(zero_t, x3_mid, 0)
    ar_start(0, 0)

    def keep_gp(r, acc):
        grad = gmid[r].astype(F32) + acc * bend[r]
        gp[r * COLS : (r + 1) * COLS, :] = (grad * inv[r]).astype(BF16)

    conv(x3_mid, 0, keep_gp, flip=True, low=0, high=2)
    ar_step(1, 1)
    ar_step(0, 0)
    conv(x3_mid, 0, keep_gp, flip=True, low=2, high=3)

    esum[...] = jnp.zeros_like(esum)

    def vg_copy(j):
        dx, dy, dz = offset(j)
        sx, sy, sz = lax.rem(xi + 4 - dx, 4), lax.rem(yi + 4 - dy, 4), lax.rem(lat + 4 - dz, 4)
        return remote(vg.at[j], relay.at[chip], vg_send, vg_recv, sz, sx * 8 + sy * 2 + ci)

    def gather(b):
        at = slice(b * 512, b * 512 + 512)
        chips = slice(b * 8, b * 8 + 8)
        hot = jnp.where(
            colb[at, :].astype(F32) == iota((512, COLS), 1).astype(F32), 1.0, 0.0
        ).astype(BF16)
        row_of = rowb[at, :]
        pieces = [
            jnp.where(row_of == jnp.array(r, BF16), hot, jnp.zeros_like(hot)) for r in range(ROWS)
        ]
        found = dot(jnp.concatenate(pieces, axis=1), gp[...])
        grad = (found * weight[at, :]).astype(BF16)
        vg[chips] = dot(grad, embed_t[...]).astype(BF16).reshape(8, 2, CAP, VALS)
        own = vals[chips].reshape(512, VALS)
        esum[...] += lax.dot_general(own, grad, TN, preferred_element_type=F32)
        for j in range(8 * b, 8 * b + 8):
            if j == 0:
                pltpu.make_async_copy(vg.at[0], relay.at[chip], vg_recv).start()
            else:
                vg_copy(j).start()

    gather(0)
    gather(1)
    ar_step(1, 2)
    gather(2)
    ar_step(0, 1)
    gather(3)
    ar_step(1, 3)
    gather(4)
    ar_step(0, 2)
    gather(5)
    ar_step(1, 4)
    gather(6)
    ar_step(0, 3)
    gather(7)
    ar_step(0, 4)

    member = yc
    column = xi * 4 + lat

    def embed_copies(stage):
        copies = []
        for d in range(1, 16 if stage == 1 else 8):
            if stage == 1:
                c = lax.rem(column + d, 16)
                tlat, tlon = lax.rem(c, 4), lax.div(c, 4) * 8 + member
                src, dst = esum.at[aligned(member * 16, 16, 16)], qe.at[column]
            else:
                m = lax.rem(member + d, 8)
                tlat, tlon = lat, xi * 8 + m
                if stage == 0:
                    src, dst = esum.at[aligned(m * 16, 16, 16)], pe.at[d - 1]
                else:
                    src = dst = etotal.at[aligned(member * 16, 16, 16)]
            copies.append(remote(src, dst, em_send.at[stage, d - 1], em_recv.at[stage, d - 1], tlat, tlon))
        return copies

    def embed_start(stage):
        for copy in embed_copies(stage):
            copy.start()

    def embed_wait(stage):
        for copy in embed_copies(stage):
            copy.wait()

    embed_start(0)
    widen(act_one, x3_act)
    halo_finish(act_one, 3, x3_act)
    ar_step(1, 5)

    def keep_enc(r, acc):
        enc[r] = (mid[r].astype(F32) + acc).astype(BF16)

    conv(x3_act, 1, keep_enc, low=0, high=2)
    embed_wait(0)
    own_rows = aligned(member * 16, 16, 16)
    mine = esum[own_rows, :]
    for d in range(7):
        mine += pe[d]
    esum[own_rows, :] = mine
    embed_start(1)
    ar_step(0, 5)
    ar_finish(1, 6)
    ar_leave(1).start()
    conv(x3_act, 1, keep_enc, low=2, high=3)
    enc_copy = pltpu.make_async_copy(enc, enc_out, local_sem.at[2])
    enc_copy.start()
    embed_wait(1)
    qe[column] = esum[own_rows, :]
    whole = qe[0]
    for d in range(1, 16):
        whole += qe[d]
    etotal[own_rows, :] = whole
    embed_start(2)
    await_bytes(relay, vg_recv)
    vg_own = pltpu.make_async_copy(relay.at[:, ci], vg_out.at[:, ci], local_sem.at[5])
    vg_own.start()
    vg_other = remote(
        relay.at[:, 1 - ci], vg_out.at[:, ci], pair_send.at[1], pair_recv.at[1], lat, other_core
    )
    vg_other.start()
    ar_finish(0, 6)
    ar_leave(0).start()
    embed_wait(2)
    embed_out[...] = etotal[...] * (1.0 / 512.0)
    for g in range(4):
        await_bytes(vals.at[pl.ds(0, 15 if g == 0 else 16)], a2a_send.at[g])
    for stage in range(3):
        meta_sent(stage)
    await_bytes(vg.at[pl.ds(0, 63)], vg_send)
    vg_own.wait()
    vg_other.wait()
    enc_copy.wait()
    ar_leave(1).wait()
    ar_leave(0).wait()


def hand_over(
    enc_in, vg_in, grads_in, embed_in, enc_out, vg_out, grads_out, embed_out,
    enc, vg, embed, narrow, wide, in_sem, out_sem,
):
    steps = []
    for i in range(18):
        src, dst = slice(i % 9 * 2 * CH, (i % 9 + 1) * 2 * CH), slice(i * CH, i * CH + CH)
        k = i // 9
        steps.append(
            (grads_in.at[k, src], narrow.at[k, src], wide.at[dst], grads_out.at[dst], (k, src, dst))
        )
    for i in range(2):
        at = slice(i * 8, i * 8 + 8)
        steps.append((enc_in.at[at], enc.at[at], enc.at[at], enc_out.at[at], None))
        at = slice(i * 32, i * 32 + 32)
        steps.append((vg_in.at[at], vg.at[at], vg.at[at], vg_out.at[at], None))
    steps.append((embed_in, embed, embed, embed_out, None))
    moves = [
        pltpu.make_async_copy(step[0], step[1], in_sem.at[i]) for i, step in enumerate(steps)
    ]
    for move in moves:
        move.start()
    results = []
    for i, (_, _, src, dst, at) in enumerate(steps):
        moves[i].wait()
        if at is not None:
            k, rows, to = at
            for h in range(2):
                half = slice(rows.start + h * CH, rows.start + h * CH + CH)
                wide[to, h * 128 : h * 128 + 128] = narrow[k, half, :].astype(F32) * (1.0 / 512.0)
        results.append(pltpu.make_async_copy(src, dst, out_sem.at[i]))
        results[i].start()
    for copy in results:
        copy.wait()


def on_device(
    obs_values, obs_cells, obs_subcell, slot_counts, sharpness, embed_weight, conv_weight, cotangent
):
    anywhere = pl.BlockSpec(memory_space=pl.ANY)
    vmem = pl.BlockSpec(memory_space=pltpu.VMEM)
    grid = (ROWS, COLS, CH)
    wide = (ROWS + 2, COLS, 3 * CH)
    dma = pltpu.SemaphoreType.DMA
    scratch = [
        pltpu.VMEM((64, 2, CAP, VALS), BF16),
        pltpu.VMEM((64, 2, CAP, VALS), BF16),
        pltpu.VMEM((64, 2, CAP, VALS), BF16),
        pltpu.VMEM((4, 32, 1, 128), F32),
        pltpu.VMEM((4, 4, 8, 1, 128), F32),
        pltpu.VMEM((4, 4, 4, 2, 1, 128), F32),
        pltpu.VMEM((8, 4, 4, 1, 128), F32),
        pltpu.VMEM((GROUP, 128), BF16),
        pltpu.VMEM((OBS, 128), BF16),
        pltpu.VMEM((OBS, 128), BF16),
        pltpu.VMEM((OBS, CH), F32),
        pltpu.VMEM((GROUP, CH), BF16),
        pltpu.VMEM((GROUP, 256), BF16),
        pltpu.VMEM((COLS, GROUP), BF16),
        pltpu.VMEM((16, GROUP), F32),
        pltpu.VMEM((CELLS, CH), F32),
        pltpu.VMEM((COLS, 256), F32),
        pltpu.VMEM(grid, F32),
        pltpu.VMEM(grid, BF16),
        pltpu.VMEM((2, 3, 3 * CH, CH), BF16),
        pltpu.VMEM((CH, VALS), BF16),
        pltpu.VMEM(grid, F32),
        pltpu.VMEM(grid, F32),
        pltpu.VMEM(grid, F32),
        pltpu.VMEM(grid, BF16),
        pltpu.VMEM(grid, BF16),
        pltpu.VMEM(grid, BF16),
        pltpu.VMEM(grid, BF16),
        pltpu.VMEM(grid, BF16),
        pltpu.VMEM((CELLS, CH), BF16),
        pltpu.VMEM((CH, CELLS), BF16),
        pltpu.VMEM((CH, CELLS), BF16),
        pltpu.VMEM(wide, BF16),
        pltpu.VMEM(wide, BF16),
        pltpu.VMEM(wide, BF16),
        pltpu.VMEM((4, 2, COLS, CH), BF16),
        pltpu.VMEM((4, 2, 3, 16, CH), BF16),
        pltpu.VMEM((4, 2, 16, CH), BF16),
        pltpu.VMEM((2, 16, CH), F32),
        pltpu.VMEM((64, 2, CAP, VALS), BF16),
        pltpu.VMEM((2, 3 * PART, 128), BF16),
        pltpu.VMEM((2, 3 * PART, 128), BF16),
        pltpu.VMEM((2, 3, HALF, 128), BF16),
        pltpu.VMEM((2, 3, HALF, 128), BF16),
        pltpu.VMEM((2, 3, 3, QUARTER, 128), BF16),
        pltpu.VMEM((2, 3, QUARTER, 128), BF16),
        pltpu.VMEM((2, 3, 3, SHARD, 128), BF16),
        pltpu.VMEM((2, 3, SHARD, 128), BF16),
        pltpu.VMEM((2, 3, 4, SHARD, 128), BF16),
        pltpu.VMEM((VALS, CH), F32),
        pltpu.VMEM((7, 16, CH), F32),
        pltpu.VMEM((16, 16, CH), F32),
        pltpu.VMEM((VALS, CH), F32),
        pltpu.VMEM(grid, BF16),
        dma((7,)),
        dma((2,)),
        dma((2,)),
        dma((4,)),
        dma((4,)),
        dma((3,)),
        dma((3,)),
        dma,
        dma,
        dma((4, 8)),
        dma((4, 8)),
        dma((2, 7, 3, 3)),
        dma((2, 7, 3, 3)),
        dma((3, 15)),
        dma((3, 15)),
    ]
    encoded, value_grads, grads, embed_total = pl.pallas_call(
        kernel,
        out_shape=(
            jax.ShapeDtypeStruct(grid, BF16),
            jax.ShapeDtypeStruct((64, 2, CAP, VALS), BF16),
            jax.ShapeDtypeStruct((2, 3 * PART, 128), BF16),
            jax.ShapeDtypeStruct((VALS, CH), F32),
        ),
        in_specs=[anywhere, vmem, vmem, vmem, vmem, vmem, anywhere, anywhere],
        out_specs=(anywhere, anywhere, anywhere, vmem),
        scratch_shapes=scratch,
        compiler_params=pltpu.CompilerParams(
            collective_id=0, has_side_effects=True, vmem_limit_bytes=60 * 1024 * 1024
        ),
        cost_estimate=pl.CostEstimate(
            flops=30_000_000_000, bytes_accessed=20_000_000, transcendentals=4_000_000
        ),
    )(
        obs_values.reshape(64, 2, CAP, VALS),
        obs_cells.reshape(32, 128),
        obs_subcell.reshape(32, 128),
        slot_counts,
        sharpness.reshape(1, CH),
        embed_weight,
        conv_weight.reshape(2, 3, 3 * CH, CH),
        cotangent,
    )
    encoded, value_grads, conv_grads, embed_grads = pl.pallas_call(
        hand_over,
        out_shape=(
            jax.ShapeDtypeStruct(grid, BF16),
            jax.ShapeDtypeStruct((64, 2, CAP, VALS), BF16),
            jax.ShapeDtypeStruct((3 * PART, CH), F32),
            jax.ShapeDtypeStruct((VALS, CH), F32),
        ),
        in_specs=[anywhere] * 4,
        out_specs=(anywhere,) * 4,
        scratch_shapes=[
            pltpu.VMEM(grid, BF16),
            pltpu.VMEM((64, 2, CAP, VALS), BF16),
            pltpu.VMEM((VALS, CH), F32),
            pltpu.VMEM((2, 3 * PART, 128), BF16),
            pltpu.VMEM((3 * PART, CH), F32),
            dma((23,)),
            dma((23,)),
        ],
        compiler_params=pltpu.CompilerParams(vmem_limit_bytes=60 * 1024 * 1024),
    )(encoded, value_grads, grads, embed_total)
    return (
        encoded,
        value_grads.reshape(OBS, VALS),
        conv_grads.reshape(2, 3, 3, CH, CH),
        embed_grads,
    )


def solution(mesh):
    placed = (
        P(("lat", "lon"), None),
        P(("lat", "lon")),
        P(("lat", "lon")),
        P(("lat", "lon"), None),
        P(),
        P(),
        P(),
        P("lat", "lon", None),
    )
    return jax.shard_map(
        on_device,
        mesh=mesh,
        in_specs=placed,
        out_specs=(P("lat", "lon", None), P(("lat", "lon"), None), P(), P()),
        check_vma=False,
    )
```

```python
import jax
import jax.numpy as jnp
from jax import lax
from jax.experimental import pallas as pl
from jax.experimental.pallas import tpu as pltpu
from jax.sharding import PartitionSpec as P

F32 = jnp.float32
BF16 = jnp.bfloat16
N_LAT, N_LON = 4, 32
DEVICES = N_LAT * N_LON
CAP, VALS, CH = 32, 128, 256
ROWS, COLS = 16, 128
CELLS = ROWS * COLS
OBS = DEVICES * CAP
GROUP = 32 * CAP
PART, HALF, QUARTER, SHARD = 1536, 768, 192, 48
NT = (((1,), (1,)), ((), ()))
TN = (((0,), (0,)), ((), ()))


def dot(a, b):
    return jnp.dot(a, b, preferred_element_type=F32)


def iota(shape, axis):
    return lax.broadcasted_iota(jnp.int32, shape, axis)


def sigmoid(x):
    return 0.5 + 0.5 * jnp.tanh(0.5 * x)


def remote(src, dst, send, recv, lat, lon):
    return pltpu.make_async_remote_copy(
        src_ref=src,
        dst_ref=dst,
        send_sem=send,
        recv_sem=recv,
        device_id=(lat, lon),
        device_id_type=pl.DeviceIdType.MESH,
    )


def await_bytes(ref, sem):
    pltpu.make_async_copy(ref, ref, sem).wait()


def loop(low, high, body):
    def step(i, carry):
        body(i)
        return carry

    lax.fori_loop(low, high, step, 0)


def aligned(start, size, unit):
    return pl.ds(pl.multiple_of(start, unit), size)


def kernel(
    obs_in, cells, subs, live_counts, sharp, embed_w, conv_in, cot_in,
    enc_out, vg_out, grads_out, embed_out,
    vals, queue, relay, meta_own, meta_z, meta_x, meta, tmeta, colb, rowb, weight, ew, rk, colhot, rowl, placed, counts, inv,
    cot, conv_w, embed_t, back, bend, base, act_zero, mid, act_one, gmid, gp, act_t, zero_t,
    x3_act, x3_cot, x3_mid, halo, strip, stripf,
    vg, grads, total, p0, s1, p1, s2, p2, s3, p3, esum, pe, qe, etotal, enc,
    local_sem, pair_send, pair_recv, a2a_send, a2a_recv, meta_send, meta_recv, vg_send, vg_recv,
    halo_send, halo_recv, ar_send, ar_recv, em_send, em_recv,
):
    lat = lax.axis_index("lat")
    lon = lax.axis_index("lon")
    me = lat * N_LON + lon
    xi, yi, ci = lax.div(lon, 8), lax.rem(lax.div(lon, 2), 4), lax.rem(lon, 2)

    chip = lat * 16 + xi * 4 + yi
    yc = lax.rem(lon, 8)
    other_core = lon + 1 - 2 * ci

    def offset(j):
        g, dx, dy = lax.div(j, 16), lax.rem(lax.div(j, 4), 4), lax.rem(j, 4)
        return dx, dy, lax.rem(g + 8 - dx - dy, 4)

    barrier = pltpu.get_barrier_semaphore()

    cot_copy = pltpu.make_async_copy(cot_in, cot, local_sem.at[0])
    cot_copy.start()
    pair_own = pltpu.make_async_copy(obs_in.at[:, ci], queue.at[:, ci], local_sem.at[4])
    pair_own.start()
    pair_other = remote(
        obs_in.at[:, 1 - ci], queue.at[:, ci], pair_send.at[0], pair_recv.at[0], lat, other_core
    )

    def signal(tlat, tlon):
        pl.semaphore_signal(
            barrier, inc=1, device_id=(tlat, tlon), device_id_type=pl.DeviceIdType.MESH
        )

    def greet(j):
        tx, ty = lax.rem(xi + lax.div(j, 16), 4), lax.rem(yi + lax.rem(j, 4), 4)
        signal(lax.rem(lat + lax.rem(lax.div(j, 4), 4), 4), tx * 8 + ty * 2 + ci)

    loop(1, 64, greet)
    beside = lax.rem(lon + N_LON - 1 + 2 * ci, N_LON)
    for turn in (0, 1, 3):
        signal(lax.rem(lat + turn, N_LAT), other_core)
        signal(lax.rem(lat + turn, N_LAT), beside)
    for d in range(1, 4):
        signal(lat, xi * 8 + lax.rem(yi + d, 4) * 2 + 1 - ci)

    def meta_copies(stage):
        copies = []
        for d in range(1, 8 if stage == 2 else 4):
            if stage == 0:
                c = lax.rem(lat + d, 4)
                src, dst, target = meta_own.at[:, pl.ds(c * 8, 8)], meta_z.at[lat], (c, lon)
            elif stage == 1:
                c = lax.rem(xi + d, 4)
                src, dst = meta_z.at[:, :, pl.ds(c * 2, 2)], meta_x.at[xi]
                target = (lat, c * 8 + yc)
            else:
                c = lax.rem(yc + d, 8)
                src, dst = meta_x.at[:, :, lax.rem(c, 4), lax.div(c, 4)], meta.at[yc]
                target = (lat, xi * 8 + c)
            copies.append(remote(src, dst, meta_send.at[stage], meta_recv.at[stage], *target))
        own = (
            (meta_own.at[:, pl.ds(lat * 8, 8)], meta_z.at[lat]),
            (meta_z.at[:, :, pl.ds(xi * 2, 2)], meta_x.at[xi]),
            (meta_x.at[:, :, lax.rem(yc, 4), lax.div(yc, 4)], meta.at[yc]),
        )[stage]
        copies.append(pltpu.make_async_copy(*own, meta_recv.at[stage]))
        return copies

    def meta_start(stage):
        for copy in meta_copies(stage):
            copy.start()

    def meta_wait(stage):
        await_bytes((meta_z, meta_x, meta)[stage], meta_recv.at[stage])

    def meta_sent(stage):
        await_bytes((meta_z, meta_x, meta)[stage].at[pl.ds(0, (3, 3, 7)[stage])], meta_send.at[stage])

    line, lane = iota((32, 128), 0), iota((32, 128), 1)
    own_four = jnp.where(lax.div(lane, 4) == line, live_counts[...].astype(F32), 0.0).astype(BF16)
    to_slots = jnp.where(
        lax.rem(iota((128, 128), 0), 4) == lax.div(iota((128, 128), 1), 32), 1.0, 0.0
    ).astype(BF16)
    live = lax.rem(lane, 32).astype(F32) < dot(own_four, to_slots)
    cell, sub = cells[...], subs[...]
    u, v = sub >> 3, sub & 7
    u = jnp.where(u >= 4, u - 4, 3 - u)
    v = jnp.where(v >= 4, v - 4, 3 - v)
    row = cell >> 7
    fields = [
        jnp.where(live, (cell & 127).astype(F32), 255.0),
        (row * 16 + u * 4 + v).astype(F32),
        ((2 * u + 1) * (2 * u + 1) + (2 * v + 1) * (2 * v + 1)).astype(F32),
        row.astype(F32),
    ]
    for i in range(4):
        mixed = jnp.zeros((32, 128), F32)
        for f in range(4):
            shift = (f - i) * 32 % 128
            turned_field = pltpu.roll(fields[f], shift, 1) if shift else fields[f]
            mixed = jnp.where(lax.div(lane, 32) == f, turned_field, mixed)
        for r in range(32):
            meta_own[i, r] = mixed[r : r + 1, :]

    conv_copy = pltpu.make_async_copy(conv_in, conv_w, local_sem.at[1])
    conv_copy.start()

    def send_slot(j):
        dx, dy, dz = offset(j)
        tx, ty, tz = lax.rem(xi + dx, 4), lax.rem(yi + dy, 4), lax.rem(lat + dz, 4)
        g = lax.div(j, 16)
        remote(
            queue.at[tz * 16 + tx * 4 + ty], vals.at[j], a2a_send.at[g], a2a_recv.at[g],
            tz, tx * 8 + ty * 2 + ci,
        ).start()

    north, south = lax.rem(lat + 3, N_LAT), lax.rem(lat + 1, N_LAT)
    west, east = lax.rem(lon + N_LON - 1, N_LON), lax.rem(lon + 1, N_LON)

    def halo_row(k, side):
        return halo.at[k, side * COLS : (side + 1) * COLS]

    def halo_col(k, side, turn):
        at = 2 * COLS + 16 * (3 * side + turn)
        return halo.at[k, at : at + 16]

    def halo_copies(src, k):
        pieces = [(src.at[ROWS - 1], halo_row(k, 0), south, lon)]
        pieces.append((src.at[0], halo_row(k, 1), north, lon))
        for side, column, target in ((0, 1, east), (1, 0, west)):
            for turn, tlat in enumerate((lat, south, north)):
                pieces.append((strip.at[k, column], halo_col(k, side, turn), tlat, target))
        return [remote(s, d, halo_send.at[k], halo_recv.at[k], a, b) for s, d, a, b in pieces]

    def halo_pack(src, k):
        for r in range(ROWS):
            stripf[0, r : r + 1, :] = src[r, 0:16, :].astype(F32)[0:1, :]
            stripf[1, r : r + 1, :] = src[r, COLS - 16 : COLS, :].astype(F32)[15:16, :]
        strip[k, 0] = stripf[0].astype(BF16)
        strip[k, 1] = stripf[1].astype(BF16)

    def halo_start(src, k):
        for copy in halo_copies(src, k):
            copy.start()

    def widen(src, x3, low=0, high=4):
        def body(b):
            for i in range(4):
                r = 4 * b + i
                row = src[r].astype(F32)
                x3[r + 1, :, 0:CH] = pltpu.roll(row, 1, 0).astype(BF16)
                x3[r + 1, :, CH : 2 * CH] = src[r]
                x3[r + 1, :, 2 * CH : 3 * CH] = pltpu.roll(row, COLS - 1, 0).astype(BF16)

        loop(low, high, body)

    def halo_finish(src, k, x3):
        await_bytes(halo.at[k], halo_recv.at[k])
        await_bytes(halo.at[k], halo_send.at[k])
        first = iota((16, CH), 0) == 0
        last = iota((16, CH), 0) == 15
        left = halo_col(k, 0, 0)[...].astype(F32)
        right = halo_col(k, 1, 0)[...].astype(F32)
        for r in range(ROWS):
            low = x3[r + 1, 0:16, 0:CH].astype(F32)
            x3[r + 1, 0:16, 0:CH] = jnp.where(first, left[r : r + 1, :], low).astype(BF16)
            high = x3[r + 1, COLS - 16 : COLS, 2 * CH : 3 * CH].astype(F32)
            x3[r + 1, COLS - 16 : COLS, 2 * CH : 3 * CH] = jnp.where(
                last, right[r : r + 1, :], high
            ).astype(BF16)
        spot = iota((COLS, CH), 0)
        for side, r, turn, pick, valid in (
            (0, 0, 1, ROWS - 1, lat > 0),
            (1, ROWS + 1, 2, 0, lat < N_LAT - 1),
        ):
            keep = jnp.where(valid, 1.0, 0.0).astype(F32)
            row = halo_row(k, side)[...].astype(F32) * keep
            lcorner = halo_col(k, 0, turn)[...].astype(F32)[pick : pick + 1, :] * keep
            rcorner = halo_col(k, 1, turn)[...].astype(F32)[pick : pick + 1, :] * keep
            x3[r, :, 0:CH] = jnp.where(spot == 0, lcorner, pltpu.roll(row, 1, 0)).astype(BF16)
            x3[r, :, CH : 2 * CH] = row.astype(BF16)
            x3[r, :, 2 * CH : 3 * CH] = jnp.where(
                spot == COLS - 1, rcorner, pltpu.roll(row, COLS - 1, 0)
            ).astype(BF16)

    def conv(x3, k, finish, flip=False, low=0, high=4):
        if flip:
            taps = [
                conv_w[k, 2 - p, (2 - q) * CH : (3 - q) * CH, :] for p in range(3) for q in range(3)
            ]
            taps = jnp.concatenate(taps, axis=1)
        else:
            taps = conv_w[k].reshape(9 * CH, CH)
        for b in range(low, high):
            near = [x3[4 * b + p : 4 * b + p + 4].reshape(4 * COLS, 3 * CH) for p in range(3)]
            near = jnp.concatenate(near, axis=1)
            if flip:
                acc = lax.dot_general(near, taps, NT, preferred_element_type=F32)
            else:
                acc = dot(near, taps)
            finish(slice(4 * b, 4 * b + 4), acc)

    def tile4(x):
        return x.reshape(4 * COLS, CH)

    def grid4(x):
        return x.reshape(4, COLS, CH)

    def turn_act(act, act_t):
        for r in range(ROWS):
            act_t[:, r * COLS : (r + 1) * COLS] = act[r].T

    cot_copy.wait()
    halo_pack(cot, 0)
    pl.semaphore_wait(barrier, 72)
    pair_other.start()
    meta_start(0)
    halo_start(cot, 0)
    widen(cot, x3_cot, 0, 2)
    meta_wait(0)
    meta_start(1)
    widen(cot, x3_cot, 2, 4)
    meta_wait(1)
    meta_start(2)
    pair_own.wait()
    pair_other.wait()
    pltpu.make_async_copy(queue.at[chip], vals.at[0], a2a_recv.at[0]).start()
    loop(1, 16, send_slot)
    conv_copy.wait()
    embed_t[...] = embed_w[...].T
    halo_finish(cot, 0, x3_cot)

    def keep_back(rows, acc):
        back[rows] = grid4(acc)

    for g in range(1, 4):
        for j in range(16 * g, 16 * g + 16):
            send_slot(j)
        conv(x3_cot, 1, keep_back, flip=True, low=g - 1, high=4 if g == 3 else g)
    meta_wait(2)

    placed[...] = jnp.zeros_like(placed)
    counts[...] = jnp.zeros_like(counts)
    slot_mask = jnp.where(
        lax.rem(iota((CAP, 128), 1), 32) == iota((CAP, 128), 0), 1.0, 0.0
    ).astype(F32)
    spread = jnp.where(
        lax.div(iota((128, 512), 0), 32) == lax.div(iota((128, 512), 1), 128), 1.0, 0.0
    ).astype(BF16)
    lane, line = iota((COLS + 16, 128), 1), iota((COLS + 16, 128), 0)
    pick = jnp.where(lax.div(lane, 32) == jnp.where(line < COLS, 0, 3), 1.0, 0.0).astype(BF16)
    decay = sharp[...] * (-1.0 / 256.0)

    for g in range(4):
        def stretch(b, g=g):
            for i in range(8):
                s = 8 * b + i
                dx, dy, dz = offset(g * 16 + 4 * b + i // 2)
                sx, sy = lax.rem(xi + 4 - dx, 4), lax.rem(yi + 4 - dy, 4)
                source = meta[sy * 2 + i % 2, sx, lax.rem(lat + 4 - dz, 4)]
                line = jnp.broadcast_to(source, (CAP, 128)) * slot_mask
                tmeta[aligned(s * CAP, CAP, CAP), :] = line.astype(BF16)

        loop(0, 4, stretch)
        await_bytes(vals.at[pl.ds(g * 16, 16)], a2a_recv.at[g])

        for b in range(4):
            at = slice(b * 256, b * 256 + 256)
            of = slice(g * GROUP + b * 256, g * GROUP + b * 256 + 256)
            wide = dot(tmeta[at, :], spread)
            colb[of, :] = wide[:, 0:128].astype(BF16)
            rowb[of, :] = wide[:, 384:512].astype(BF16)
            rk_of = jnp.concatenate([wide[:, 128:256]] * 2, axis=1)
            radius = jnp.concatenate([wide[:, 256:384]] * 2, axis=1)
            rk[at, :] = jnp.where(
                rk_of == iota((256, 256), 1).astype(F32), 1.0, 0.0
            ).astype(BF16)
            w = jnp.exp(radius * decay)
            weight[of, :] = w
            ew[at, :] = (dot(vals[g * 16 + 4 * b : g * 16 + 4 * b + 4].reshape(256, VALS), embed_w[...]) * w).astype(BF16)

        both = lax.dot_general(pick, tmeta[...], NT, preferred_element_type=F32)
        colhot[...] = jnp.where(
            both[0:COLS] == iota((COLS, GROUP), 0).astype(F32), 1.0, 0.0
        ).astype(BF16)
        rowl[...] = both[COLS : COLS + 16]
        counts[...] += dot(colhot[...], rk[...])

        hot = colhot[...].reshape(8, 16, GROUP)
        for b in range(4):
            rows = []
            for r in range(4 * b, 4 * b + 4):
                mask = jnp.where(rowl[...] == float(r), 1.0, 0.0).astype(BF16)
                rows.append((hot * mask[None]).reshape(COLS, GROUP))
            at = slice(b * 512, b * 512 + 512)
            placed[at, :] += dot(jnp.concatenate(rows, axis=0), ew[...])

    kind = lax.rem(iota((256, CH), 0), 16)
    half_u, half_v = 2 * lax.div(kind, 4) + 1, 2 * lax.rem(kind, 4) + 1
    table = jnp.exp((half_u * half_u + half_v * half_v).astype(F32) * decay)
    table_hi = table.astype(BF16)
    table_lo = (table - table_hi.astype(F32)).astype(BF16)
    tables = jnp.concatenate([table_hi, table_lo], axis=0)
    row_of_lane = lax.div(iota((COLS, 256), 1), 16)
    for b in range(4):
        rows = []
        for r in range(4 * b, 4 * b + 4):
            rows.append(jnp.where(row_of_lane == r, counts[...], 0.0).astype(BF16))
        tally = jnp.concatenate(rows, axis=0)
        recip = 1.0 / (dot(jnp.concatenate([tally, tally], axis=1), tables) + 1.0)
        at = slice(4 * b, 4 * b + 4)
        inv[at] = grid4(recip)
        value = (placed[b * 512 : b * 512 + 512, :] * recip).astype(BF16)
        base[at] = grid4(value)
        x = value.astype(F32)
        s = sigmoid(x)
        act_zero[at] = grid4((x * s).astype(BF16))
        bend[at] = grid4(s * (1.0 + x * (1.0 - s)))

    halo_pack(act_zero, 1)
    halo_start(act_zero, 1)
    widen(act_zero, x3_act)
    turn_act(act_zero, zero_t)
    halo_finish(act_zero, 1, x3_act)

    def keep_mid(rows, acc):
        value = (tile4(base[rows]).astype(F32) + acc).astype(BF16)
        mid[rows] = grid4(value)
        x = value.astype(F32)
        s = sigmoid(x)
        act_one[rows] = grid4((x * s).astype(BF16))
        slope = s * (1.0 + x * (1.0 - s))
        grad = tile4(cot[rows]).astype(F32) + tile4(back[rows]) * slope
        gmid[rows] = grid4(grad.astype(BF16))

    conv(x3_act, 0, keep_mid)
    halo_pack(gmid, 2)
    halo_start(gmid, 2)
    halo_pack(act_one, 3)
    halo_start(act_one, 3)

    def kernel_grad(act_t, x3, k):
        for p in range(3):
            block = dot(act_t[...], x3[2 - p : 2 - p + ROWS].reshape(CELLS, 3 * CH))
            for q in range(3):
                for h in range(2):
                    at, lanes = (6 * p + 2 * q + h) * CH, (2 - q) * CH + h * 128
                    grads[k, at : at + CH, :] = block[:, lanes : lanes + 128].astype(BF16)

    coords = {"x": xi, "y": yi, "z": lat}
    orders = (("x", "y", "z"), ("y", "z", "x"), ("z", "x", "y"))

    def along(axis, c):
        cx, cy, cz = [c if axis == n else coords[n] for n in ("x", "y", "z")]
        return cz, cx * 8 + cy * 2 + ci

    def turned(axis, d):
        return lax.rem(coords[axis] + d, 4)

    def part_copies(k, stage):
        copies = []
        for a, order in enumerate(orders):
            own = a * PART + ci * HALF
            sems = (ar_send.at[k, stage], ar_recv.at[k, stage])
            quarter = own + coords[order[0]] * QUARTER
            shard = quarter + coords[order[1]] * SHARD
            if stage == 0:
                src = grads.at[k, aligned(a * PART + (1 - ci) * HALF, HALF, 16)]
                copies.append(remote(src, p0.at[k, a], *sems, lat, other_core))
            elif stage == 6:
                piece = total.at[k, aligned(own, HALF, 16)]
                copies.append(remote(piece, piece, *sems, lat, other_core))
            else:
                axis = order[{1: 0, 2: 1, 3: 2, 4: 1, 5: 0}[stage]]
                for d in (1, 3, 2):
                    c = turned(axis, d)
                    if stage == 1:
                        src = s1.at[k, a, aligned(c * QUARTER, QUARTER, 16)]
                        dst = p1.at[k, a, d - 1]
                    elif stage == 2:
                        src = s2.at[k, a, aligned(c * SHARD, SHARD, 16)]
                        dst = p2.at[k, a, d - 1]
                    elif stage == 3:
                        src, dst = s3.at[k, a], p3.at[k, a, coords[axis]]
                    elif stage == 4:
                        src = dst = total.at[k, aligned(shard, SHARD, 16)]
                    else:
                        src = dst = total.at[k, aligned(quarter, QUARTER, 16)]
                    copies.append(remote(src, dst, *sems, *along(axis, c)))
        return copies

    def ar_start(k, stage):
        for copy in part_copies(k, stage):
            copy.start()

    def ar_finish(k, stage):
        amount = (p0, p1, p2, p2, p2, p1, p0)[stage].at[k]
        await_bytes(amount, ar_recv.at[k, stage])
        await_bytes(amount, ar_send.at[k, stage])
        for a, order in enumerate(orders):
            own = a * PART + ci * HALF
            if stage == 0:
                here = grads[k, aligned(own, HALF, 16), :].astype(F32)
                s1[k, a] = (here + p0[k, a].astype(F32)).astype(BF16)
            elif stage in (1, 2):
                size = QUARTER if stage == 1 else SHARD
                src, came, dst = (s1, p1, s2) if stage == 1 else (s2, p2, s3)
                at = aligned(coords[order[stage - 1]] * size, size, 16)
                here = src[k, a, at, :].astype(F32)
                for d in range(3):
                    here += came[k, a, d].astype(F32)
                dst[k, a] = here.astype(BF16)
            elif stage == 3:
                p3[k, a, coords[order[2]]] = s3[k, a]
                whole = p3[k, a, 0].astype(F32)
                for d in range(1, 4):
                    whole += p3[k, a, d].astype(F32)
                quarter = own + coords[order[0]] * QUARTER
                at = aligned(quarter + coords[order[1]] * SHARD, SHARD, 16)
                total[k, at, :] = whole.astype(BF16)

    def ar_step(k, stage):
        ar_finish(k, stage)
        ar_start(k, stage + 1)

    def ar_leave(k):
        return pltpu.make_async_copy(total.at[k], grads_out.at[k], local_sem.at[3 if k else 6])

    turn_act(act_one, act_t)
    kernel_grad(act_t, x3_cot, 1)
    ar_start(1, 0)
    widen(gmid, x3_mid)
    halo_finish(gmid, 2, x3_mid)
    ar_step(1, 0)
    kernel_grad(zero_t, x3_mid, 0)
    ar_start(0, 0)

    def keep_gp(rows, acc):
        grad = tile4(gmid[rows]).astype(F32) + acc * tile4(bend[rows])
        gp[rows.start * COLS : rows.stop * COLS, :] = (
            grad * tile4(inv[rows])
        ).astype(BF16)

    conv(x3_mid, 0, keep_gp, flip=True, low=0, high=2)
    ar_step(1, 1)
    ar_step(0, 0)
    conv(x3_mid, 0, keep_gp, flip=True, low=2, high=4)

    esum[...] = jnp.zeros_like(esum)

    def vg_copy(j):
        dx, dy, dz = offset(j)
        sx, sy, sz = lax.rem(xi + 4 - dx, 4), lax.rem(yi + 4 - dy, 4), lax.rem(lat + 4 - dz, 4)
        return remote(vg.at[j], relay.at[chip], vg_send, vg_recv, sz, sx * 8 + sy * 2 + ci)

    def gather(b):
        at = slice(b * 512, b * 512 + 512)
        chips = slice(b * 8, b * 8 + 8)
        hot = jnp.where(
            colb[at, :].astype(F32) == iota((512, COLS), 1).astype(F32), 1.0, 0.0
        ).astype(BF16)
        row_of = rowb[at, :]
        pieces = [
            jnp.where(row_of == jnp.array(r, BF16), hot, jnp.zeros_like(hot)) for r in range(ROWS)
        ]
        found = dot(jnp.concatenate(pieces, axis=1), gp[...])
        grad = (found * weight[at, :]).astype(BF16)
        vg[chips] = dot(grad, embed_t[...]).astype(BF16).reshape(8, 2, CAP, VALS)
        own = vals[chips].reshape(512, VALS)
        esum[...] += lax.dot_general(own, grad, TN, preferred_element_type=F32)
        for j in range(8 * b, 8 * b + 8):
            if j == 0:
                pltpu.make_async_copy(vg.at[0], relay.at[chip], vg_recv).start()
            else:
                vg_copy(j).start()

    gather(0)
    gather(1)
    ar_step(1, 2)
    gather(2)
    ar_step(0, 1)
    gather(3)
    ar_step(1, 3)
    gather(4)
    ar_step(0, 2)
    gather(5)
    ar_step(1, 4)
    gather(6)
    ar_step(0, 3)
    gather(7)
    ar_step(0, 4)

    member = yc
    column = xi * 4 + lat

    def embed_copies(stage):
        copies = []
        for d in range(1, 16 if stage == 1 else 8):
            if stage == 1:
                c = lax.rem(column + d, 16)
                tlat, tlon = lax.rem(c, 4), lax.div(c, 4) * 8 + member
                src, dst = esum.at[aligned(member * 16, 16, 16)], qe.at[column]
            else:
                m = lax.rem(member + d, 8)
                tlat, tlon = lat, xi * 8 + m
                if stage == 0:
                    src, dst = esum.at[aligned(m * 16, 16, 16)], pe.at[d - 1]
                else:
                    src = dst = etotal.at[aligned(member * 16, 16, 16)]
            copies.append(remote(src, dst, em_send.at[stage], em_recv.at[stage], tlat, tlon))
        return copies

    def embed_start(stage):
        for copy in embed_copies(stage):
            copy.start()

    def embed_wait(stage):
        amount = qe.at[pl.ds(0, 15)] if stage == 1 else pe
        await_bytes(amount, em_recv.at[stage])
        await_bytes(amount, em_send.at[stage])

    embed_start(0)
    widen(act_one, x3_act)
    halo_finish(act_one, 3, x3_act)
    ar_step(1, 5)

    def keep_enc(rows, acc):
        enc[rows] = grid4((tile4(mid[rows]).astype(F32) + acc).astype(BF16))

    conv(x3_act, 1, keep_enc, low=0, high=2)
    embed_wait(0)
    own_rows = aligned(member * 16, 16, 16)
    mine = esum[own_rows, :]
    for d in range(7):
        mine += pe[d]
    esum[own_rows, :] = mine
    embed_start(1)
    ar_step(0, 5)
    ar_finish(1, 6)
    ar_leave(1).start()
    conv(x3_act, 1, keep_enc, low=2, high=4)
    enc_copy = pltpu.make_async_copy(enc, enc_out, local_sem.at[2])
    enc_copy.start()
    embed_wait(1)
    qe[column] = esum[own_rows, :]
    whole = qe[0]
    for d in range(1, 16):
        whole += qe[d]
    etotal[own_rows, :] = whole
    embed_start(2)
    await_bytes(relay, vg_recv)
    vg_own = pltpu.make_async_copy(relay.at[:, ci], vg_out.at[:, ci], local_sem.at[5])
    vg_own.start()
    vg_other = remote(
        relay.at[:, 1 - ci], vg_out.at[:, ci], pair_send.at[1], pair_recv.at[1], lat, other_core
    )
    vg_other.start()
    ar_finish(0, 6)
    ar_leave(0).start()
    embed_wait(2)
    embed_out[...] = etotal[...] * (1.0 / 512.0)
    for g in range(4):
        await_bytes(vals.at[pl.ds(0, 15 if g == 0 else 16)], a2a_send.at[g])
    for stage in range(3):
        meta_sent(stage)
    await_bytes(vg.at[pl.ds(0, 63)], vg_send)
    vg_own.wait()
    vg_other.wait()
    enc_copy.wait()
    ar_leave(1).wait()
    ar_leave(0).wait()


def hand_over(
    enc_in, vg_in, grads_in, embed_in, enc_out, vg_out, grads_out, embed_out,
    enc, vg, embed, narrow, wide, in_sem, out_sem,
):
    steps = []
    for i in range(6):
        src, dst = slice(i % 3 * PART, (i % 3 + 1) * PART), slice(i * 3 * CH, (i + 1) * 3 * CH)
        k = i // 3
        steps.append(
            (grads_in.at[k, src], narrow.at[k, src], wide.at[dst], grads_out.at[dst], (k, src, dst))
        )
    steps.append((enc_in, enc, enc, enc_out, None))
    steps.append((vg_in, vg, vg, vg_out, None))
    steps.append((embed_in, embed, embed, embed_out, None))
    moves = [
        pltpu.make_async_copy(step[0], step[1], in_sem.at[i]) for i, step in enumerate(steps)
    ]
    for move in moves:
        move.start()
    results = []
    for i, (_, _, src, dst, at) in enumerate(steps):
        moves[i].wait()
        if at is not None:
            k, rows, to = at
            for n in range(6):
                half = slice(rows.start + n * CH, rows.start + n * CH + CH)
                into = slice(to.start + n // 2 * CH, to.start + (n // 2 + 1) * CH)
                lanes = slice(n % 2 * 128, n % 2 * 128 + 128)
                wide[into, lanes] = narrow[k, half, :].astype(F32) * (1.0 / 512.0)
        results.append(pltpu.make_async_copy(src, dst, out_sem.at[i]))
        results[i].start()
    for copy in results:
        copy.wait()


def on_device(
    obs_values, obs_cells, obs_subcell, slot_counts, sharpness, embed_weight, conv_weight, cotangent
):
    anywhere = pl.BlockSpec(memory_space=pl.ANY)
    vmem = pl.BlockSpec(memory_space=pltpu.VMEM)
    grid = (ROWS, COLS, CH)
    wide = (ROWS + 2, COLS, 3 * CH)
    dma = pltpu.SemaphoreType.DMA
    scratch = [
        pltpu.VMEM((64, 2, CAP, VALS), BF16),
        pltpu.VMEM((64, 2, CAP, VALS), BF16),
        pltpu.VMEM((64, 2, CAP, VALS), BF16),
        pltpu.VMEM((4, 32, 1, 128), F32),
        pltpu.VMEM((4, 4, 8, 1, 128), F32),
        pltpu.VMEM((4, 4, 4, 2, 1, 128), F32),
        pltpu.VMEM((8, 4, 4, 1, 128), F32),
        pltpu.VMEM((GROUP, 128), BF16),
        pltpu.VMEM((OBS, 128), BF16),
        pltpu.VMEM((OBS, 128), BF16),
        pltpu.VMEM((OBS, CH), F32),
        pltpu.VMEM((GROUP, CH), BF16),
        pltpu.VMEM((GROUP, 256), BF16),
        pltpu.VMEM((COLS, GROUP), BF16),
        pltpu.VMEM((16, GROUP), F32),
        pltpu.VMEM((CELLS, CH), F32),
        pltpu.VMEM((COLS, 256), F32),
        pltpu.VMEM(grid, F32),
        pltpu.VMEM(grid, BF16),
        pltpu.VMEM((2, 3, 3 * CH, CH), BF16),
        pltpu.VMEM((CH, VALS), BF16),
        pltpu.VMEM(grid, F32),
        pltpu.VMEM(grid, F32),
        pltpu.VMEM(grid, BF16),
        pltpu.VMEM(grid, BF16),
        pltpu.VMEM(grid, BF16),
        pltpu.VMEM(grid, BF16),
        pltpu.VMEM(grid, BF16),
        pltpu.VMEM((CELLS, CH), BF16),
        pltpu.VMEM((CH, CELLS), BF16),
        pltpu.VMEM((CH, CELLS), BF16),
        pltpu.VMEM(wide, BF16),
        pltpu.VMEM(wide, BF16),
        pltpu.VMEM(wide, BF16),
        pltpu.VMEM((4, 2 * COLS + 6 * 16, CH), BF16),
        pltpu.VMEM((4, 2, 16, CH), BF16),
        pltpu.VMEM((2, 16, CH), F32),
        pltpu.VMEM((64, 2, CAP, VALS), BF16),
        pltpu.VMEM((2, 3 * PART, 128), BF16),
        pltpu.VMEM((2, 3 * PART, 128), BF16),
        pltpu.VMEM((2, 3, HALF, 128), BF16),
        pltpu.VMEM((2, 3, HALF, 128), BF16),
        pltpu.VMEM((2, 3, 3, QUARTER, 128), BF16),
        pltpu.VMEM((2, 3, QUARTER, 128), BF16),
        pltpu.VMEM((2, 3, 3, SHARD, 128), BF16),
        pltpu.VMEM((2, 3, SHARD, 128), BF16),
        pltpu.VMEM((2, 3, 4, SHARD, 128), BF16),
        pltpu.VMEM((VALS, CH), F32),
        pltpu.VMEM((7, 16, CH), F32),
        pltpu.VMEM((16, 16, CH), F32),
        pltpu.VMEM((VALS, CH), F32),
        pltpu.VMEM(grid, BF16),
        dma((7,)),
        dma((2,)),
        dma((2,)),
        dma((4,)),
        dma((4,)),
        dma((3,)),
        dma((3,)),
        dma,
        dma,
        dma((4,)),
        dma((4,)),
        dma((2, 7)),
        dma((2, 7)),
        dma((3,)),
        dma((3,)),
    ]
    encoded, value_grads, grads, embed_total = pl.pallas_call(
        kernel,
        out_shape=(
            jax.ShapeDtypeStruct(grid, BF16),
            jax.ShapeDtypeStruct((64, 2, CAP, VALS), BF16),
            jax.ShapeDtypeStruct((2, 3 * PART, 128), BF16),
            jax.ShapeDtypeStruct((VALS, CH), F32),
        ),
        in_specs=[anywhere, vmem, vmem, vmem, vmem, vmem, anywhere, anywhere],
        out_specs=(anywhere, anywhere, anywhere, vmem),
        scratch_shapes=scratch,
        compiler_params=pltpu.CompilerParams(
            collective_id=0, has_side_effects=True, vmem_limit_bytes=60 * 1024 * 1024
        ),
        cost_estimate=pl.CostEstimate(
            flops=30_000_000_000, bytes_accessed=20_000_000, transcendentals=4_000_000
        ),
    )(
        obs_values.reshape(64, 2, CAP, VALS),
        obs_cells.reshape(32, 128),
        obs_subcell.reshape(32, 128),
        slot_counts,
        sharpness.reshape(1, CH),
        embed_weight,
        conv_weight.reshape(2, 3, 3 * CH, CH),
        cotangent,
    )
    encoded, value_grads, conv_grads, embed_grads = pl.pallas_call(
        hand_over,
        out_shape=(
            jax.ShapeDtypeStruct(grid, BF16),
            jax.ShapeDtypeStruct((64, 2, CAP, VALS), BF16),
            jax.ShapeDtypeStruct((3 * PART, CH), F32),
            jax.ShapeDtypeStruct((VALS, CH), F32),
        ),
        in_specs=[anywhere] * 4,
        out_specs=(anywhere,) * 4,
        scratch_shapes=[
            pltpu.VMEM(grid, BF16),
            pltpu.VMEM((64, 2, CAP, VALS), BF16),
            pltpu.VMEM((VALS, CH), F32),
            pltpu.VMEM((2, 3 * PART, 128), BF16),
            pltpu.VMEM((3 * PART, CH), F32),
            dma((9,)),
            dma((9,)),
        ],
        compiler_params=pltpu.CompilerParams(vmem_limit_bytes=60 * 1024 * 1024),
    )(encoded, value_grads, grads, embed_total)
    return (
        encoded,
        value_grads.reshape(OBS, VALS),
        conv_grads.reshape(2, 3, 3, CH, CH),
        embed_grads,
    )


def solution(mesh):
    placed = (
        P(("lat", "lon"), None),
        P(("lat", "lon")),
        P(("lat", "lon")),
        P(("lat", "lon"), None),
        P(),
        P(),
        P(),
        P("lat", "lon", None),
    )
    return jax.shard_map(
        on_device,
        mesh=mesh,
        in_specs=placed,
        out_specs=(P("lat", "lon", None), P(("lat", "lon"), None), P(), P()),
        check_vma=False,
    )
```

```python
import jax
import jax.numpy as jnp
from jax import lax
from jax.experimental import pallas as pl
from jax.experimental.pallas import tpu as pltpu
from jax.sharding import PartitionSpec as P

F32 = jnp.float32
BF16 = jnp.bfloat16
N_LAT, N_LON = 4, 32
DEVICES = N_LAT * N_LON
CAP, VALS, CH = 32, 128, 256
ROWS, COLS = 16, 128
CELLS = ROWS * COLS
OBS = DEVICES * CAP
GROUP = 32 * CAP
PART, HALF, QUARTER, SHARD = 1536, 768, 192, 48
NT = (((1,), (1,)), ((), ()))
TN = (((0,), (0,)), ((), ()))


def dot(a, b):
    return jnp.dot(a, b, preferred_element_type=F32)


def iota(shape, axis):
    return lax.broadcasted_iota(jnp.int32, shape, axis)


def sigmoid(x):
    return 0.5 + 0.5 * jnp.tanh(0.5 * x)


def remote(src, dst, send, recv, lat, lon):
    return pltpu.make_async_remote_copy(
        src_ref=src,
        dst_ref=dst,
        send_sem=send,
        recv_sem=recv,
        device_id=(lat, lon),
        device_id_type=pl.DeviceIdType.MESH,
    )


def await_bytes(ref, sem):
    pltpu.make_async_copy(ref, ref, sem).wait()


def loop(low, high, body):
    def step(i, carry):
        body(i)
        return carry

    lax.fori_loop(low, high, step, 0)


def aligned(start, size, unit):
    return pl.ds(pl.multiple_of(start, unit), size)


def kernel(
    obs_in, cells, subs, live_counts, sharp, embed_w, conv_in, cot_in,
    enc_out, vg_out, grads_out, embed_out,
    vals, queue, relay, meta_own, meta_z, meta_x, meta, tmeta, colb, rowb, weight, ew, rk, colhot, rowl, placed, counts, inv,
    cot, conv_w, embed_t, back, bend, base, act_zero, mid, act_one, gmid, gp, act_t, zero_t,
    x3_act, x3_cot, x3_mid, halo, strip, stripf,
    vg, grads, total, p0, s1, p1, s2, p2, s3, p3, esum, pe, qe, etotal, enc,
    local_sem, pair_send, pair_recv, a2a_send, a2a_recv, meta_send, meta_recv, vg_send, vg_recv,
    halo_send, halo_recv, ar_send, ar_recv, em_send, em_recv,
):
    lat = lax.axis_index("lat")
    lon = lax.axis_index("lon")
    me = lat * N_LON + lon
    xi, yi, ci = lax.div(lon, 8), lax.rem(lax.div(lon, 2), 4), lax.rem(lon, 2)

    chip = lat * 16 + xi * 4 + yi
    yc = lax.rem(lon, 8)
    other_core = lon + 1 - 2 * ci

    to_x = [xi] + [lax.rem(xi + d, 4) for d in range(1, 4)]
    to_y = [yi] + [lax.rem(yi + d, 4) for d in range(1, 4)]
    to_z = [lat] + [lax.rem(lat + d, 4) for d in range(1, 4)]

    def offset(j):
        dx, dy = j // 4 % 4, j % 4
        return dx, dy, (j // 16 + 8 - dx - dy) % 4

    def source(j):
        dx, dy, dz = offset(j)
        return to_x[-dx % 4], to_y[-dy % 4], to_z[-dz % 4]

    barrier = pltpu.get_barrier_semaphore()

    cot_copy = pltpu.make_async_copy(cot_in, cot, local_sem.at[0])
    cot_copy.start()
    pair_own = pltpu.make_async_copy(obs_in.at[:, ci], queue.at[:, ci], local_sem.at[4])
    pair_own.start()
    pair_other = remote(
        obs_in.at[:, 1 - ci], queue.at[:, ci], pair_send.at[0], pair_recv.at[0], lat, other_core
    )

    def signal(tlat, tlon):
        pl.semaphore_signal(
            barrier, inc=1, device_id=(tlat, tlon), device_id_type=pl.DeviceIdType.MESH
        )

    for j in range(1, 64):
        signal(to_z[j // 4 % 4], to_x[j // 16] * 8 + to_y[j % 4] * 2 + ci)
    beside = lax.rem(lon + N_LON - 1 + 2 * ci, N_LON)
    for turn in (0, 1, 3):
        signal(to_z[turn], other_core)
        signal(to_z[turn], beside)
    for d in range(1, 4):
        signal(lat, xi * 8 + to_y[d] * 2 + 1 - ci)

    def meta_copies(stage):
        copies = []
        for d in range(1, 8 if stage == 2 else 4):
            if stage == 0:
                c = lax.rem(lat + d, 4)
                src, dst, target = meta_own.at[:, pl.ds(c * 8, 8)], meta_z.at[lat], (c, lon)
            elif stage == 1:
                c = lax.rem(xi + d, 4)
                src, dst = meta_z.at[:, :, pl.ds(c * 2, 2)], meta_x.at[xi]
                target = (lat, c * 8 + yc)
            else:
                c = lax.rem(yc + d, 8)
                src, dst = meta_x.at[:, :, lax.rem(c, 4), lax.div(c, 4)], meta.at[yc]
                target = (lat, xi * 8 + c)
            copies.append(remote(src, dst, meta_send.at[stage], meta_recv.at[stage], *target))
        own = (
            (meta_own.at[:, pl.ds(lat * 8, 8)], meta_z.at[lat]),
            (meta_z.at[:, :, pl.ds(xi * 2, 2)], meta_x.at[xi]),
            (meta_x.at[:, :, lax.rem(yc, 4), lax.div(yc, 4)], meta.at[yc]),
        )[stage]
        copies.append(pltpu.make_async_copy(*own, meta_recv.at[stage]))
        return copies

    def meta_start(stage):
        for copy in meta_copies(stage):
            copy.start()

    def meta_wait(stage):
        await_bytes((meta_z, meta_x, meta)[stage], meta_recv.at[stage])

    def meta_sent(stage):
        await_bytes((meta_z, meta_x, meta)[stage].at[pl.ds(0, (3, 3, 7)[stage])], meta_send.at[stage])

    line, lane = iota((32, 128), 0), iota((32, 128), 1)
    own_four = jnp.where(lax.div(lane, 4) == line, live_counts[...].astype(F32), 0.0).astype(BF16)
    to_slots = jnp.where(
        lax.rem(iota((128, 128), 0), 4) == lax.div(iota((128, 128), 1), 32), 1.0, 0.0
    ).astype(BF16)
    live = lax.rem(lane, 32).astype(F32) < dot(own_four, to_slots)
    cell, sub = cells[...], subs[...]
    u, v = sub >> 3, sub & 7
    u = jnp.where(u >= 4, u - 4, 3 - u)
    v = jnp.where(v >= 4, v - 4, 3 - v)
    row = cell >> 7
    fields = [
        jnp.where(live, (cell & 127).astype(F32), 255.0),
        (row * 16 + u * 4 + v).astype(F32),
        ((2 * u + 1) * (2 * u + 1) + (2 * v + 1) * (2 * v + 1)).astype(F32),
        row.astype(F32),
    ]
    for i in range(4):
        mixed = jnp.zeros((32, 128), F32)
        for f in range(4):
            shift = (f - i) * 32 % 128
            turned_field = pltpu.roll(fields[f], shift, 1) if shift else fields[f]
            mixed = jnp.where(lax.div(lane, 32) == f, turned_field, mixed)
        for r in range(32):
            meta_own[i, r] = mixed[r : r + 1, :]

    conv_copy = pltpu.make_async_copy(conv_in, conv_w, local_sem.at[1])
    conv_copy.start()

    def send_slot(j):
        dx, dy, dz = offset(j)
        tx, ty, tz = to_x[dx], to_y[dy], to_z[dz]
        g = j // 16
        remote(
            queue.at[tz * 16 + tx * 4 + ty], vals.at[j], a2a_send.at[g], a2a_recv.at[g],
            tz, tx * 8 + ty * 2 + ci,
        ).start()

    north, south = lax.rem(lat + 3, N_LAT), lax.rem(lat + 1, N_LAT)
    west, east = lax.rem(lon + N_LON - 1, N_LON), lax.rem(lon + 1, N_LON)

    def halo_row(k, side):
        return halo.at[k, side * COLS : (side + 1) * COLS]

    def halo_col(k, side, turn):
        at = 2 * COLS + 16 * (3 * side + turn)
        return halo.at[k, at : at + 16]

    def halo_copies(src, k):
        pieces = [(src.at[ROWS - 1], halo_row(k, 0), south, lon)]
        pieces.append((src.at[0], halo_row(k, 1), north, lon))
        for side, column, target in ((0, 1, east), (1, 0, west)):
            for turn, tlat in enumerate((lat, south, north)):
                pieces.append((strip.at[k, column], halo_col(k, side, turn), tlat, target))
        return [remote(s, d, halo_send.at[k], halo_recv.at[k], a, b) for s, d, a, b in pieces]

    def halo_pack(src, k):
        for r in range(ROWS):
            stripf[0, r : r + 1, :] = src[r, 0:16, :].astype(F32)[0:1, :]
            stripf[1, r : r + 1, :] = src[r, COLS - 16 : COLS, :].astype(F32)[15:16, :]
        strip[k, 0] = stripf[0].astype(BF16)
        strip[k, 1] = stripf[1].astype(BF16)

    def halo_start(src, k):
        for copy in halo_copies(src, k):
            copy.start()

    def widen(src, x3, low=0, high=4):
        def body(b):
            for i in range(4):
                r = 4 * b + i
                row = src[r].astype(F32)
                x3[r + 1, :, 0:CH] = pltpu.roll(row, 1, 0).astype(BF16)
                x3[r + 1, :, CH : 2 * CH] = src[r]
                x3[r + 1, :, 2 * CH : 3 * CH] = pltpu.roll(row, COLS - 1, 0).astype(BF16)

        loop(low, high, body)

    def halo_finish(src, k, x3):
        await_bytes(halo.at[k], halo_recv.at[k])
        await_bytes(halo.at[k], halo_send.at[k])
        first = iota((16, CH), 0) == 0
        last = iota((16, CH), 0) == 15
        left = halo_col(k, 0, 0)[...].astype(F32)
        right = halo_col(k, 1, 0)[...].astype(F32)
        for r in range(ROWS):
            low = x3[r + 1, 0:16, 0:CH].astype(F32)
            x3[r + 1, 0:16, 0:CH] = jnp.where(first, left[r : r + 1, :], low).astype(BF16)
            high = x3[r + 1, COLS - 16 : COLS, 2 * CH : 3 * CH].astype(F32)
            x3[r + 1, COLS - 16 : COLS, 2 * CH : 3 * CH] = jnp.where(
                last, right[r : r + 1, :], high
            ).astype(BF16)
        spot = iota((COLS, CH), 0)
        for side, r, turn, pick, valid in (
            (0, 0, 1, ROWS - 1, lat > 0),
            (1, ROWS + 1, 2, 0, lat < N_LAT - 1),
        ):
            keep = jnp.where(valid, 1.0, 0.0).astype(F32)
            row = halo_row(k, side)[...].astype(F32) * keep
            lcorner = halo_col(k, 0, turn)[...].astype(F32)[pick : pick + 1, :] * keep
            rcorner = halo_col(k, 1, turn)[...].astype(F32)[pick : pick + 1, :] * keep
            x3[r, :, 0:CH] = jnp.where(spot == 0, lcorner, pltpu.roll(row, 1, 0)).astype(BF16)
            x3[r, :, CH : 2 * CH] = row.astype(BF16)
            x3[r, :, 2 * CH : 3 * CH] = jnp.where(
                spot == COLS - 1, rcorner, pltpu.roll(row, COLS - 1, 0)
            ).astype(BF16)

    def conv(x3, k, finish, flip=False, low=0, high=4):
        if flip:
            taps = [
                conv_w[k, 2 - p, (2 - q) * CH : (3 - q) * CH, :] for p in range(3) for q in range(3)
            ]
            taps = jnp.concatenate(taps, axis=1)
        else:
            taps = conv_w[k].reshape(9 * CH, CH)
        for b in range(low, high):
            near = [x3[4 * b + p : 4 * b + p + 4].reshape(4 * COLS, 3 * CH) for p in range(3)]
            near = jnp.concatenate(near, axis=1)
            if flip:
                acc = lax.dot_general(near, taps, NT, preferred_element_type=F32)
            else:
                acc = dot(near, taps)
            finish(slice(4 * b, 4 * b + 4), acc)

    def tile4(x):
        return x.reshape(4 * COLS, CH)

    def grid4(x):
        return x.reshape(4, COLS, CH)

    def turn_act(act, act_t):
        for r in range(ROWS):
            act_t[:, r * COLS : (r + 1) * COLS] = act[r].T

    cot_copy.wait()
    halo_pack(cot, 0)
    pl.semaphore_wait(barrier, 72)
    pair_other.start()
    meta_start(0)
    halo_start(cot, 0)
    widen(cot, x3_cot, 0, 2)
    meta_wait(0)
    meta_start(1)
    widen(cot, x3_cot, 2, 4)
    meta_wait(1)
    meta_start(2)
    pair_own.wait()
    pair_other.wait()
    pltpu.make_async_copy(queue.at[chip], vals.at[0], a2a_recv.at[0]).start()
    for j in range(1, 16):
        send_slot(j)
    conv_copy.wait()
    embed_t[...] = embed_w[...].T
    halo_finish(cot, 0, x3_cot)

    def keep_back(rows, acc):
        back[rows] = grid4(acc)

    for g in range(1, 4):
        for j in range(16 * g, 16 * g + 16):
            send_slot(j)
        conv(x3_cot, 1, keep_back, flip=True, low=g - 1, high=4 if g == 3 else g)
    meta_wait(2)

    placed[...] = jnp.zeros_like(placed)
    counts[...] = jnp.zeros_like(counts)
    slot_mask = jnp.where(
        lax.rem(iota((CAP, 128), 1), 32) == iota((CAP, 128), 0), 1.0, 0.0
    ).astype(F32)
    spread = jnp.where(
        lax.div(iota((128, 512), 0), 32) == lax.div(iota((128, 512), 1), 128), 1.0, 0.0
    ).astype(BF16)
    lane, line = iota((COLS + 16, 128), 1), iota((COLS + 16, 128), 0)
    pick = jnp.where(lax.div(lane, 32) == jnp.where(line < COLS, 0, 3), 1.0, 0.0).astype(BF16)
    decay = sharp[...] * (-1.0 / 256.0)

    for g in range(4):
        for s in range(32):
            sx, sy, sz = source(g * 16 + s // 2)
            line = jnp.broadcast_to(meta[sy * 2 + s % 2, sx, sz], (CAP, 128)) * slot_mask
            tmeta[s * CAP : s * CAP + CAP, :] = line.astype(BF16)
        await_bytes(vals.at[pl.ds(g * 16, 16)], a2a_recv.at[g])

        for b in range(4):
            at = slice(b * 256, b * 256 + 256)
            of = slice(g * GROUP + b * 256, g * GROUP + b * 256 + 256)
            wide = dot(tmeta[at, :], spread)
            colb[of, :] = wide[:, 0:128].astype(BF16)
            rowb[of, :] = wide[:, 384:512].astype(BF16)
            rk_of = jnp.concatenate([wide[:, 128:256]] * 2, axis=1)
            radius = jnp.concatenate([wide[:, 256:384]] * 2, axis=1)
            rk[at, :] = jnp.where(
                rk_of == iota((256, 256), 1).astype(F32), 1.0, 0.0
            ).astype(BF16)
            w = jnp.exp(radius * decay)
            weight[of, :] = w
            ew[at, :] = (dot(vals[g * 16 + 4 * b : g * 16 + 4 * b + 4].reshape(256, VALS), embed_w[...]) * w).astype(BF16)

        both = lax.dot_general(pick, tmeta[...], NT, preferred_element_type=F32)
        colhot[...] = jnp.where(
            both[0:COLS] == iota((COLS, GROUP), 0).astype(F32), 1.0, 0.0
        ).astype(BF16)
        rowl[...] = both[COLS : COLS + 16]
        counts[...] += dot(colhot[...], rk[...])

        hot = colhot[...].reshape(8, 16, GROUP)
        for b in range(4):
            rows = []
            for r in range(4 * b, 4 * b + 4):
                mask = jnp.where(rowl[...] == float(r), 1.0, 0.0).astype(BF16)
                rows.append((hot * mask[None]).reshape(COLS, GROUP))
            at = slice(b * 512, b * 512 + 512)
            placed[at, :] += dot(jnp.concatenate(rows, axis=0), ew[...])

    kind = lax.rem(iota((256, CH), 0), 16)
    half_u, half_v = 2 * lax.div(kind, 4) + 1, 2 * lax.rem(kind, 4) + 1
    table = jnp.exp((half_u * half_u + half_v * half_v).astype(F32) * decay)
    table_hi = table.astype(BF16)
    table_lo = (table - table_hi.astype(F32)).astype(BF16)
    tables = jnp.concatenate([table_hi, table_lo], axis=0)
    row_of_lane = lax.div(iota((COLS, 256), 1), 16)
    for b in range(4):
        rows = []
        for r in range(4 * b, 4 * b + 4):
            rows.append(jnp.where(row_of_lane == r, counts[...], 0.0).astype(BF16))
        tally = jnp.concatenate(rows, axis=0)
        recip = 1.0 / (dot(jnp.concatenate([tally, tally], axis=1), tables) + 1.0)
        at = slice(4 * b, 4 * b + 4)
        inv[at] = grid4(recip)
        value = (placed[b * 512 : b * 512 + 512, :] * recip).astype(BF16)
        base[at] = grid4(value)
        x = value.astype(F32)
        s = sigmoid(x)
        act_zero[at] = grid4((x * s).astype(BF16))
        bend[at] = grid4(s * (1.0 + x * (1.0 - s)))

    halo_pack(act_zero, 1)
    halo_start(act_zero, 1)
    widen(act_zero, x3_act)
    turn_act(act_zero, zero_t)
    halo_finish(act_zero, 1, x3_act)

    def keep_mid(rows, acc):
        value = (tile4(base[rows]).astype(F32) + acc).astype(BF16)
        mid[rows] = grid4(value)
        x = value.astype(F32)
        s = sigmoid(x)
        act_one[rows] = grid4((x * s).astype(BF16))
        slope = s * (1.0 + x * (1.0 - s))
        grad = tile4(cot[rows]).astype(F32) + tile4(back[rows]) * slope
        gmid[rows] = grid4(grad.astype(BF16))

    conv(x3_act, 0, keep_mid)
    halo_pack(gmid, 2)
    halo_start(gmid, 2)
    halo_pack(act_one, 3)
    halo_start(act_one, 3)

    def kernel_grad(act_t, x3, k):
        for p in range(3):
            block = dot(act_t[...], x3[2 - p : 2 - p + ROWS].reshape(CELLS, 3 * CH))
            for q in range(3):
                for h in range(2):
                    n, lanes = 6 * p + 2 * q + h, (2 - q) * CH + h * 128
                    at = n % 3 * CH
                    grads[k, n // 6, n // 3 % 2, at : at + CH, :] = block[
                        :, lanes : lanes + 128
                    ].astype(BF16)

    coords = {"x": xi, "y": yi, "z": lat}
    orders = (("x", "y", "z"), ("y", "z", "x"), ("z", "x", "y"))

    def along(axis, c):
        cx, cy, cz = [c if axis == n else coords[n] for n in ("x", "y", "z")]
        return cz, cx * 8 + cy * 2 + ci

    def turned(axis, d):
        return {"x": to_x, "y": to_y, "z": to_z}[axis][d]

    def part_copies(k, stage):
        sems = (ar_send.at[k, stage], ar_recv.at[k, stage])
        if stage == 0:
            return [remote(grads.at[k, :, 1 - ci], p0.at[k], *sems, lat, other_core)]
        if stage == 6:
            half = total.at[k, :, ci]
            return [remote(half, half, *sems, lat, other_core)]
        copies = []
        for a, order in enumerate(orders):
            quarter = coords[order[0]] * QUARTER
            shard = quarter + coords[order[1]] * SHARD
            axis = order[{1: 0, 2: 1, 3: 2, 4: 1, 5: 0}[stage]]
            for d in (1, 3, 2):
                c = turned(axis, d)
                if stage == 1:
                    src, dst = s1.at[k, a, aligned(c * QUARTER, QUARTER, 16)], p1.at[k, a, d - 1]
                elif stage == 2:
                    src, dst = s2.at[k, a, aligned(c * SHARD, SHARD, 16)], p2.at[k, a, d - 1]
                elif stage == 3:
                    src, dst = s3.at[k, a], p3.at[k, a, coords[axis]]
                elif stage == 4:
                    src = dst = total.at[k, a, ci, aligned(shard, SHARD, 16)]
                else:
                    src = dst = total.at[k, a, ci, aligned(quarter, QUARTER, 16)]
                copies.append(remote(src, dst, *sems, *along(axis, c)))
        return copies

    def ar_start(k, stage):
        for copy in part_copies(k, stage):
            copy.start()

    def ar_finish(k, stage):
        amount = (p0, p1, p2, p2, p2, p1, p0)[stage].at[k]
        await_bytes(amount, ar_recv.at[k, stage])
        await_bytes(amount, ar_send.at[k, stage])
        for a, order in enumerate(orders):
            if stage == 0:
                here = grads[k, a, ci].astype(F32)
                s1[k, a] = (here + p0[k, a].astype(F32)).astype(BF16)
            elif stage in (1, 2):
                size = QUARTER if stage == 1 else SHARD
                src, came, dst = (s1, p1, s2) if stage == 1 else (s2, p2, s3)
                at = aligned(coords[order[stage - 1]] * size, size, 16)
                here = src[k, a, at, :].astype(F32)
                for d in range(3):
                    here += came[k, a, d].astype(F32)
                dst[k, a] = here.astype(BF16)
            elif stage == 3:
                p3[k, a, coords[order[2]]] = s3[k, a]
                whole = p3[k, a, 0].astype(F32)
                for d in range(1, 4):
                    whole += p3[k, a, d].astype(F32)
                quarter = coords[order[0]] * QUARTER
                at = aligned(quarter + coords[order[1]] * SHARD, SHARD, 16)
                total[k, a, ci, at, :] = whole.astype(BF16)

    def ar_step(k, stage):
        ar_finish(k, stage)
        ar_start(k, stage + 1)

    def ar_leave(k):
        return pltpu.make_async_copy(total.at[k], grads_out.at[k], local_sem.at[3 if k else 6])

    turn_act(act_one, act_t)
    kernel_grad(act_t, x3_cot, 1)
    ar_start(1, 0)
    widen(gmid, x3_mid)
    halo_finish(gmid, 2, x3_mid)
    ar_step(1, 0)
    kernel_grad(zero_t, x3_mid, 0)
    ar_start(0, 0)

    def keep_gp(rows, acc):
        grad = tile4(gmid[rows]).astype(F32) + acc * tile4(bend[rows])
        gp[rows.start * COLS : rows.stop * COLS, :] = (
            grad * tile4(inv[rows])
        ).astype(BF16)

    conv(x3_mid, 0, keep_gp, flip=True, low=0, high=2)
    ar_step(1, 1)
    ar_step(0, 0)
    conv(x3_mid, 0, keep_gp, flip=True, low=2, high=4)

    esum[...] = jnp.zeros_like(esum)

    def vg_copy(j):
        sx, sy, sz = source(j)
        return remote(vg.at[j], relay.at[chip], vg_send, vg_recv, sz, sx * 8 + sy * 2 + ci)

    def gather(b):
        at = slice(b * 512, b * 512 + 512)
        chips = slice(b * 8, b * 8 + 8)
        hot = jnp.where(
            colb[at, :].astype(F32) == iota((512, COLS), 1).astype(F32), 1.0, 0.0
        ).astype(BF16)
        row_of = rowb[at, :]
        pieces = [
            jnp.where(row_of == jnp.array(r, BF16), hot, jnp.zeros_like(hot)) for r in range(ROWS)
        ]
        found = dot(jnp.concatenate(pieces, axis=1), gp[...])
        grad = (found * weight[at, :]).astype(BF16)
        vg[chips] = dot(grad, embed_t[...]).astype(BF16).reshape(8, 2, CAP, VALS)
        own = vals[chips].reshape(512, VALS)
        esum[...] += lax.dot_general(own, grad, TN, preferred_element_type=F32)
        for j in range(8 * b, 8 * b + 8):
            if j == 0:
                pltpu.make_async_copy(vg.at[0], relay.at[chip], vg_recv).start()
            else:
                vg_copy(j).start()

    gather(0)
    gather(1)
    ar_step(1, 2)
    gather(2)
    ar_step(0, 1)
    gather(3)
    ar_step(1, 3)
    gather(4)
    ar_step(0, 2)
    gather(5)
    ar_step(1, 4)
    gather(6)
    ar_step(0, 3)
    gather(7)
    ar_step(0, 4)

    member = yc
    column = xi * 4 + lat

    def embed_copies(stage):
        copies = []
        for d in range(1, 16 if stage == 1 else 8):
            if stage == 1:
                c = lax.rem(column + d, 16)
                tlat, tlon = lax.rem(c, 4), lax.div(c, 4) * 8 + member
                src, dst = esum.at[aligned(member * 16, 16, 16)], qe.at[column]
            else:
                m = lax.rem(member + d, 8)
                tlat, tlon = lat, xi * 8 + m
                if stage == 0:
                    src, dst = esum.at[aligned(m * 16, 16, 16)], pe.at[d - 1]
                else:
                    src = dst = etotal.at[aligned(member * 16, 16, 16)]
            copies.append(remote(src, dst, em_send.at[stage], em_recv.at[stage], tlat, tlon))
        return copies

    def embed_start(stage):
        for copy in embed_copies(stage):
            copy.start()

    def embed_wait(stage):
        amount = qe.at[pl.ds(0, 15)] if stage == 1 else pe
        await_bytes(amount, em_recv.at[stage])
        await_bytes(amount, em_send.at[stage])

    embed_start(0)
    widen(act_one, x3_act)
    halo_finish(act_one, 3, x3_act)

    def keep_enc(rows, acc):
        enc[rows] = grid4((tile4(mid[rows]).astype(F32) + acc).astype(BF16))

    conv(x3_act, 1, keep_enc, low=0, high=1)
    ar_step(1, 5)
    embed_wait(0)
    own_rows = aligned(member * 16, 16, 16)
    mine = esum[own_rows, :]
    for d in range(7):
        mine += pe[d]
    esum[own_rows, :] = mine
    embed_start(1)
    conv(x3_act, 1, keep_enc, low=1, high=2)
    ar_step(0, 5)
    conv(x3_act, 1, keep_enc, low=2, high=3)
    ar_finish(1, 6)
    ar_leave(1).start()
    embed_wait(1)
    qe[column] = esum[own_rows, :]
    whole = qe[0]
    for d in range(1, 16):
        whole += qe[d]
    etotal[own_rows, :] = whole
    embed_start(2)
    await_bytes(relay, vg_recv)
    vg_own = pltpu.make_async_copy(relay.at[:, ci], vg_out.at[:, ci], local_sem.at[5])
    vg_own.start()
    vg_other = remote(
        relay.at[:, 1 - ci], vg_out.at[:, ci], pair_send.at[1], pair_recv.at[1], lat, other_core
    )
    vg_other.start()
    conv(x3_act, 1, keep_enc, low=3, high=4)
    enc_copy = pltpu.make_async_copy(enc, enc_out, local_sem.at[2])
    enc_copy.start()
    ar_finish(0, 6)
    ar_leave(0).start()
    embed_wait(2)
    embed_out[...] = etotal[...] * (1.0 / 512.0)
    for g in range(4):
        await_bytes(vals.at[pl.ds(0, 15 if g == 0 else 16)], a2a_send.at[g])
    for stage in range(3):
        meta_sent(stage)
    await_bytes(vg.at[pl.ds(0, 63)], vg_send)
    vg_own.wait()
    vg_other.wait()
    enc_copy.wait()
    ar_leave(1).wait()
    ar_leave(0).wait()


def hand_over(
    enc_in, vg_in, grads_in, embed_in, enc_out, vg_out, grads_out, embed_out,
    enc, vg, embed, narrow, wide, in_sem, out_sem,
):
    steps = []
    for i in range(6):
        src, dst = slice(i % 3 * PART, (i % 3 + 1) * PART), slice(i * 3 * CH, (i + 1) * 3 * CH)
        k = i // 3
        steps.append(
            (grads_in.at[k, src], narrow.at[k, src], wide.at[dst], grads_out.at[dst], (k, src, dst))
        )
    steps.append((enc_in, enc, enc, enc_out, None))
    steps.append((vg_in, vg, vg, vg_out, None))
    steps.append((embed_in, embed, embed, embed_out, None))
    moves = [
        pltpu.make_async_copy(step[0], step[1], in_sem.at[i]) for i, step in enumerate(steps)
    ]
    for move in moves:
        move.start()
    results = []
    for i, (_, _, src, dst, at) in enumerate(steps):
        moves[i].wait()
        if at is not None:
            k, rows, to = at
            for n in range(6):
                half = slice(rows.start + n * CH, rows.start + n * CH + CH)
                into = slice(to.start + n // 2 * CH, to.start + (n // 2 + 1) * CH)
                lanes = slice(n % 2 * 128, n % 2 * 128 + 128)
                wide[into, lanes] = narrow[k, half, :].astype(F32) * (1.0 / 512.0)
        results.append(pltpu.make_async_copy(src, dst, out_sem.at[i]))
        results[i].start()
    for copy in results:
        copy.wait()


def on_device(
    obs_values, obs_cells, obs_subcell, slot_counts, sharpness, embed_weight, conv_weight, cotangent
):
    anywhere = pl.BlockSpec(memory_space=pl.ANY)
    vmem = pl.BlockSpec(memory_space=pltpu.VMEM)
    grid = (ROWS, COLS, CH)
    wide = (ROWS + 2, COLS, 3 * CH)
    dma = pltpu.SemaphoreType.DMA
    scratch = [
        pltpu.VMEM((64, 2, CAP, VALS), BF16),
        pltpu.VMEM((64, 2, CAP, VALS), BF16),
        pltpu.VMEM((64, 2, CAP, VALS), BF16),
        pltpu.VMEM((4, 32, 1, 128), F32),
        pltpu.VMEM((4, 4, 8, 1, 128), F32),
        pltpu.VMEM((4, 4, 4, 2, 1, 128), F32),
        pltpu.VMEM((8, 4, 4, 1, 128), F32),
        pltpu.VMEM((GROUP, 128), BF16),
        pltpu.VMEM((OBS, 128), BF16),
        pltpu.VMEM((OBS, 128), BF16),
        pltpu.VMEM((OBS, CH), F32),
        pltpu.VMEM((GROUP, CH), BF16),
        pltpu.VMEM((GROUP, 256), BF16),
        pltpu.VMEM((COLS, GROUP), BF16),
        pltpu.VMEM((16, GROUP), F32),
        pltpu.VMEM((CELLS, CH), F32),
        pltpu.VMEM((COLS, 256), F32),
        pltpu.VMEM(grid, F32),
        pltpu.VMEM(grid, BF16),
        pltpu.VMEM((2, 3, 3 * CH, CH), BF16),
        pltpu.VMEM((CH, VALS), BF16),
        pltpu.VMEM(grid, F32),
        pltpu.VMEM(grid, F32),
        pltpu.VMEM(grid, BF16),
        pltpu.VMEM(grid, BF16),
        pltpu.VMEM(grid, BF16),
        pltpu.VMEM(grid, BF16),
        pltpu.VMEM(grid, BF16),
        pltpu.VMEM((CELLS, CH), BF16),
        pltpu.VMEM((CH, CELLS), BF16),
        pltpu.VMEM((CH, CELLS), BF16),
        pltpu.VMEM(wide, BF16),
        pltpu.VMEM(wide, BF16),
        pltpu.VMEM(wide, BF16),
        pltpu.VMEM((4, 2 * COLS + 6 * 16, CH), BF16),
        pltpu.VMEM((4, 2, 16, CH), BF16),
        pltpu.VMEM((2, 16, CH), F32),
        pltpu.VMEM((64, 2, CAP, VALS), BF16),
        pltpu.VMEM((2, 3, 2, HALF, 128), BF16),
        pltpu.VMEM((2, 3, 2, HALF, 128), BF16),
        pltpu.VMEM((2, 3, HALF, 128), BF16),
        pltpu.VMEM((2, 3, HALF, 128), BF16),
        pltpu.VMEM((2, 3, 3, QUARTER, 128), BF16),
        pltpu.VMEM((2, 3, QUARTER, 128), BF16),
        pltpu.VMEM((2, 3, 3, SHARD, 128), BF16),
        pltpu.VMEM((2, 3, SHARD, 128), BF16),
        pltpu.VMEM((2, 3, 4, SHARD, 128), BF16),
        pltpu.VMEM((VALS, CH), F32),
        pltpu.VMEM((7, 16, CH), F32),
        pltpu.VMEM((16, 16, CH), F32),
        pltpu.VMEM((VALS, CH), F32),
        pltpu.VMEM(grid, BF16),
        dma((7,)),
        dma((2,)),
        dma((2,)),
        dma((4,)),
        dma((4,)),
        dma((3,)),
        dma((3,)),
        dma,
        dma,
        dma((4,)),
        dma((4,)),
        dma((2, 7)),
        dma((2, 7)),
        dma((3,)),
        dma((3,)),
    ]
    encoded, value_grads, grads, embed_total = pl.pallas_call(
        kernel,
        out_shape=(
            jax.ShapeDtypeStruct(grid, BF16),
            jax.ShapeDtypeStruct((64, 2, CAP, VALS), BF16),
            jax.ShapeDtypeStruct((2, 3, 2, HALF, 128), BF16),
            jax.ShapeDtypeStruct((VALS, CH), F32),
        ),
        in_specs=[anywhere, vmem, vmem, vmem, vmem, vmem, anywhere, anywhere],
        out_specs=(anywhere, anywhere, anywhere, vmem),
        scratch_shapes=scratch,
        compiler_params=pltpu.CompilerParams(
            collective_id=0, has_side_effects=True, vmem_limit_bytes=60 * 1024 * 1024
        ),
        cost_estimate=pl.CostEstimate(
            flops=30_000_000_000, bytes_accessed=20_000_000, transcendentals=4_000_000
        ),
    )(
        obs_values.reshape(64, 2, CAP, VALS),
        obs_cells.reshape(32, 128),
        obs_subcell.reshape(32, 128),
        slot_counts,
        sharpness.reshape(1, CH),
        embed_weight,
        conv_weight.reshape(2, 3, 3 * CH, CH),
        cotangent,
    )
    encoded, value_grads, conv_grads, embed_grads = pl.pallas_call(
        hand_over,
        out_shape=(
            jax.ShapeDtypeStruct(grid, BF16),
            jax.ShapeDtypeStruct((64, 2, CAP, VALS), BF16),
            jax.ShapeDtypeStruct((3 * PART, CH), F32),
            jax.ShapeDtypeStruct((VALS, CH), F32),
        ),
        in_specs=[anywhere] * 4,
        out_specs=(anywhere,) * 4,
        scratch_shapes=[
            pltpu.VMEM(grid, BF16),
            pltpu.VMEM((64, 2, CAP, VALS), BF16),
            pltpu.VMEM((VALS, CH), F32),
            pltpu.VMEM((2, 3 * PART, 128), BF16),
            pltpu.VMEM((3 * PART, CH), F32),
            dma((9,)),
            dma((9,)),
        ],
        compiler_params=pltpu.CompilerParams(vmem_limit_bytes=60 * 1024 * 1024),
    )(encoded, value_grads, grads.reshape(2, 3 * PART, 128), embed_total)
    return (
        encoded,
        value_grads.reshape(OBS, VALS),
        conv_grads.reshape(2, 3, 3, CH, CH),
        embed_grads,
    )


def solution(mesh):
    placed = (
        P(("lat", "lon"), None),
        P(("lat", "lon")),
        P(("lat", "lon")),
        P(("lat", "lon"), None),
        P(),
        P(),
        P(),
        P("lat", "lon", None),
    )
    return jax.shard_map(
        on_device,
        mesh=mesh,
        in_specs=placed,
        out_specs=(P("lat", "lon", None), P(("lat", "lon"), None), P(), P()),
        check_vma=False,
    )
```

```python
import jax
import jax.numpy as jnp
from jax import lax
from jax.experimental import pallas as pl
from jax.experimental.pallas import tpu as pltpu
from jax.sharding import PartitionSpec as P

F32 = jnp.float32
BF16 = jnp.bfloat16
N_LAT, N_LON = 4, 32
DEVICES = N_LAT * N_LON
CAP, VALS, CH = 32, 128, 256
ROWS, COLS = 16, 128
CELLS = ROWS * COLS
OBS = DEVICES * CAP
GROUP = 32 * CAP
PART, HALF, QUARTER, SHARD = 1536, 768, 192, 48
NT = (((1,), (1,)), ((), ()))
TN = (((0,), (0,)), ((), ()))


def dot(a, b):
    return jnp.dot(a, b, preferred_element_type=F32)


def iota(shape, axis):
    return lax.broadcasted_iota(jnp.int32, shape, axis)


def sigmoid(x):
    return 0.5 + 0.5 * jnp.tanh(0.5 * x)


def remote(src, dst, send, recv, lat, lon):
    return pltpu.make_async_remote_copy(
        src_ref=src,
        dst_ref=dst,
        send_sem=send,
        recv_sem=recv,
        device_id=(lat, lon),
        device_id_type=pl.DeviceIdType.MESH,
    )


def await_bytes(ref, sem):
    pltpu.make_async_copy(ref, ref, sem).wait()


def loop(low, high, body):
    def step(i, carry):
        body(i)
        return carry

    lax.fori_loop(low, high, step, 0)


def aligned(start, size, unit):
    return pl.ds(pl.multiple_of(start, unit), size)


def kernel(
    obs_in, cells, subs, live_counts, sharp, embed_w, conv_in, cot_in,
    enc_out, vg_out, grads_out, embed_out,
    vals, queue, relay, meta_own, meta_z, meta_x, meta, tmeta, colb, rowb, weight, ew, rk, colhot, rowl, placed, counts, inv,
    cot, conv_w, embed_t, back, bend, base, act_zero, mid, act_one, gmid, gp, act_t, zero_t,
    x3_act, x3_cot, x3_mid, halo, strip, stripf,
    vg, grads, total, p0, s1, p1, s2, p2, s3, p3, esum, pe, qe, etotal, enc,
    local_sem, pair_send, pair_recv, a2a_send, a2a_recv, meta_send, meta_recv, vg_send, vg_recv,
    halo_send, halo_recv, ar_send, ar_recv, em_send, em_recv,
):
    lat = lax.axis_index("lat")
    lon = lax.axis_index("lon")
    me = lat * N_LON + lon
    xi, yi, ci = lax.div(lon, 8), lax.rem(lax.div(lon, 2), 4), lax.rem(lon, 2)

    chip = lat * 16 + xi * 4 + yi
    yc = lax.rem(lon, 8)
    other_core = lon + 1 - 2 * ci

    to_x = [xi] + [lax.rem(xi + d, 4) for d in range(1, 4)]
    to_y = [yi] + [lax.rem(yi + d, 4) for d in range(1, 4)]
    to_z = [lat] + [lax.rem(lat + d, 4) for d in range(1, 4)]

    def offset(j):
        dx, dy = j // 4 % 4, j % 4
        return dx, dy, (j // 16 + 8 - dx - dy) % 4

    def source(j):
        dx, dy, dz = offset(j)
        return to_x[-dx % 4], to_y[-dy % 4], to_z[-dz % 4]

    barrier = pltpu.get_barrier_semaphore()

    cot_copy = pltpu.make_async_copy(cot_in, cot, local_sem.at[0])
    cot_copy.start()
    pair_own = pltpu.make_async_copy(obs_in.at[:, ci], queue.at[:, ci], local_sem.at[4])
    pair_own.start()
    pair_other = remote(
        obs_in.at[:, 1 - ci], queue.at[:, ci], pair_send.at[0], pair_recv.at[0], lat, other_core
    )

    def signal(tlat, tlon):
        pl.semaphore_signal(
            barrier, inc=1, device_id=(tlat, tlon), device_id_type=pl.DeviceIdType.MESH
        )

    for j in range(1, 64):
        signal(to_z[j // 4 % 4], to_x[j // 16] * 8 + to_y[j % 4] * 2 + ci)
    beside = lax.rem(lon + N_LON - 1 + 2 * ci, N_LON)
    for turn in (0, 1, 3):
        signal(to_z[turn], other_core)
        signal(to_z[turn], beside)
    for d in range(1, 4):
        signal(lat, xi * 8 + to_y[d] * 2 + 1 - ci)

    def meta_copies(stage):
        copies = []
        for d in range(1, 8 if stage == 2 else 4):
            if stage == 0:
                c = lax.rem(lat + d, 4)
                src, dst, target = meta_own.at[:, pl.ds(c * 8, 8)], meta_z.at[lat], (c, lon)
            elif stage == 1:
                c = lax.rem(xi + d, 4)
                src, dst = meta_z.at[:, :, pl.ds(c * 2, 2)], meta_x.at[xi]
                target = (lat, c * 8 + yc)
            else:
                c = lax.rem(yc + d, 8)
                src, dst = meta_x.at[:, :, lax.rem(c, 4), lax.div(c, 4)], meta.at[yc]
                target = (lat, xi * 8 + c)
            copies.append(remote(src, dst, meta_send.at[stage], meta_recv.at[stage], *target))
        own = (
            (meta_own.at[:, pl.ds(lat * 8, 8)], meta_z.at[lat]),
            (meta_z.at[:, :, pl.ds(xi * 2, 2)], meta_x.at[xi]),
            (meta_x.at[:, :, lax.rem(yc, 4), lax.div(yc, 4)], meta.at[yc]),
        )[stage]
        copies.append(pltpu.make_async_copy(*own, meta_recv.at[stage]))
        return copies

    def meta_start(stage):
        for copy in meta_copies(stage):
            copy.start()

    def meta_wait(stage):
        await_bytes((meta_z, meta_x, meta)[stage], meta_recv.at[stage])

    def meta_sent(stage):
        await_bytes((meta_z, meta_x, meta)[stage].at[pl.ds(0, (3, 3, 7)[stage])], meta_send.at[stage])

    conv_copy = pltpu.make_async_copy(conv_in, conv_w, local_sem.at[1])
    conv_copy.start()

    def send_slot(j):
        dx, dy, dz = offset(j)
        tx, ty, tz = to_x[dx], to_y[dy], to_z[dz]
        g = j // 16
        remote(
            queue.at[tz * 16 + tx * 4 + ty], vals.at[j], a2a_send.at[g], a2a_recv.at[g],
            tz, tx * 8 + ty * 2 + ci,
        ).start()

    north, south = lax.rem(lat + 3, N_LAT), lax.rem(lat + 1, N_LAT)
    west, east = lax.rem(lon + N_LON - 1, N_LON), lax.rem(lon + 1, N_LON)

    def halo_row(k, side):
        return halo.at[k, side * COLS : (side + 1) * COLS]

    def halo_col(k, side, turn):
        at = 2 * COLS + 16 * (3 * side + turn)
        return halo.at[k, at : at + 16]

    def halo_copies(src, k):
        pieces = [(src.at[ROWS - 1], halo_row(k, 0), south, lon)]
        pieces.append((src.at[0], halo_row(k, 1), north, lon))
        for side, column, target in ((0, 1, east), (1, 0, west)):
            for turn, tlat in enumerate((lat, south, north)):
                pieces.append((strip.at[k, column], halo_col(k, side, turn), tlat, target))
        return [remote(s, d, halo_send.at[k], halo_recv.at[k], a, b) for s, d, a, b in pieces]

    def halo_pack(src, k):
        for r in range(ROWS):
            stripf[0, r : r + 1, :] = src[r, 0:16, :].astype(F32)[0:1, :]
            stripf[1, r : r + 1, :] = src[r, COLS - 16 : COLS, :].astype(F32)[15:16, :]
        strip[k, 0] = stripf[0].astype(BF16)
        strip[k, 1] = stripf[1].astype(BF16)

    def halo_start(src, k):
        for copy in halo_copies(src, k):
            copy.start()

    def widen(src, x3, low=0, high=ROWS):
        for r in range(low, high):
            row = src[r].astype(F32)
            x3[r + 1, :, 0:CH] = pltpu.roll(row, 1, 0).astype(BF16)
            x3[r + 1, :, CH : 2 * CH] = src[r]
            x3[r + 1, :, 2 * CH : 3 * CH] = pltpu.roll(row, COLS - 1, 0).astype(BF16)

    def halo_finish(src, k, x3):
        await_bytes(halo.at[k], halo_recv.at[k])
        await_bytes(halo.at[k], halo_send.at[k])
        first = iota((16, CH), 0) == 0
        last = iota((16, CH), 0) == 15
        left = halo_col(k, 0, 0)[...].astype(F32)
        right = halo_col(k, 1, 0)[...].astype(F32)
        for r in range(ROWS):
            low = x3[r + 1, 0:16, 0:CH].astype(F32)
            x3[r + 1, 0:16, 0:CH] = jnp.where(first, left[r : r + 1, :], low).astype(BF16)
            high = x3[r + 1, COLS - 16 : COLS, 2 * CH : 3 * CH].astype(F32)
            x3[r + 1, COLS - 16 : COLS, 2 * CH : 3 * CH] = jnp.where(
                last, right[r : r + 1, :], high
            ).astype(BF16)
        spot = iota((COLS, CH), 0)
        for side, r, turn, pick, valid in (
            (0, 0, 1, ROWS - 1, lat > 0),
            (1, ROWS + 1, 2, 0, lat < N_LAT - 1),
        ):
            keep = jnp.where(valid, 1.0, 0.0).astype(F32)
            row = halo_row(k, side)[...].astype(F32) * keep
            lcorner = halo_col(k, 0, turn)[...].astype(F32)[pick : pick + 1, :] * keep
            rcorner = halo_col(k, 1, turn)[...].astype(F32)[pick : pick + 1, :] * keep
            x3[r, :, 0:CH] = jnp.where(spot == 0, lcorner, pltpu.roll(row, 1, 0)).astype(BF16)
            x3[r, :, CH : 2 * CH] = row.astype(BF16)
            x3[r, :, 2 * CH : 3 * CH] = jnp.where(
                spot == COLS - 1, rcorner, pltpu.roll(row, COLS - 1, 0)
            ).astype(BF16)

    def conv(x3, k, finish, flip=False, low=0, high=4):
        if flip:
            taps = [
                conv_w[k, 2 - p, (2 - q) * CH : (3 - q) * CH, :] for p in range(3) for q in range(3)
            ]
            taps = jnp.concatenate(taps, axis=1)
        else:
            taps = conv_w[k].reshape(9 * CH, CH)
        for b in range(low, high):
            near = [x3[4 * b + p : 4 * b + p + 4].reshape(4 * COLS, 3 * CH) for p in range(3)]
            near = jnp.concatenate(near, axis=1)
            if flip:
                acc = lax.dot_general(near, taps, NT, preferred_element_type=F32)
            else:
                acc = dot(near, taps)
            finish(slice(4 * b, 4 * b + 4), acc)

    def tile4(x):
        return x.reshape(4 * COLS, CH)

    def grid4(x):
        return x.reshape(4, COLS, CH)

    def turn_act(act, act_t):
        for r in range(ROWS):
            act_t[:, r * COLS : (r + 1) * COLS] = act[r].T

    def own_meta():
        line, lane = iota((32, 128), 0), iota((32, 128), 1)
        own_four = jnp.where(lax.div(lane, 4) == line, live_counts[...].astype(F32), 0.0).astype(BF16)
        to_slots = jnp.where(
            lax.rem(iota((128, 128), 0), 4) == lax.div(iota((128, 128), 1), 32), 1.0, 0.0
        ).astype(BF16)
        live = lax.rem(lane, 32).astype(F32) < dot(own_four, to_slots)
        cell, sub = cells[...], subs[...]
        u, v = sub >> 3, sub & 7
        u = jnp.where(u >= 4, u - 4, 3 - u)
        v = jnp.where(v >= 4, v - 4, 3 - v)
        row = cell >> 7
        fields = [
            jnp.where(live, (cell & 127).astype(F32), 255.0),
            (row * 16 + u * 4 + v).astype(F32),
            ((2 * u + 1) * (2 * u + 1) + (2 * v + 1) * (2 * v + 1)).astype(F32),
            row.astype(F32),
        ]
        for i in range(4):
            mixed = jnp.zeros((32, 128), F32)
            for f in range(4):
                shift = (f - i) * 32 % 128
                turned_field = pltpu.roll(fields[f], shift, 1) if shift else fields[f]
                mixed = jnp.where(lax.div(lane, 32) == f, turned_field, mixed)
            for r in range(32):
                meta_own[i, r] = mixed[r : r + 1, :]

    pl.semaphore_wait(barrier, 72)
    pair_other.start()
    own_meta()
    meta_start(0)
    cot_copy.wait()
    halo_pack(cot, 0)
    halo_start(cot, 0)
    widen(cot, x3_cot, 0, 8)
    meta_wait(0)
    meta_start(1)
    widen(cot, x3_cot, 8, 16)
    meta_wait(1)
    meta_start(2)
    pair_own.wait()
    pair_other.wait()
    pltpu.make_async_copy(queue.at[chip], vals.at[0], a2a_recv.at[0]).start()
    for j in range(1, 16):
        send_slot(j)
    conv_copy.wait()
    embed_t[...] = embed_w[...].T
    halo_finish(cot, 0, x3_cot)

    def keep_back(rows, acc):
        back[rows] = grid4(acc)

    for g in range(1, 4):
        for j in range(16 * g, 16 * g + 16):
            send_slot(j)
        conv(x3_cot, 1, keep_back, flip=True, low=g - 1, high=4 if g == 3 else g)
    meta_wait(2)

    placed[...] = jnp.zeros_like(placed)
    counts[...] = jnp.zeros_like(counts)
    slot_mask = jnp.where(
        lax.rem(iota((CAP, 128), 1), 32) == iota((CAP, 128), 0), 1.0, 0.0
    ).astype(F32)
    spread = jnp.where(
        lax.div(iota((128, 512), 0), 32) == lax.div(iota((128, 512), 1), 128), 1.0, 0.0
    ).astype(BF16)
    lane, line = iota((COLS + 16, 128), 1), iota((COLS + 16, 128), 0)
    pick = jnp.where(lax.div(lane, 32) == jnp.where(line < COLS, 0, 3), 1.0, 0.0).astype(BF16)
    decay = sharp[...] * (-1.0 / 256.0)

    for g in range(4):
        for s in range(32):
            sx, sy, sz = source(g * 16 + s // 2)
            line = jnp.broadcast_to(meta[sy * 2 + s % 2, sx, sz], (CAP, 128)) * slot_mask
            tmeta[s * CAP : s * CAP + CAP, :] = line.astype(BF16)
        await_bytes(vals.at[pl.ds(g * 16, 16)], a2a_recv.at[g])

        for b in range(4):
            at = slice(b * 256, b * 256 + 256)
            of = slice(g * GROUP + b * 256, g * GROUP + b * 256 + 256)
            wide = dot(tmeta[at, :], spread)
            colb[of, :] = wide[:, 0:128].astype(BF16)
            rowb[of, :] = wide[:, 384:512].astype(BF16)
            rk_of = jnp.concatenate([wide[:, 128:256]] * 2, axis=1)
            radius = jnp.concatenate([wide[:, 256:384]] * 2, axis=1)
            rk[at, :] = jnp.where(
                rk_of == iota((256, 256), 1).astype(F32), 1.0, 0.0
            ).astype(BF16)
            w = jnp.exp(radius * decay)
            weight[of, :] = w
            ew[at, :] = (dot(vals[g * 16 + 4 * b : g * 16 + 4 * b + 4].reshape(256, VALS), embed_w[...]) * w).astype(BF16)

        both = lax.dot_general(pick, tmeta[...], NT, preferred_element_type=F32)
        colhot[...] = jnp.where(
            both[0:COLS] == iota((COLS, GROUP), 0).astype(F32), 1.0, 0.0
        ).astype(BF16)
        rowl[...] = both[COLS : COLS + 16]
        counts[...] += dot(colhot[...], rk[...])

        hot = colhot[...].reshape(8, 16, GROUP)
        for b in range(4):
            rows = []
            for r in range(4 * b, 4 * b + 4):
                mask = jnp.where(rowl[...] == float(r), 1.0, 0.0).astype(BF16)
                rows.append((hot * mask[None]).reshape(COLS, GROUP))
            at = slice(b * 512, b * 512 + 512)
            placed[at, :] += dot(jnp.concatenate(rows, axis=0), ew[...])

    kind = lax.rem(iota((256, CH), 0), 16)
    half_u, half_v = 2 * lax.div(kind, 4) + 1, 2 * lax.rem(kind, 4) + 1
    table = jnp.exp((half_u * half_u + half_v * half_v).astype(F32) * decay)
    table_hi = table.astype(BF16)
    table_lo = (table - table_hi.astype(F32)).astype(BF16)
    tables = jnp.concatenate([table_hi, table_lo], axis=0)
    row_of_lane = lax.div(iota((COLS, 256), 1), 16)
    for b in range(4):
        rows = []
        for r in range(4 * b, 4 * b + 4):
            rows.append(jnp.where(row_of_lane == r, counts[...], 0.0).astype(BF16))
        tally = jnp.concatenate(rows, axis=0)
        recip = 1.0 / (dot(jnp.concatenate([tally, tally], axis=1), tables) + 1.0)
        at = slice(4 * b, 4 * b + 4)
        inv[at] = grid4(recip)
        value = (placed[b * 512 : b * 512 + 512, :] * recip).astype(BF16)
        base[at] = grid4(value)
        x = value.astype(F32)
        s = sigmoid(x)
        act_zero[at] = grid4((x * s).astype(BF16))
        bend[at] = grid4(s * (1.0 + x * (1.0 - s)))

    halo_pack(act_zero, 1)
    halo_start(act_zero, 1)
    widen(act_zero, x3_act)
    turn_act(act_zero, zero_t)
    halo_finish(act_zero, 1, x3_act)

    def keep_mid(rows, acc):
        value = (tile4(base[rows]).astype(F32) + acc).astype(BF16)
        mid[rows] = grid4(value)
        x = value.astype(F32)
        s = sigmoid(x)
        act_one[rows] = grid4((x * s).astype(BF16))
        slope = s * (1.0 + x * (1.0 - s))
        grad = tile4(cot[rows]).astype(F32) + tile4(back[rows]) * slope
        gmid[rows] = grid4(grad.astype(BF16))

    conv(x3_act, 0, keep_mid)
    halo_pack(gmid, 2)
    halo_start(gmid, 2)
    halo_pack(act_one, 3)
    halo_start(act_one, 3)

    def kernel_grad(act_t, x3, k, beside=None):
        for p in range(3):
            if beside is not None:
                beside(p)
            block = dot(act_t[...], x3[2 - p : 2 - p + ROWS].reshape(CELLS, 3 * CH))
            for q in range(3):
                for h in range(2):
                    n, lanes = 6 * p + 2 * q + h, (2 - q) * CH + h * 128
                    at = n % 3 * CH
                    grads[k, n // 6, n // 3 % 2, at : at + CH, :] = block[
                        :, lanes : lanes + 128
                    ].astype(BF16)

    coords = {"x": xi, "y": yi, "z": lat}
    orders = (("x", "y", "z"), ("y", "z", "x"), ("z", "x", "y"))

    def along(axis, c):
        cx, cy, cz = [c if axis == n else coords[n] for n in ("x", "y", "z")]
        return cz, cx * 8 + cy * 2 + ci

    def turned(axis, d):
        return {"x": to_x, "y": to_y, "z": to_z}[axis][d]

    def part_copies(k, stage):
        sems = (ar_send.at[k, stage], ar_recv.at[k, stage])
        if stage == 0:
            return [remote(grads.at[k, :, 1 - ci], p0.at[k], *sems, lat, other_core)]
        if stage == 6:
            half = total.at[k, :, ci]
            return [remote(half, half, *sems, lat, other_core)]
        copies = []
        for a, order in enumerate(orders):
            quarter = coords[order[0]] * QUARTER
            shard = quarter + coords[order[1]] * SHARD
            axis = order[{1: 0, 2: 1, 3: 2, 4: 1, 5: 0}[stage]]
            for d in (1, 3, 2):
                c = turned(axis, d)
                if stage == 1:
                    src, dst = s1.at[k, a, aligned(c * QUARTER, QUARTER, 16)], p1.at[k, a, d - 1]
                elif stage == 2:
                    src, dst = s2.at[k, a, aligned(c * SHARD, SHARD, 16)], p2.at[k, a, d - 1]
                elif stage == 3:
                    src, dst = s3.at[k, a], p3.at[k, a, coords[axis]]
                elif stage == 4:
                    src = dst = total.at[k, a, ci, aligned(shard, SHARD, 16)]
                else:
                    src = dst = total.at[k, a, ci, aligned(quarter, QUARTER, 16)]
                copies.append(remote(src, dst, *sems, *along(axis, c)))
        return copies

    def ar_start(k, stage):
        for copy in part_copies(k, stage):
            copy.start()

    def ar_finish(k, stage):
        amount = (p0, p1, p2, p2, p2, p1, p0)[stage].at[k]
        await_bytes(amount, ar_recv.at[k, stage])
        await_bytes(amount, ar_send.at[k, stage])
        for a, order in enumerate(orders):
            if stage == 0:
                here = grads[k, a, ci].astype(F32)
                s1[k, a] = (here + p0[k, a].astype(F32)).astype(BF16)
            elif stage in (1, 2):
                size = QUARTER if stage == 1 else SHARD
                src, came, dst = (s1, p1, s2) if stage == 1 else (s2, p2, s3)
                at = aligned(coords[order[stage - 1]] * size, size, 16)
                here = src[k, a, at, :].astype(F32)
                for d in range(3):
                    here += came[k, a, d].astype(F32)
                dst[k, a] = here.astype(BF16)
            elif stage == 3:
                p3[k, a, coords[order[2]]] = s3[k, a]
                whole = p3[k, a, 0].astype(F32)
                for d in range(1, 4):
                    whole += p3[k, a, d].astype(F32)
                quarter = coords[order[0]] * QUARTER
                at = aligned(quarter + coords[order[1]] * SHARD, SHARD, 16)
                total[k, a, ci, at, :] = whole.astype(BF16)

    def ar_step(k, stage):
        ar_finish(k, stage)
        ar_start(k, stage + 1)

    def ar_leave(k):
        return pltpu.make_async_copy(total.at[k], grads_out.at[k], local_sem.at[3 if k else 6])

    turn_act(act_one, act_t)
    kernel_grad(act_t, x3_cot, 1, lambda p: widen(gmid, x3_mid, (0, 6, 11)[p], (6, 11, 16)[p]))
    ar_start(1, 0)
    halo_finish(gmid, 2, x3_mid)
    ar_step(1, 0)
    kernel_grad(zero_t, x3_mid, 0)
    ar_start(0, 0)

    def keep_gp(rows, acc):
        grad = tile4(gmid[rows]).astype(F32) + acc * tile4(bend[rows])
        gp[rows.start * COLS : rows.stop * COLS, :] = (
            grad * tile4(inv[rows])
        ).astype(BF16)

    conv(x3_mid, 0, keep_gp, flip=True, low=0, high=2)
    ar_step(1, 1)
    ar_step(0, 0)
    conv(x3_mid, 0, keep_gp, flip=True, low=2, high=4)

    esum[...] = jnp.zeros_like(esum)

    def vg_copy(j):
        sx, sy, sz = source(j)
        return remote(vg.at[j], relay.at[chip], vg_send, vg_recv, sz, sx * 8 + sy * 2 + ci)

    def gather(b):
        widen(act_one, x3_act, 2 * b, 2 * b + 2)
        at = slice(b * 512, b * 512 + 512)
        chips = slice(b * 8, b * 8 + 8)
        hot = jnp.where(
            colb[at, :].astype(F32) == iota((512, COLS), 1).astype(F32), 1.0, 0.0
        ).astype(BF16)
        row_of = rowb[at, :]
        pieces = [
            jnp.where(row_of == jnp.array(r, BF16), hot, jnp.zeros_like(hot)) for r in range(ROWS)
        ]
        found = dot(jnp.concatenate(pieces, axis=1), gp[...])
        grad = (found * weight[at, :]).astype(BF16)
        vg[chips] = dot(grad, embed_t[...]).astype(BF16).reshape(8, 2, CAP, VALS)
        own = vals[chips].reshape(512, VALS)
        esum[...] += lax.dot_general(own, grad, TN, preferred_element_type=F32)
        for j in range(8 * b, 8 * b + 8):
            if j == 0:
                pltpu.make_async_copy(vg.at[0], relay.at[chip], vg_recv).start()
            else:
                vg_copy(j).start()

    gather(0)
    gather(1)
    ar_step(1, 2)
    gather(2)
    ar_step(0, 1)
    gather(3)
    ar_step(1, 3)
    gather(4)
    ar_step(0, 2)
    gather(5)
    ar_step(1, 4)
    gather(6)
    ar_step(0, 3)
    gather(7)
    ar_step(0, 4)

    member = yc
    column = xi * 4 + lat

    def embed_copies(stage):
        copies = []
        for d in range(1, 16 if stage == 1 else 8):
            if stage == 1:
                c = lax.rem(column + d, 16)
                tlat, tlon = lax.rem(c, 4), lax.div(c, 4) * 8 + member
                src, dst = esum.at[aligned(member * 16, 16, 16)], qe.at[column]
            else:
                m = lax.rem(member + d, 8)
                tlat, tlon = lat, xi * 8 + m
                if stage == 0:
                    src, dst = esum.at[aligned(m * 16, 16, 16)], pe.at[d - 1]
                else:
                    src = dst = etotal.at[aligned(member * 16, 16, 16)]
            copies.append(remote(src, dst, em_send.at[stage], em_recv.at[stage], tlat, tlon))
        return copies

    def embed_start(stage):
        for copy in embed_copies(stage):
            copy.start()

    def embed_wait(stage):
        amount = qe.at[pl.ds(0, 15)] if stage == 1 else pe
        await_bytes(amount, em_recv.at[stage])
        await_bytes(amount, em_send.at[stage])

    embed_start(0)
    halo_finish(act_one, 3, x3_act)

    def keep_enc(rows, acc):
        enc[rows] = grid4((tile4(mid[rows]).astype(F32) + acc).astype(BF16))

    conv(x3_act, 1, keep_enc, low=0, high=1)
    ar_step(1, 5)
    embed_wait(0)
    own_rows = aligned(member * 16, 16, 16)
    mine = esum[own_rows, :]
    for d in range(7):
        mine += pe[d]
    esum[own_rows, :] = mine
    embed_start(1)
    conv(x3_act, 1, keep_enc, low=1, high=2)
    ar_step(0, 5)
    conv(x3_act, 1, keep_enc, low=2, high=3)
    ar_finish(1, 6)
    ar_leave(1).start()
    embed_wait(1)
    qe[column] = esum[own_rows, :]
    whole = qe[0]
    for d in range(1, 16):
        whole += qe[d]
    etotal[own_rows, :] = whole
    embed_start(2)
    await_bytes(relay, vg_recv)
    vg_own = pltpu.make_async_copy(relay.at[:, ci], vg_out.at[:, ci], local_sem.at[5])
    vg_own.start()
    vg_other = remote(
        relay.at[:, 1 - ci], vg_out.at[:, ci], pair_send.at[1], pair_recv.at[1], lat, other_core
    )
    vg_other.start()
    conv(x3_act, 1, keep_enc, low=3, high=4)
    enc_copy = pltpu.make_async_copy(enc, enc_out, local_sem.at[2])
    enc_copy.start()
    ar_finish(0, 6)
    ar_leave(0).start()
    embed_wait(2)
    embed_out[...] = etotal[...] * (1.0 / 512.0)
    for g in range(4):
        await_bytes(vals.at[pl.ds(0, 15 if g == 0 else 16)], a2a_send.at[g])
    for stage in range(3):
        meta_sent(stage)
    await_bytes(vg.at[pl.ds(0, 63)], vg_send)
    vg_own.wait()
    vg_other.wait()
    enc_copy.wait()
    ar_leave(1).wait()
    ar_leave(0).wait()


def hand_over(
    enc_in, vg_in, grads_in, embed_in, enc_out, vg_out, grads_out, embed_out,
    enc, vg, embed, narrow, wide, in_sem, out_sem,
):
    steps = []
    for i in range(6):
        src, dst = slice(i % 3 * PART, (i % 3 + 1) * PART), slice(i * 3 * CH, (i + 1) * 3 * CH)
        k = i // 3
        steps.append(
            (grads_in.at[k, src], narrow.at[k, src], wide.at[dst], grads_out.at[dst], (k, src, dst))
        )
    steps.append((enc_in, enc, enc, enc_out, None))
    steps.append((vg_in, vg, vg, vg_out, None))
    steps.append((embed_in, embed, embed, embed_out, None))
    moves = [
        pltpu.make_async_copy(step[0], step[1], in_sem.at[i]) for i, step in enumerate(steps)
    ]
    for move in moves:
        move.start()
    results = []
    for i, (_, _, src, dst, at) in enumerate(steps):
        moves[i].wait()
        if at is not None:
            k, rows, to = at
            for n in range(6):
                half = slice(rows.start + n * CH, rows.start + n * CH + CH)
                into = slice(to.start + n // 2 * CH, to.start + (n // 2 + 1) * CH)
                lanes = slice(n % 2 * 128, n % 2 * 128 + 128)
                wide[into, lanes] = narrow[k, half, :].astype(F32) * (1.0 / 512.0)
        results.append(pltpu.make_async_copy(src, dst, out_sem.at[i]))
        results[i].start()
    for copy in results:
        copy.wait()


def on_device(
    obs_values, obs_cells, obs_subcell, slot_counts, sharpness, embed_weight, conv_weight, cotangent
):
    anywhere = pl.BlockSpec(memory_space=pl.ANY)
    vmem = pl.BlockSpec(memory_space=pltpu.VMEM)
    grid = (ROWS, COLS, CH)
    wide = (ROWS + 2, COLS, 3 * CH)
    dma = pltpu.SemaphoreType.DMA
    scratch = [
        pltpu.VMEM((64, 2, CAP, VALS), BF16),
        pltpu.VMEM((64, 2, CAP, VALS), BF16),
        pltpu.VMEM((64, 2, CAP, VALS), BF16),
        pltpu.VMEM((4, 32, 1, 128), F32),
        pltpu.VMEM((4, 4, 8, 1, 128), F32),
        pltpu.VMEM((4, 4, 4, 2, 1, 128), F32),
        pltpu.VMEM((8, 4, 4, 1, 128), F32),
        pltpu.VMEM((GROUP, 128), BF16),
        pltpu.VMEM((OBS, 128), BF16),
        pltpu.VMEM((OBS, 128), BF16),
        pltpu.VMEM((OBS, CH), F32),
        pltpu.VMEM((GROUP, CH), BF16),
        pltpu.VMEM((GROUP, 256), BF16),
        pltpu.VMEM((COLS, GROUP), BF16),
        pltpu.VMEM((16, GROUP), F32),
        pltpu.VMEM((CELLS, CH), F32),
        pltpu.VMEM((COLS, 256), F32),
        pltpu.VMEM(grid, F32),
        pltpu.VMEM(grid, BF16),
        pltpu.VMEM((2, 3, 3 * CH, CH), BF16),
        pltpu.VMEM((CH, VALS), BF16),
        pltpu.VMEM(grid, F32),
        pltpu.VMEM(grid, F32),
        pltpu.VMEM(grid, BF16),
        pltpu.VMEM(grid, BF16),
        pltpu.VMEM(grid, BF16),
        pltpu.VMEM(grid, BF16),
        pltpu.VMEM(grid, BF16),
        pltpu.VMEM((CELLS, CH), BF16),
        pltpu.VMEM((CH, CELLS), BF16),
        pltpu.VMEM((CH, CELLS), BF16),
        pltpu.VMEM(wide, BF16),
        pltpu.VMEM(wide, BF16),
        pltpu.VMEM(wide, BF16),
        pltpu.VMEM((4, 2 * COLS + 6 * 16, CH), BF16),
        pltpu.VMEM((4, 2, 16, CH), BF16),
        pltpu.VMEM((2, 16, CH), F32),
        pltpu.VMEM((64, 2, CAP, VALS), BF16),
        pltpu.VMEM((2, 3, 2, HALF, 128), BF16),
        pltpu.VMEM((2, 3, 2, HALF, 128), BF16),
        pltpu.VMEM((2, 3, HALF, 128), BF16),
        pltpu.VMEM((2, 3, HALF, 128), BF16),
        pltpu.VMEM((2, 3, 3, QUARTER, 128), BF16),
        pltpu.VMEM((2, 3, QUARTER, 128), BF16),
        pltpu.VMEM((2, 3, 3, SHARD, 128), BF16),
        pltpu.VMEM((2, 3, SHARD, 128), BF16),
        pltpu.VMEM((2, 3, 4, SHARD, 128), BF16),
        pltpu.VMEM((VALS, CH), F32),
        pltpu.VMEM((7, 16, CH), F32),
        pltpu.VMEM((16, 16, CH), F32),
        pltpu.VMEM((VALS, CH), F32),
        pltpu.VMEM(grid, BF16),
        dma((7,)),
        dma((2,)),
        dma((2,)),
        dma((4,)),
        dma((4,)),
        dma((3,)),
        dma((3,)),
        dma,
        dma,
        dma((4,)),
        dma((4,)),
        dma((2, 7)),
        dma((2, 7)),
        dma((3,)),
        dma((3,)),
    ]
    encoded, value_grads, grads, embed_total = pl.pallas_call(
        kernel,
        out_shape=(
            jax.ShapeDtypeStruct(grid, BF16),
            jax.ShapeDtypeStruct((64, 2, CAP, VALS), BF16),
            jax.ShapeDtypeStruct((2, 3, 2, HALF, 128), BF16),
            jax.ShapeDtypeStruct((VALS, CH), F32),
        ),
        in_specs=[anywhere, vmem, vmem, vmem, vmem, vmem, anywhere, anywhere],
        out_specs=(anywhere, anywhere, anywhere, vmem),
        scratch_shapes=scratch,
        compiler_params=pltpu.CompilerParams(
            collective_id=0, has_side_effects=True, vmem_limit_bytes=60 * 1024 * 1024
        ),
        cost_estimate=pl.CostEstimate(
            flops=30_000_000_000, bytes_accessed=20_000_000, transcendentals=4_000_000
        ),
    )(
        obs_values.reshape(64, 2, CAP, VALS),
        obs_cells.reshape(32, 128),
        obs_subcell.reshape(32, 128),
        slot_counts,
        sharpness.reshape(1, CH),
        embed_weight,
        conv_weight.reshape(2, 3, 3 * CH, CH),
        cotangent,
    )
    encoded, value_grads, conv_grads, embed_grads = pl.pallas_call(
        hand_over,
        out_shape=(
            jax.ShapeDtypeStruct(grid, BF16),
            jax.ShapeDtypeStruct((64, 2, CAP, VALS), BF16),
            jax.ShapeDtypeStruct((3 * PART, CH), F32),
            jax.ShapeDtypeStruct((VALS, CH), F32),
        ),
        in_specs=[anywhere] * 4,
        out_specs=(anywhere,) * 4,
        scratch_shapes=[
            pltpu.VMEM(grid, BF16),
            pltpu.VMEM((64, 2, CAP, VALS), BF16),
            pltpu.VMEM((VALS, CH), F32),
            pltpu.VMEM((2, 3 * PART, 128), BF16),
            pltpu.VMEM((3 * PART, CH), F32),
            dma((9,)),
            dma((9,)),
        ],
        compiler_params=pltpu.CompilerParams(vmem_limit_bytes=60 * 1024 * 1024),
    )(encoded, value_grads, grads.reshape(2, 3 * PART, 128), embed_total)
    return (
        encoded,
        value_grads.reshape(OBS, VALS),
        conv_grads.reshape(2, 3, 3, CH, CH),
        embed_grads,
    )


def solution(mesh):
    placed = (
        P(("lat", "lon"), None),
        P(("lat", "lon")),
        P(("lat", "lon")),
        P(("lat", "lon"), None),
        P(),
        P(),
        P(),
        P("lat", "lon", None),
    )
    return jax.shard_map(
        on_device,
        mesh=mesh,
        in_specs=placed,
        out_specs=(P("lat", "lon", None), P(("lat", "lon"), None), P(), P()),
        check_vma=False,
    )
```

```python
import jax
import jax.numpy as jnp
from jax import lax
from jax.experimental import pallas as pl
from jax.experimental.pallas import tpu as pltpu
from jax.sharding import PartitionSpec as P

F32 = jnp.float32
BF16 = jnp.bfloat16
N_LAT, N_LON = 4, 32
DEVICES = N_LAT * N_LON
CAP, VALS, CH = 32, 128, 256
ROWS, COLS = 16, 128
CELLS = ROWS * COLS
OBS = DEVICES * CAP
GROUP = 32 * CAP
PART, HALF, QUARTER, SHARD = 1536, 768, 192, 48
NT = (((1,), (1,)), ((), ()))
TN = (((0,), (0,)), ((), ()))


def dot(a, b):
    return jnp.dot(a, b, preferred_element_type=F32)


def iota(shape, axis):
    return lax.broadcasted_iota(jnp.int32, shape, axis)


def sigmoid(x):
    return 0.5 + 0.5 * jnp.tanh(0.5 * x)


def remote(src, dst, send, recv, lat, lon):
    return pltpu.make_async_remote_copy(
        src_ref=src,
        dst_ref=dst,
        send_sem=send,
        recv_sem=recv,
        device_id=(lat, lon),
        device_id_type=pl.DeviceIdType.MESH,
    )


def await_bytes(ref, sem):
    pltpu.make_async_copy(ref, ref, sem).wait()


def loop(low, high, body):
    def step(i, carry):
        body(i)
        return carry

    lax.fori_loop(low, high, step, 0)


def aligned(start, size, unit):
    return pl.ds(pl.multiple_of(start, unit), size)


def kernel(
    obs_in, cells, subs, live_counts, sharp, embed_w, conv_in, cot_in,
    enc_out, vg_out, grads_out, embed_out,
    vals, queue, relay, meta_own, meta_z, meta_x, meta, tmeta, colb, rowb, weight, ew, rk, colhot, rowl, placed, counts, inv,
    cot, conv_w, embed_t, back, bend, base, act_zero, mid, act_one, gmid, gp, act_t, zero_t,
    x3_act, x3_cot, x3_mid, halo, strip, stripf,
    vg, grads, total, p0, s1, p1, s2, p2, s3, p3, esum, pe, qe, etotal, enc,
    local_sem, pair_send, pair_recv, a2a_send, a2a_recv, meta_send, meta_recv, vg_send, vg_recv,
    halo_send, halo_recv, ar_send, ar_recv, em_send, em_recv,
):
    lat = lax.axis_index("lat")
    lon = lax.axis_index("lon")
    me = lat * N_LON + lon
    xi, yi, ci = lax.div(lon, 8), lax.rem(lax.div(lon, 2), 4), lax.rem(lon, 2)

    chip = lat * 16 + xi * 4 + yi
    yc = lax.rem(lon, 8)
    other_core = lon + 1 - 2 * ci

    to_x = [xi] + [lax.rem(xi + d, 4) for d in range(1, 4)]
    to_y = [yi] + [lax.rem(yi + d, 4) for d in range(1, 4)]
    to_z = [lat] + [lax.rem(lat + d, 4) for d in range(1, 4)]

    def offset(j):
        dx, dy = j // 4 % 4, j % 4
        return dx, dy, (j // 16 + 8 - dx - dy) % 4

    def source(j):
        dx, dy, dz = offset(j)
        return to_x[-dx % 4], to_y[-dy % 4], to_z[-dz % 4]

    barrier = pltpu.get_barrier_semaphore()

    cot_copy = pltpu.make_async_copy(cot_in, cot, local_sem.at[0])
    cot_copy.start()
    pair_own = pltpu.make_async_copy(obs_in.at[:, ci], queue.at[:, ci], local_sem.at[4])
    pair_own.start()
    pair_other = remote(
        obs_in.at[:, 1 - ci], queue.at[:, ci], pair_send.at[0], pair_recv.at[0], lat, other_core
    )

    def signal(tlat, tlon):
        pl.semaphore_signal(
            barrier, inc=1, device_id=(tlat, tlon), device_id_type=pl.DeviceIdType.MESH
        )

    for j in range(1, 64):
        signal(to_z[j // 4 % 4], to_x[j // 16] * 8 + to_y[j % 4] * 2 + ci)
    beside = lax.rem(lon + N_LON - 1 + 2 * ci, N_LON)
    for turn in (0, 1, 3):
        signal(to_z[turn], other_core)
        signal(to_z[turn], beside)
    for d in range(1, 4):
        signal(lat, xi * 8 + to_y[d] * 2 + 1 - ci)

    def meta_copies(stage):
        copies = []
        for d in range(1, 8 if stage == 2 else 4):
            if stage == 0:
                c = lax.rem(lat + d, 4)
                src, dst, target = meta_own.at[:, pl.ds(c * 8, 8)], meta_z.at[lat], (c, lon)
            elif stage == 1:
                c = lax.rem(xi + d, 4)
                src, dst = meta_z.at[:, :, pl.ds(c * 2, 2)], meta_x.at[xi]
                target = (lat, c * 8 + yc)
            else:
                c = lax.rem(yc + d, 8)
                src, dst = meta_x.at[:, :, lax.rem(c, 4), lax.div(c, 4)], meta.at[yc]
                target = (lat, xi * 8 + c)
            copies.append(remote(src, dst, meta_send.at[stage], meta_recv.at[stage], *target))
        own = (
            (meta_own.at[:, pl.ds(lat * 8, 8)], meta_z.at[lat]),
            (meta_z.at[:, :, pl.ds(xi * 2, 2)], meta_x.at[xi]),
            (meta_x.at[:, :, lax.rem(yc, 4), lax.div(yc, 4)], meta.at[yc]),
        )[stage]
        copies.append(pltpu.make_async_copy(*own, meta_recv.at[stage]))
        return copies

    def meta_start(stage):
        for copy in meta_copies(stage):
            copy.start()

    def meta_wait(stage):
        await_bytes((meta_z, meta_x, meta)[stage], meta_recv.at[stage])

    def meta_sent(stage):
        await_bytes((meta_z, meta_x, meta)[stage].at[pl.ds(0, (3, 3, 7)[stage])], meta_send.at[stage])

    line, lane = iota((32, 128), 0), iota((32, 128), 1)
    own_four = jnp.where(lax.div(lane, 4) == line, live_counts[...].astype(F32), 0.0).astype(BF16)
    to_slots = jnp.where(
        lax.rem(iota((128, 128), 0), 4) == lax.div(iota((128, 128), 1), 32), 1.0, 0.0
    ).astype(BF16)
    live = lax.rem(lane, 32).astype(F32) < dot(own_four, to_slots)
    cell, sub = cells[...], subs[...]
    u, v = sub >> 3, sub & 7
    u = jnp.where(u >= 4, u - 4, 3 - u)
    v = jnp.where(v >= 4, v - 4, 3 - v)
    row = cell >> 7
    fields = [
        jnp.where(live, (cell & 127).astype(F32), 255.0),
        (row * 16 + u * 4 + v).astype(F32),
        ((2 * u + 1) * (2 * u + 1) + (2 * v + 1) * (2 * v + 1)).astype(F32),
        row.astype(F32),
    ]
    for i in range(4):
        mixed = jnp.zeros((32, 128), F32)
        for f in range(4):
            shift = (f - i) * 32 % 128
            turned_field = pltpu.roll(fields[f], shift, 1) if shift else fields[f]
            mixed = jnp.where(lax.div(lane, 32) == f, turned_field, mixed)
        for r in range(32):
            meta_own[i, r] = mixed[r : r + 1, :]

    conv_copy = pltpu.make_async_copy(conv_in, conv_w, local_sem.at[1])
    conv_copy.start()

    def send_slot(j):
        dx, dy, dz = offset(j)
        tx, ty, tz = to_x[dx], to_y[dy], to_z[dz]
        g = j // 16
        remote(
            queue.at[tz * 16 + tx * 4 + ty], vals.at[j], a2a_send.at[g], a2a_recv.at[g],
            tz, tx * 8 + ty * 2 + ci,
        ).start()

    north, south = lax.rem(lat + 3, N_LAT), lax.rem(lat + 1, N_LAT)
    west, east = lax.rem(lon + N_LON - 1, N_LON), lax.rem(lon + 1, N_LON)

    def halo_row(k, side):
        return halo.at[k, side * COLS : (side + 1) * COLS]

    def halo_col(k, side, turn):
        at = 2 * COLS + 16 * (3 * side + turn)
        return halo.at[k, at : at + 16]

    def halo_copies(src, k):
        pieces = [(src.at[ROWS - 1], halo_row(k, 0), south, lon)]
        pieces.append((src.at[0], halo_row(k, 1), north, lon))
        for side, column, target in ((0, 1, east), (1, 0, west)):
            for turn, tlat in enumerate((lat, south, north)):
                pieces.append((strip.at[k, column], halo_col(k, side, turn), tlat, target))
        return [remote(s, d, halo_send.at[k], halo_recv.at[k], a, b) for s, d, a, b in pieces]

    def halo_pack(src, k):
        for r in range(ROWS):
            stripf[0, r : r + 1, :] = src[r, 0:16, :].astype(F32)[0:1, :]
            stripf[1, r : r + 1, :] = src[r, COLS - 16 : COLS, :].astype(F32)[15:16, :]
        strip[k, 0] = stripf[0].astype(BF16)
        strip[k, 1] = stripf[1].astype(BF16)

    def halo_start(src, k):
        for copy in halo_copies(src, k):
            copy.start()

    def widen(src, x3, low=0, high=4):
        def body(b):
            for i in range(4):
                r = 4 * b + i
                row = src[r].astype(F32)
                x3[r + 1, :, 0:CH] = pltpu.roll(row, 1, 0).astype(BF16)
                x3[r + 1, :, CH : 2 * CH] = src[r]
                x3[r + 1, :, 2 * CH : 3 * CH] = pltpu.roll(row, COLS - 1, 0).astype(BF16)

        loop(low, high, body)

    def halo_finish(src, k, x3):
        await_bytes(halo.at[k], halo_recv.at[k])
        await_bytes(halo.at[k], halo_send.at[k])
        first = iota((16, CH), 0) == 0
        last = iota((16, CH), 0) == 15
        left = halo_col(k, 0, 0)[...].astype(F32)
        right = halo_col(k, 1, 0)[...].astype(F32)
        for r in range(ROWS):
            low = x3[r + 1, 0:16, 0:CH].astype(F32)
            x3[r + 1, 0:16, 0:CH] = jnp.where(first, left[r : r + 1, :], low).astype(BF16)
            high = x3[r + 1, COLS - 16 : COLS, 2 * CH : 3 * CH].astype(F32)
            x3[r + 1, COLS - 16 : COLS, 2 * CH : 3 * CH] = jnp.where(
                last, right[r : r + 1, :], high
            ).astype(BF16)
        spot = iota((COLS, CH), 0)
        for side, r, turn, pick, valid in (
            (0, 0, 1, ROWS - 1, lat > 0),
            (1, ROWS + 1, 2, 0, lat < N_LAT - 1),
        ):
            keep = jnp.where(valid, 1.0, 0.0).astype(F32)
            row = halo_row(k, side)[...].astype(F32) * keep
            lcorner = halo_col(k, 0, turn)[...].astype(F32)[pick : pick + 1, :] * keep
            rcorner = halo_col(k, 1, turn)[...].astype(F32)[pick : pick + 1, :] * keep
            x3[r, :, 0:CH] = jnp.where(spot == 0, lcorner, pltpu.roll(row, 1, 0)).astype(BF16)
            x3[r, :, CH : 2 * CH] = row.astype(BF16)
            x3[r, :, 2 * CH : 3 * CH] = jnp.where(
                spot == COLS - 1, rcorner, pltpu.roll(row, COLS - 1, 0)
            ).astype(BF16)

    def conv(x3, k, finish, flip=False, low=0, high=4):
        if flip:
            taps = [
                conv_w[k, 2 - p, (2 - q) * CH : (3 - q) * CH, :] for p in range(3) for q in range(3)
            ]
            taps = jnp.concatenate(taps, axis=1)
        else:
            taps = conv_w[k].reshape(9 * CH, CH)
        for b in range(low, high):
            near = [x3[4 * b + p : 4 * b + p + 4].reshape(4 * COLS, 3 * CH) for p in range(3)]
            near = jnp.concatenate(near, axis=1)
            if flip:
                acc = lax.dot_general(near, taps, NT, preferred_element_type=F32)
            else:
                acc = dot(near, taps)
            finish(slice(4 * b, 4 * b + 4), acc)

    def tile4(x):
        return x.reshape(4 * COLS, CH)

    def grid4(x):
        return x.reshape(4, COLS, CH)

    def turn_act(act, act_t):
        for r in range(ROWS):
            act_t[:, r * COLS : (r + 1) * COLS] = act[r].T

    cot_copy.wait()
    halo_pack(cot, 0)
    pl.semaphore_wait(barrier, 72)
    pair_other.start()
    meta_start(0)
    halo_start(cot, 0)
    meta_wait(0)
    meta_start(1)
    widen(cot, x3_cot, 0, 2)
    pair_own.wait()
    pair_other.wait()
    pltpu.make_async_copy(queue.at[chip], vals.at[0], a2a_recv.at[0]).start()
    for j in range(1, 16):
        send_slot(j)
    meta_wait(1)
    meta_start(2)
    for j in range(16, 32):
        send_slot(j)
    widen(cot, x3_cot, 2, 4)
    conv_copy.wait()
    embed_t[...] = embed_w[...].T
    halo_finish(cot, 0, x3_cot)

    def keep_back(rows, acc):
        back[rows] = grid4(acc)

    for g in range(2, 4):
        for j in range(16 * g, 16 * g + 16):
            send_slot(j)
        conv(x3_cot, 1, keep_back, flip=True, low=2 * g - 4, high=2 * g - 2)
    meta_wait(2)

    placed[...] = jnp.zeros_like(placed)
    counts[...] = jnp.zeros_like(counts)
    slot_mask = jnp.where(
        lax.rem(iota((CAP, 128), 1), 32) == iota((CAP, 128), 0), 1.0, 0.0
    ).astype(F32)
    spread = jnp.where(
        lax.div(iota((128, 512), 0), 32) == lax.div(iota((128, 512), 1), 128), 1.0, 0.0
    ).astype(BF16)
    lane, line = iota((COLS + 16, 128), 1), iota((COLS + 16, 128), 0)
    pick = jnp.where(lax.div(lane, 32) == jnp.where(line < COLS, 0, 3), 1.0, 0.0).astype(BF16)
    decay = sharp[...] * (-1.0 / 256.0)

    for g in range(4):
        for s in range(32):
            sx, sy, sz = source(g * 16 + s // 2)
            line = jnp.broadcast_to(meta[sy * 2 + s % 2, sx, sz], (CAP, 128)) * slot_mask
            tmeta[s * CAP : s * CAP + CAP, :] = line.astype(BF16)
        await_bytes(vals.at[pl.ds(g * 16, 16)], a2a_recv.at[g])

        for b in range(4):
            at = slice(b * 256, b * 256 + 256)
            of = slice(g * GROUP + b * 256, g * GROUP + b * 256 + 256)
            wide = dot(tmeta[at, :], spread)
            colb[of, :] = wide[:, 0:128].astype(BF16)
            rowb[of, :] = wide[:, 384:512].astype(BF16)
            rk_of = jnp.concatenate([wide[:, 128:256]] * 2, axis=1)
            radius = jnp.concatenate([wide[:, 256:384]] * 2, axis=1)
            rk[at, :] = jnp.where(
                rk_of == iota((256, 256), 1).astype(F32), 1.0, 0.0
            ).astype(BF16)
            w = jnp.exp(radius * decay)
            weight[of, :] = w
            ew[at, :] = (dot(vals[g * 16 + 4 * b : g * 16 + 4 * b + 4].reshape(256, VALS), embed_w[...]) * w).astype(BF16)

        both = lax.dot_general(pick, tmeta[...], NT, preferred_element_type=F32)
        colhot[...] = jnp.where(
            both[0:COLS] == iota((COLS, GROUP), 0).astype(F32), 1.0, 0.0
        ).astype(BF16)
        rowl[...] = both[COLS : COLS + 16]
        counts[...] += dot(colhot[...], rk[...])

        hot = colhot[...].reshape(8, 16, GROUP)
        for b in range(4):
            rows = []
            for r in range(4 * b, 4 * b + 4):
                mask = jnp.where(rowl[...] == float(r), 1.0, 0.0).astype(BF16)
                rows.append((hot * mask[None]).reshape(COLS, GROUP))
            at = slice(b * 512, b * 512 + 512)
            placed[at, :] += dot(jnp.concatenate(rows, axis=0), ew[...])

    kind = lax.rem(iota((256, CH), 0), 16)
    half_u, half_v = 2 * lax.div(kind, 4) + 1, 2 * lax.rem(kind, 4) + 1
    table = jnp.exp((half_u * half_u + half_v * half_v).astype(F32) * decay)
    table_hi = table.astype(BF16)
    table_lo = (table - table_hi.astype(F32)).astype(BF16)
    tables = jnp.concatenate([table_hi, table_lo], axis=0)
    row_of_lane = lax.div(iota((COLS, 256), 1), 16)
    for b in range(4):
        rows = []
        for r in range(4 * b, 4 * b + 4):
            rows.append(jnp.where(row_of_lane == r, counts[...], 0.0).astype(BF16))
        tally = jnp.concatenate(rows, axis=0)
        recip = 1.0 / (dot(jnp.concatenate([tally, tally], axis=1), tables) + 1.0)
        at = slice(4 * b, 4 * b + 4)
        inv[at] = grid4(recip)
        value = (placed[b * 512 : b * 512 + 512, :] * recip).astype(BF16)
        base[at] = grid4(value)
        x = value.astype(F32)
        s = sigmoid(x)
        act_zero[at] = grid4((x * s).astype(BF16))
        bend[at] = grid4(s * (1.0 + x * (1.0 - s)))

    halo_pack(act_zero, 1)
    halo_start(act_zero, 1)
    widen(act_zero, x3_act)
    turn_act(act_zero, zero_t)
    halo_finish(act_zero, 1, x3_act)

    def keep_mid(rows, acc):
        value = (tile4(base[rows]).astype(F32) + acc).astype(BF16)
        mid[rows] = grid4(value)
        x = value.astype(F32)
        s = sigmoid(x)
        act_one[rows] = grid4((x * s).astype(BF16))
        slope = s * (1.0 + x * (1.0 - s))
        grad = tile4(cot[rows]).astype(F32) + tile4(back[rows]) * slope
        gmid[rows] = grid4(grad.astype(BF16))

    conv(x3_act, 0, keep_mid)
    halo_pack(gmid, 2)
    halo_start(gmid, 2)
    halo_pack(act_one, 3)
    halo_start(act_one, 3)

    def kernel_grad(act_t, x3, k):
        for p in range(3):
            block = dot(act_t[...], x3[2 - p : 2 - p + ROWS].reshape(CELLS, 3 * CH))
            for q in range(3):
                for h in range(2):
                    n, lanes = 6 * p + 2 * q + h, (2 - q) * CH + h * 128
                    at = n % 3 * CH
                    grads[k, n // 6, n // 3 % 2, at : at + CH, :] = block[
                        :, lanes : lanes + 128
                    ].astype(BF16)

    coords = {"x": xi, "y": yi, "z": lat}
    orders = (("x", "y", "z"), ("y", "z", "x"), ("z", "x", "y"))

    def along(axis, c):
        cx, cy, cz = [c if axis == n else coords[n] for n in ("x", "y", "z")]
        return cz, cx * 8 + cy * 2 + ci

    def turned(axis, d):
        return {"x": to_x, "y": to_y, "z": to_z}[axis][d]

    def part_copies(k, stage):
        sems = (ar_send.at[k, stage], ar_recv.at[k, stage])
        if stage == 0:
            return [remote(grads.at[k, :, 1 - ci], p0.at[k], *sems, lat, other_core)]
        if stage == 6:
            half = total.at[k, :, ci]
            return [remote(half, half, *sems, lat, other_core)]
        copies = []
        for a, order in enumerate(orders):
            quarter = coords[order[0]] * QUARTER
            shard = quarter + coords[order[1]] * SHARD
            axis = order[{1: 0, 2: 1, 3: 2, 4: 1, 5: 0}[stage]]
            for d in (1, 3, 2):
                c = turned(axis, d)
                if stage == 1:
                    src, dst = s1.at[k, a, aligned(c * QUARTER, QUARTER, 16)], p1.at[k, a, d - 1]
                elif stage == 2:
                    src, dst = s2.at[k, a, aligned(c * SHARD, SHARD, 16)], p2.at[k, a, d - 1]
                elif stage == 3:
                    src, dst = s3.at[k, a], p3.at[k, a, coords[axis]]
                elif stage == 4:
                    src = dst = total.at[k, a, ci, aligned(shard, SHARD, 16)]
                else:
                    src = dst = total.at[k, a, ci, aligned(quarter, QUARTER, 16)]
                copies.append(remote(src, dst, *sems, *along(axis, c)))
        return copies

    def ar_start(k, stage):
        for copy in part_copies(k, stage):
            copy.start()

    def ar_finish(k, stage):
        amount = (p0, p1, p2, p2, p2, p1, p0)[stage].at[k]
        await_bytes(amount, ar_recv.at[k, stage])
        await_bytes(amount, ar_send.at[k, stage])
        for a, order in enumerate(orders):
            if stage == 0:
                here = grads[k, a, ci].astype(F32)
                s1[k, a] = (here + p0[k, a].astype(F32)).astype(BF16)
            elif stage in (1, 2):
                size = QUARTER if stage == 1 else SHARD
                src, came, dst = (s1, p1, s2) if stage == 1 else (s2, p2, s3)
                at = aligned(coords[order[stage - 1]] * size, size, 16)
                here = src[k, a, at, :].astype(F32)
                for d in range(3):
                    here += came[k, a, d].astype(F32)
                dst[k, a] = here.astype(BF16)
            elif stage == 3:
                p3[k, a, coords[order[2]]] = s3[k, a]
                whole = p3[k, a, 0].astype(F32)
                for d in range(1, 4):
                    whole += p3[k, a, d].astype(F32)
                quarter = coords[order[0]] * QUARTER
                at = aligned(quarter + coords[order[1]] * SHARD, SHARD, 16)
                total[k, a, ci, at, :] = whole.astype(BF16)

    def ar_step(k, stage):
        ar_finish(k, stage)
        ar_start(k, stage + 1)

    def ar_leave(k):
        return pltpu.make_async_copy(total.at[k], grads_out.at[k], local_sem.at[3 if k else 6])

    turn_act(act_one, act_t)
    kernel_grad(act_t, x3_cot, 1)
    ar_start(1, 0)
    widen(gmid, x3_mid)
    halo_finish(gmid, 2, x3_mid)
    ar_step(1, 0)
    kernel_grad(zero_t, x3_mid, 0)
    ar_start(0, 0)

    def keep_gp(rows, acc):
        grad = tile4(gmid[rows]).astype(F32) + acc * tile4(bend[rows])
        gp[rows.start * COLS : rows.stop * COLS, :] = (
            grad * tile4(inv[rows])
        ).astype(BF16)

    conv(x3_mid, 0, keep_gp, flip=True, low=0, high=2)
    ar_step(1, 1)
    ar_step(0, 0)
    conv(x3_mid, 0, keep_gp, flip=True, low=2, high=4)

    esum[...] = jnp.zeros_like(esum)

    def vg_copy(j):
        sx, sy, sz = source(j)
        return remote(vg.at[j], relay.at[chip], vg_send, vg_recv, sz, sx * 8 + sy * 2 + ci)

    def gather(b):
        at = slice(b * 512, b * 512 + 512)
        chips = slice(b * 8, b * 8 + 8)
        hot = jnp.where(
            colb[at, :].astype(F32) == iota((512, COLS), 1).astype(F32), 1.0, 0.0
        ).astype(BF16)
        row_of = rowb[at, :]
        pieces = [
            jnp.where(row_of == jnp.array(r, BF16), hot, jnp.zeros_like(hot)) for r in range(ROWS)
        ]
        found = dot(jnp.concatenate(pieces, axis=1), gp[...])
        grad = (found * weight[at, :]).astype(BF16)
        vg[chips] = dot(grad, embed_t[...]).astype(BF16).reshape(8, 2, CAP, VALS)
        own = vals[chips].reshape(512, VALS)
        esum[...] += lax.dot_general(own, grad, TN, preferred_element_type=F32)
        for j in range(8 * b, 8 * b + 8):
            if j == 0:
                pltpu.make_async_copy(vg.at[0], relay.at[chip], vg_recv).start()
            else:
                vg_copy(j).start()

    gather(0)
    gather(1)
    ar_step(1, 2)
    gather(2)
    ar_step(0, 1)
    gather(3)
    ar_step(1, 3)
    gather(4)
    ar_step(0, 2)
    gather(5)
    ar_step(1, 4)
    gather(6)
    ar_step(0, 3)
    gather(7)
    ar_step(0, 4)

    member = yc
    column = xi * 4 + lat

    def embed_copies(stage):
        copies = []
        for d in range(1, 16 if stage == 1 else 8):
            if stage == 1:
                c = lax.rem(column + d, 16)
                tlat, tlon = lax.rem(c, 4), lax.div(c, 4) * 8 + member
                src, dst = esum.at[aligned(member * 16, 16, 16)], qe.at[column]
            else:
                m = lax.rem(member + d, 8)
                tlat, tlon = lat, xi * 8 + m
                if stage == 0:
                    src, dst = esum.at[aligned(m * 16, 16, 16)], pe.at[d - 1]
                else:
                    src = dst = etotal.at[aligned(member * 16, 16, 16)]
            copies.append(remote(src, dst, em_send.at[stage], em_recv.at[stage], tlat, tlon))
        return copies

    def embed_start(stage):
        for copy in embed_copies(stage):
            copy.start()

    def embed_wait(stage):
        amount = qe.at[pl.ds(0, 15)] if stage == 1 else pe
        await_bytes(amount, em_recv.at[stage])
        await_bytes(amount, em_send.at[stage])

    embed_start(0)
    widen(act_one, x3_act)
    halo_finish(act_one, 3, x3_act)

    def keep_enc(rows, acc):
        enc[rows] = grid4((tile4(mid[rows]).astype(F32) + acc).astype(BF16))

    conv(x3_act, 1, keep_enc, low=0, high=1)
    ar_step(1, 5)
    embed_wait(0)
    own_rows = aligned(member * 16, 16, 16)
    mine = esum[own_rows, :]
    for d in range(7):
        mine += pe[d]
    esum[own_rows, :] = mine
    embed_start(1)
    conv(x3_act, 1, keep_enc, low=1, high=2)
    ar_step(0, 5)
    conv(x3_act, 1, keep_enc, low=2, high=3)
    ar_finish(1, 6)
    ar_leave(1).start()
    embed_wait(1)
    qe[column] = esum[own_rows, :]
    whole = qe[0]
    for d in range(1, 16):
        whole += qe[d]
    etotal[own_rows, :] = whole
    embed_start(2)
    await_bytes(relay, vg_recv)
    vg_own = pltpu.make_async_copy(relay.at[:, ci], vg_out.at[:, ci], local_sem.at[5])
    vg_own.start()
    vg_other = remote(
        relay.at[:, 1 - ci], vg_out.at[:, ci], pair_send.at[1], pair_recv.at[1], lat, other_core
    )
    vg_other.start()
    conv(x3_act, 1, keep_enc, low=3, high=4)
    enc_copy = pltpu.make_async_copy(enc, enc_out, local_sem.at[2])
    enc_copy.start()
    ar_finish(0, 6)
    ar_leave(0).start()
    embed_wait(2)
    embed_out[...] = etotal[...] * (1.0 / 512.0)
    for g in range(4):
        await_bytes(vals.at[pl.ds(0, 15 if g == 0 else 16)], a2a_send.at[g])
    for stage in range(3):
        meta_sent(stage)
    await_bytes(vg.at[pl.ds(0, 63)], vg_send)
    vg_own.wait()
    vg_other.wait()
    enc_copy.wait()
    ar_leave(1).wait()
    ar_leave(0).wait()


def hand_over(
    enc_in, vg_in, grads_in, embed_in, enc_out, vg_out, grads_out, embed_out,
    enc, vg, embed, narrow, wide, in_sem, out_sem,
):
    steps = []
    for i in range(6):
        src, dst = slice(i % 3 * PART, (i % 3 + 1) * PART), slice(i * 3 * CH, (i + 1) * 3 * CH)
        k = i // 3
        steps.append(
            (grads_in.at[k, src], narrow.at[k, src], wide.at[dst], grads_out.at[dst], (k, src, dst))
        )
    steps.append((enc_in, enc, enc, enc_out, None))
    steps.append((vg_in, vg, vg, vg_out, None))
    steps.append((embed_in, embed, embed, embed_out, None))
    moves = [
        pltpu.make_async_copy(step[0], step[1], in_sem.at[i]) for i, step in enumerate(steps)
    ]
    for move in moves:
        move.start()
    results = []
    for i, (_, _, src, dst, at) in enumerate(steps):
        moves[i].wait()
        if at is not None:
            k, rows, to = at
            for n in range(6):
                half = slice(rows.start + n * CH, rows.start + n * CH + CH)
                into = slice(to.start + n // 2 * CH, to.start + (n // 2 + 1) * CH)
                lanes = slice(n % 2 * 128, n % 2 * 128 + 128)
                wide[into, lanes] = narrow[k, half, :].astype(F32) * (1.0 / 512.0)
        results.append(pltpu.make_async_copy(src, dst, out_sem.at[i]))
        results[i].start()
    for copy in results:
        copy.wait()


def on_device(
    obs_values, obs_cells, obs_subcell, slot_counts, sharpness, embed_weight, conv_weight, cotangent
):
    anywhere = pl.BlockSpec(memory_space=pl.ANY)
    vmem = pl.BlockSpec(memory_space=pltpu.VMEM)
    grid = (ROWS, COLS, CH)
    wide = (ROWS + 2, COLS, 3 * CH)
    dma = pltpu.SemaphoreType.DMA
    scratch = [
        pltpu.VMEM((64, 2, CAP, VALS), BF16),
        pltpu.VMEM((64, 2, CAP, VALS), BF16),
        pltpu.VMEM((64, 2, CAP, VALS), BF16),
        pltpu.VMEM((4, 32, 1, 128), F32),
        pltpu.VMEM((4, 4, 8, 1, 128), F32),
        pltpu.VMEM((4, 4, 4, 2, 1, 128), F32),
        pltpu.VMEM((8, 4, 4, 1, 128), F32),
        pltpu.VMEM((GROUP, 128), BF16),
        pltpu.VMEM((OBS, 128), BF16),
        pltpu.VMEM((OBS, 128), BF16),
        pltpu.VMEM((OBS, CH), F32),
        pltpu.VMEM((GROUP, CH), BF16),
        pltpu.VMEM((GROUP, 256), BF16),
        pltpu.VMEM((COLS, GROUP), BF16),
        pltpu.VMEM((16, GROUP), F32),
        pltpu.VMEM((CELLS, CH), F32),
        pltpu.VMEM((COLS, 256), F32),
        pltpu.VMEM(grid, F32),
        pltpu.VMEM(grid, BF16),
        pltpu.VMEM((2, 3, 3 * CH, CH), BF16),
        pltpu.VMEM((CH, VALS), BF16),
        pltpu.VMEM(grid, F32),
        pltpu.VMEM(grid, F32),
        pltpu.VMEM(grid, BF16),
        pltpu.VMEM(grid, BF16),
        pltpu.VMEM(grid, BF16),
        pltpu.VMEM(grid, BF16),
        pltpu.VMEM(grid, BF16),
        pltpu.VMEM((CELLS, CH), BF16),
        pltpu.VMEM((CH, CELLS), BF16),
        pltpu.VMEM((CH, CELLS), BF16),
        pltpu.VMEM(wide, BF16),
        pltpu.VMEM(wide, BF16),
        pltpu.VMEM(wide, BF16),
        pltpu.VMEM((4, 2 * COLS + 6 * 16, CH), BF16),
        pltpu.VMEM((4, 2, 16, CH), BF16),
        pltpu.VMEM((2, 16, CH), F32),
        pltpu.VMEM((64, 2, CAP, VALS), BF16),
        pltpu.VMEM((2, 3, 2, HALF, 128), BF16),
        pltpu.VMEM((2, 3, 2, HALF, 128), BF16),
        pltpu.VMEM((2, 3, HALF, 128), BF16),
        pltpu.VMEM((2, 3, HALF, 128), BF16),
        pltpu.VMEM((2, 3, 3, QUARTER, 128), BF16),
        pltpu.VMEM((2, 3, QUARTER, 128), BF16),
        pltpu.VMEM((2, 3, 3, SHARD, 128), BF16),
        pltpu.VMEM((2, 3, SHARD, 128), BF16),
        pltpu.VMEM((2, 3, 4, SHARD, 128), BF16),
        pltpu.VMEM((VALS, CH), F32),
        pltpu.VMEM((7, 16, CH), F32),
        pltpu.VMEM((16, 16, CH), F32),
        pltpu.VMEM((VALS, CH), F32),
        pltpu.VMEM(grid, BF16),
        dma((7,)),
        dma((2,)),
        dma((2,)),
        dma((4,)),
        dma((4,)),
        dma((3,)),
        dma((3,)),
        dma,
        dma,
        dma((4,)),
        dma((4,)),
        dma((2, 7)),
        dma((2, 7)),
        dma((3,)),
        dma((3,)),
    ]
    encoded, value_grads, grads, embed_total = pl.pallas_call(
        kernel,
        out_shape=(
            jax.ShapeDtypeStruct(grid, BF16),
            jax.ShapeDtypeStruct((64, 2, CAP, VALS), BF16),
            jax.ShapeDtypeStruct((2, 3, 2, HALF, 128), BF16),
            jax.ShapeDtypeStruct((VALS, CH), F32),
        ),
        in_specs=[anywhere, vmem, vmem, vmem, vmem, vmem, anywhere, anywhere],
        out_specs=(anywhere, anywhere, anywhere, vmem),
        scratch_shapes=scratch,
        compiler_params=pltpu.CompilerParams(
            collective_id=0, has_side_effects=True, vmem_limit_bytes=60 * 1024 * 1024
        ),
        cost_estimate=pl.CostEstimate(
            flops=30_000_000_000, bytes_accessed=20_000_000, transcendentals=4_000_000
        ),
    )(
        obs_values.reshape(64, 2, CAP, VALS),
        obs_cells.reshape(32, 128),
        obs_subcell.reshape(32, 128),
        slot_counts,
        sharpness.reshape(1, CH),
        embed_weight,
        conv_weight.reshape(2, 3, 3 * CH, CH),
        cotangent,
    )
    encoded, value_grads, conv_grads, embed_grads = pl.pallas_call(
        hand_over,
        out_shape=(
            jax.ShapeDtypeStruct(grid, BF16),
            jax.ShapeDtypeStruct((64, 2, CAP, VALS), BF16),
            jax.ShapeDtypeStruct((3 * PART, CH), F32),
            jax.ShapeDtypeStruct((VALS, CH), F32),
        ),
        in_specs=[anywhere] * 4,
        out_specs=(anywhere,) * 4,
        scratch_shapes=[
            pltpu.VMEM(grid, BF16),
            pltpu.VMEM((64, 2, CAP, VALS), BF16),
            pltpu.VMEM((VALS, CH), F32),
            pltpu.VMEM((2, 3 * PART, 128), BF16),
            pltpu.VMEM((3 * PART, CH), F32),
            dma((9,)),
            dma((9,)),
        ],
        compiler_params=pltpu.CompilerParams(vmem_limit_bytes=60 * 1024 * 1024),
    )(encoded, value_grads, grads.reshape(2, 3 * PART, 128), embed_total)
    return (
        encoded,
        value_grads.reshape(OBS, VALS),
        conv_grads.reshape(2, 3, 3, CH, CH),
        embed_grads,
    )


def solution(mesh):
    placed = (
        P(("lat", "lon"), None),
        P(("lat", "lon")),
        P(("lat", "lon")),
        P(("lat", "lon"), None),
        P(),
        P(),
        P(),
        P("lat", "lon", None),
    )
    return jax.shard_map(
        on_device,
        mesh=mesh,
        in_specs=placed,
        out_specs=(P("lat", "lon", None), P(("lat", "lon"), None), P(), P()),
        check_vma=False,
    )
```

```python
import jax
import jax.numpy as jnp
from jax import lax
from jax.experimental import pallas as pl
from jax.experimental.pallas import tpu as pltpu
from jax.sharding import PartitionSpec as P

F32 = jnp.float32
BF16 = jnp.bfloat16
N_LAT, N_LON = 4, 32
DEVICES = N_LAT * N_LON
CAP, VALS, CH = 32, 128, 256
ROWS, COLS = 16, 128
CELLS = ROWS * COLS
OBS = DEVICES * CAP
GROUP = 32 * CAP
PART, HALF, QUARTER, SHARD = 1536, 768, 192, 48
NT = (((1,), (1,)), ((), ()))
TN = (((0,), (0,)), ((), ()))


def dot(a, b):
    return jnp.dot(a, b, preferred_element_type=F32)


def iota(shape, axis):
    return lax.broadcasted_iota(jnp.int32, shape, axis)


def sigmoid(x):
    return 0.5 + 0.5 * jnp.tanh(0.5 * x)


def remote(src, dst, send, recv, lat, lon):
    return pltpu.make_async_remote_copy(
        src_ref=src,
        dst_ref=dst,
        send_sem=send,
        recv_sem=recv,
        device_id=(lat, lon),
        device_id_type=pl.DeviceIdType.MESH,
    )


def await_bytes(ref, sem):
    pltpu.make_async_copy(ref, ref, sem).wait()


def loop(low, high, body):
    def step(i, carry):
        body(i)
        return carry

    lax.fori_loop(low, high, step, 0)


def aligned(start, size, unit):
    return pl.ds(pl.multiple_of(start, unit), size)


def kernel(
    obs_in, cells, subs, live_counts, sharp, embed_w, conv_in, cot_in,
    enc_out, vg_out, grads_out, embed_out,
    vals, queue, relay, meta_own, meta_z, meta_x, meta, tmeta, colb, rowb, weight, ew, rk, colhot, rowl, placed, counts, inv,
    cot, conv_w, embed_t, back, bend, base, act_zero, mid, act_one, gmid, gp, act_t, zero_t,
    x3_act, x3_cot, x3_mid, halo, strip, stripf,
    vg, grads, total, p0, s1, p1, s2, p2, s3, p3, esum, pe, qe, etotal, enc,
    local_sem, pair_send, pair_recv, a2a_send, a2a_recv, meta_send, meta_recv, vg_send, vg_recv,
    halo_send, halo_recv, ar_send, ar_recv, em_send, em_recv,
):
    lat = lax.axis_index("lat")
    lon = lax.axis_index("lon")
    me = lat * N_LON + lon
    xi, yi, ci = lax.div(lon, 8), lax.rem(lax.div(lon, 2), 4), lax.rem(lon, 2)

    chip = lat * 16 + xi * 4 + yi
    yc = lax.rem(lon, 8)
    other_core = lon + 1 - 2 * ci

    to_x = [xi] + [lax.rem(xi + d, 4) for d in range(1, 4)]
    to_y = [yi] + [lax.rem(yi + d, 4) for d in range(1, 4)]
    to_z = [lat] + [lax.rem(lat + d, 4) for d in range(1, 4)]

    def offset(j):
        dx, dy = j // 4 % 4, j % 4
        return dx, dy, (j // 16 + 8 - dx - dy) % 4

    def source(j):
        dx, dy, dz = offset(j)
        return to_x[-dx % 4], to_y[-dy % 4], to_z[-dz % 4]

    barrier = pltpu.get_barrier_semaphore()

    cot_copy = pltpu.make_async_copy(cot_in, cot, local_sem.at[0])
    cot_copy.start()
    pair_own = pltpu.make_async_copy(obs_in.at[:, ci], queue.at[:, ci], local_sem.at[4])
    pair_own.start()
    pair_other = remote(
        obs_in.at[:, 1 - ci], queue.at[:, ci], pair_send.at[0], pair_recv.at[0], lat, other_core
    )

    def signal(tlat, tlon):
        pl.semaphore_signal(
            barrier, inc=1, device_id=(tlat, tlon), device_id_type=pl.DeviceIdType.MESH
        )

    for j in range(1, 64):
        signal(to_z[j // 4 % 4], to_x[j // 16] * 8 + to_y[j % 4] * 2 + ci)
    beside = lax.rem(lon + N_LON - 1 + 2 * ci, N_LON)
    for turn in (0, 1, 3):
        signal(to_z[turn], other_core)
        signal(to_z[turn], beside)
    for d in range(1, 4):
        signal(lat, xi * 8 + to_y[d] * 2 + 1 - ci)

    def meta_copies(stage):
        copies = []
        for d in range(1, 8 if stage == 2 else 4):
            if stage == 0:
                c = lax.rem(lat + d, 4)
                src, dst, target = meta_own.at[:, pl.ds(c * 8, 8)], meta_z.at[lat], (c, lon)
            elif stage == 1:
                c = lax.rem(xi + d, 4)
                src, dst = meta_z.at[:, :, pl.ds(c * 2, 2)], meta_x.at[xi]
                target = (lat, c * 8 + yc)
            else:
                c = lax.rem(yc + d, 8)
                src, dst = meta_x.at[:, :, lax.rem(c, 4), lax.div(c, 4)], meta.at[yc]
                target = (lat, xi * 8 + c)
            copies.append(remote(src, dst, meta_send.at[stage], meta_recv.at[stage], *target))
        own = (
            (meta_own.at[:, pl.ds(lat * 8, 8)], meta_z.at[lat]),
            (meta_z.at[:, :, pl.ds(xi * 2, 2)], meta_x.at[xi]),
            (meta_x.at[:, :, lax.rem(yc, 4), lax.div(yc, 4)], meta.at[yc]),
        )[stage]
        copies.append(pltpu.make_async_copy(*own, meta_recv.at[stage]))
        return copies

    def meta_start(stage):
        for copy in meta_copies(stage):
            copy.start()

    def meta_wait(stage):
        await_bytes((meta_z, meta_x, meta)[stage], meta_recv.at[stage])

    def meta_sent(stage):
        await_bytes((meta_z, meta_x, meta)[stage].at[pl.ds(0, (3, 3, 7)[stage])], meta_send.at[stage])

    conv_copy = pltpu.make_async_copy(conv_in, conv_w, local_sem.at[1])
    conv_copy.start()

    def send_slot(j):
        dx, dy, dz = offset(j)
        tx, ty, tz = to_x[dx], to_y[dy], to_z[dz]
        g = j // 16
        remote(
            queue.at[tz * 16 + tx * 4 + ty], vals.at[j], a2a_send.at[g], a2a_recv.at[g],
            tz, tx * 8 + ty * 2 + ci,
        ).start()

    north, south = lax.rem(lat + 3, N_LAT), lax.rem(lat + 1, N_LAT)
    west, east = lax.rem(lon + N_LON - 1, N_LON), lax.rem(lon + 1, N_LON)

    def halo_row(k, side):
        return halo.at[k, side * COLS : (side + 1) * COLS]

    def halo_col(k, side, turn):
        at = 2 * COLS + 16 * (3 * side + turn)
        return halo.at[k, at : at + 16]

    def halo_copies(src, k):
        pieces = [(src.at[ROWS - 1], halo_row(k, 0), south, lon)]
        pieces.append((src.at[0], halo_row(k, 1), north, lon))
        for side, column, target in ((0, 1, east), (1, 0, west)):
            for turn, tlat in enumerate((lat, south, north)):
                pieces.append((strip.at[k, column], halo_col(k, side, turn), tlat, target))
        return [remote(s, d, halo_send.at[k], halo_recv.at[k], a, b) for s, d, a, b in pieces]

    def halo_pack(src, k):
        for r in range(ROWS):
            stripf[0, r : r + 1, :] = src[r, 0:16, :].astype(F32)[0:1, :]
            stripf[1, r : r + 1, :] = src[r, COLS - 16 : COLS, :].astype(F32)[15:16, :]
        strip[k, 0] = stripf[0].astype(BF16)
        strip[k, 1] = stripf[1].astype(BF16)

    def halo_start(src, k):
        for copy in halo_copies(src, k):
            copy.start()

    def widen(src, x3, low=0, high=4):
        def body(b):
            for i in range(4):
                r = 4 * b + i
                row = src[r].astype(F32)
                x3[r + 1, :, 0:CH] = pltpu.roll(row, 1, 0).astype(BF16)
                x3[r + 1, :, CH : 2 * CH] = src[r]
                x3[r + 1, :, 2 * CH : 3 * CH] = pltpu.roll(row, COLS - 1, 0).astype(BF16)

        loop(low, high, body)

    def halo_finish(src, k, x3):
        await_bytes(halo.at[k], halo_recv.at[k])
        await_bytes(halo.at[k], halo_send.at[k])
        first = iota((16, CH), 0) == 0
        last = iota((16, CH), 0) == 15
        left = halo_col(k, 0, 0)[...].astype(F32)
        right = halo_col(k, 1, 0)[...].astype(F32)
        for r in range(ROWS):
            low = x3[r + 1, 0:16, 0:CH].astype(F32)
            x3[r + 1, 0:16, 0:CH] = jnp.where(first, left[r : r + 1, :], low).astype(BF16)
            high = x3[r + 1, COLS - 16 : COLS, 2 * CH : 3 * CH].astype(F32)
            x3[r + 1, COLS - 16 : COLS, 2 * CH : 3 * CH] = jnp.where(
                last, right[r : r + 1, :], high
            ).astype(BF16)
        spot = iota((COLS, CH), 0)
        for side, r, turn, pick, valid in (
            (0, 0, 1, ROWS - 1, lat > 0),
            (1, ROWS + 1, 2, 0, lat < N_LAT - 1),
        ):
            keep = jnp.where(valid, 1.0, 0.0).astype(F32)
            row = halo_row(k, side)[...].astype(F32) * keep
            lcorner = halo_col(k, 0, turn)[...].astype(F32)[pick : pick + 1, :] * keep
            rcorner = halo_col(k, 1, turn)[...].astype(F32)[pick : pick + 1, :] * keep
            x3[r, :, 0:CH] = jnp.where(spot == 0, lcorner, pltpu.roll(row, 1, 0)).astype(BF16)
            x3[r, :, CH : 2 * CH] = row.astype(BF16)
            x3[r, :, 2 * CH : 3 * CH] = jnp.where(
                spot == COLS - 1, rcorner, pltpu.roll(row, COLS - 1, 0)
            ).astype(BF16)

    def conv(x3, k, finish, flip=False, low=0, high=4):
        if flip:
            taps = [
                conv_w[k, 2 - p, (2 - q) * CH : (3 - q) * CH, :] for p in range(3) for q in range(3)
            ]
            taps = jnp.concatenate(taps, axis=1)
        else:
            taps = conv_w[k].reshape(9 * CH, CH)
        for b in range(low, high):
            near = [x3[4 * b + p : 4 * b + p + 4].reshape(4 * COLS, 3 * CH) for p in range(3)]
            near = jnp.concatenate(near, axis=1)
            if flip:
                acc = lax.dot_general(near, taps, NT, preferred_element_type=F32)
            else:
                acc = dot(near, taps)
            finish(slice(4 * b, 4 * b + 4), acc)

    def tile4(x):
        return x.reshape(4 * COLS, CH)

    def grid4(x):
        return x.reshape(4, COLS, CH)

    def turn_act(act, act_t):
        for r in range(ROWS):
            act_t[:, r * COLS : (r + 1) * COLS] = act[r].T

    def own_meta():
        line, lane = iota((32, 128), 0), iota((32, 128), 1)
        own_four = jnp.where(lax.div(lane, 4) == line, live_counts[...].astype(F32), 0.0).astype(BF16)
        to_slots = jnp.where(
            lax.rem(iota((128, 128), 0), 4) == lax.div(iota((128, 128), 1), 32), 1.0, 0.0
        ).astype(BF16)
        live = lax.rem(lane, 32).astype(F32) < dot(own_four, to_slots)
        cell, sub = cells[...], subs[...]
        u, v = sub >> 3, sub & 7
        u = jnp.where(u >= 4, u - 4, 3 - u)
        v = jnp.where(v >= 4, v - 4, 3 - v)
        row = cell >> 7
        fields = [
            jnp.where(live, (cell & 127).astype(F32), 255.0),
            (row * 16 + u * 4 + v).astype(F32),
            ((2 * u + 1) * (2 * u + 1) + (2 * v + 1) * (2 * v + 1)).astype(F32),
            row.astype(F32),
        ]
        for i in range(4):
            mixed = jnp.zeros((32, 128), F32)
            for f in range(4):
                shift = (f - i) * 32 % 128
                turned_field = pltpu.roll(fields[f], shift, 1) if shift else fields[f]
                mixed = jnp.where(lax.div(lane, 32) == f, turned_field, mixed)
            for r in range(32):
                meta_own[i, r] = mixed[r : r + 1, :]

    pl.semaphore_wait(barrier, 72)
    pair_other.start()
    own_meta()
    meta_start(0)
    cot_copy.wait()
    halo_pack(cot, 0)
    halo_start(cot, 0)
    meta_wait(0)
    meta_start(1)
    widen(cot, x3_cot, 0, 2)
    pair_own.wait()
    pair_other.wait()
    pltpu.make_async_copy(queue.at[chip], vals.at[0], a2a_recv.at[0]).start()
    for j in range(1, 16):
        send_slot(j)
    meta_wait(1)
    meta_start(2)
    for j in range(16, 64):
        send_slot(j)
    widen(cot, x3_cot, 2, 4)
    conv_copy.wait()
    embed_t[...] = embed_w[...].T
    halo_finish(cot, 0, x3_cot)

    def keep_back(rows, acc):
        back[rows] = grid4(acc)

    conv(x3_cot, 1, keep_back, flip=True)
    meta_wait(2)

    placed[...] = jnp.zeros_like(placed)
    counts[...] = jnp.zeros_like(counts)
    slot_mask = jnp.where(
        lax.rem(iota((CAP, 128), 1), 32) == iota((CAP, 128), 0), 1.0, 0.0
    ).astype(F32)
    spread = jnp.where(
        lax.div(iota((128, 512), 0), 32) == lax.div(iota((128, 512), 1), 128), 1.0, 0.0
    ).astype(BF16)
    lane, line = iota((COLS + 16, 128), 1), iota((COLS + 16, 128), 0)
    pick = jnp.where(lax.div(lane, 32) == jnp.where(line < COLS, 0, 3), 1.0, 0.0).astype(BF16)
    decay = sharp[...] * (-1.0 / 256.0)

    for g in range(4):
        for s in range(32):
            sx, sy, sz = source(g * 16 + s // 2)
            line = jnp.broadcast_to(meta[sy * 2 + s % 2, sx, sz], (CAP, 128)) * slot_mask
            tmeta[s * CAP : s * CAP + CAP, :] = line.astype(BF16)
        await_bytes(vals.at[pl.ds(g * 16, 16)], a2a_recv.at[g])

        for b in range(4):
            at = slice(b * 256, b * 256 + 256)
            of = slice(g * GROUP + b * 256, g * GROUP + b * 256 + 256)
            wide = dot(tmeta[at, :], spread)
            colb[of, :] = wide[:, 0:128].astype(BF16)
            rowb[of, :] = wide[:, 384:512].astype(BF16)
            rk_of = jnp.concatenate([wide[:, 128:256]] * 2, axis=1)
            radius = jnp.concatenate([wide[:, 256:384]] * 2, axis=1)
            rk[at, :] = jnp.where(
                rk_of == iota((256, 256), 1).astype(F32), 1.0, 0.0
            ).astype(BF16)
            w = jnp.exp(radius * decay)
            weight[of, :] = w
            ew[at, :] = (dot(vals[g * 16 + 4 * b : g * 16 + 4 * b + 4].reshape(256, VALS), embed_w[...]) * w).astype(BF16)

        both = lax.dot_general(pick, tmeta[...], NT, preferred_element_type=F32)
        colhot[...] = jnp.where(
            both[0:COLS] == iota((COLS, GROUP), 0).astype(F32), 1.0, 0.0
        ).astype(BF16)
        rowl[...] = both[COLS : COLS + 16]
        counts[...] += dot(colhot[...], rk[...])

        hot = colhot[...].reshape(8, 16, GROUP)
        for b in range(4):
            rows = []
            for r in range(4 * b, 4 * b + 4):
                mask = jnp.where(rowl[...] == float(r), 1.0, 0.0).astype(BF16)
                rows.append((hot * mask[None]).reshape(COLS, GROUP))
            at = slice(b * 512, b * 512 + 512)
            placed[at, :] += dot(jnp.concatenate(rows, axis=0), ew[...])

    kind = lax.rem(iota((256, CH), 0), 16)
    half_u, half_v = 2 * lax.div(kind, 4) + 1, 2 * lax.rem(kind, 4) + 1
    table = jnp.exp((half_u * half_u + half_v * half_v).astype(F32) * decay)
    table_hi = table.astype(BF16)
    table_lo = (table - table_hi.astype(F32)).astype(BF16)
    tables = jnp.concatenate([table_hi, table_lo], axis=0)
    row_of_lane = lax.div(iota((COLS, 256), 1), 16)
    for b in range(4):
        rows = []
        for r in range(4 * b, 4 * b + 4):
            rows.append(jnp.where(row_of_lane == r, counts[...], 0.0).astype(BF16))
        tally = jnp.concatenate(rows, axis=0)
        recip = 1.0 / (dot(jnp.concatenate([tally, tally], axis=1), tables) + 1.0)
        at = slice(4 * b, 4 * b + 4)
        inv[at] = grid4(recip)
        value = (placed[b * 512 : b * 512 + 512, :] * recip).astype(BF16)
        base[at] = grid4(value)
        x = value.astype(F32)
        s = sigmoid(x)
        act_zero[at] = grid4((x * s).astype(BF16))
        bend[at] = grid4(s * (1.0 + x * (1.0 - s)))

    halo_pack(act_zero, 1)
    halo_start(act_zero, 1)
    widen(act_zero, x3_act)
    turn_act(act_zero, zero_t)
    halo_finish(act_zero, 1, x3_act)

    def keep_mid(rows, acc):
        value = (tile4(base[rows]).astype(F32) + acc).astype(BF16)
        mid[rows] = grid4(value)
        x = value.astype(F32)
        s = sigmoid(x)
        act_one[rows] = grid4((x * s).astype(BF16))
        slope = s * (1.0 + x * (1.0 - s))
        grad = tile4(cot[rows]).astype(F32) + tile4(back[rows]) * slope
        gmid[rows] = grid4(grad.astype(BF16))

    conv(x3_act, 0, keep_mid)
    halo_pack(gmid, 2)
    halo_start(gmid, 2)
    halo_pack(act_one, 3)
    halo_start(act_one, 3)

    def kernel_grad(act_t, x3, k):
        for p in range(3):
            block = dot(act_t[...], x3[2 - p : 2 - p + ROWS].reshape(CELLS, 3 * CH))
            for q in range(3):
                for h in range(2):
                    n, lanes = 6 * p + 2 * q + h, (2 - q) * CH + h * 128
                    at = n % 3 * CH
                    grads[k, n // 6, n // 3 % 2, at : at + CH, :] = block[
                        :, lanes : lanes + 128
                    ].astype(BF16)

    coords = {"x": xi, "y": yi, "z": lat}
    orders = (("x", "y", "z"), ("y", "z", "x"), ("z", "x", "y"))

    def along(axis, c):
        cx, cy, cz = [c if axis == n else coords[n] for n in ("x", "y", "z")]
        return cz, cx * 8 + cy * 2 + ci

    def turned(axis, d):
        return {"x": to_x, "y": to_y, "z": to_z}[axis][d]

    def part_copies(k, stage):
        sems = (ar_send.at[k, stage], ar_recv.at[k, stage])
        if stage == 0:
            return [remote(grads.at[k, :, 1 - ci], p0.at[k], *sems, lat, other_core)]
        if stage == 6:
            half = total.at[k, :, ci]
            return [remote(half, half, *sems, lat, other_core)]
        copies = []
        for a, order in enumerate(orders):
            quarter = coords[order[0]] * QUARTER
            shard = quarter + coords[order[1]] * SHARD
            axis = order[{1: 0, 2: 1, 3: 2, 4: 1, 5: 0}[stage]]
            for d in (1, 3, 2):
                c = turned(axis, d)
                if stage == 1:
                    src, dst = s1.at[k, a, aligned(c * QUARTER, QUARTER, 16)], p1.at[k, a, d - 1]
                elif stage == 2:
                    src, dst = s2.at[k, a, aligned(c * SHARD, SHARD, 16)], p2.at[k, a, d - 1]
                elif stage == 3:
                    src, dst = s3.at[k, a], p3.at[k, a, coords[axis]]
                elif stage == 4:
                    src = dst = total.at[k, a, ci, aligned(shard, SHARD, 16)]
                else:
                    src = dst = total.at[k, a, ci, aligned(quarter, QUARTER, 16)]
                copies.append(remote(src, dst, *sems, *along(axis, c)))
        return copies

    def ar_start(k, stage):
        for copy in part_copies(k, stage):
            copy.start()

    def ar_finish(k, stage):
        amount = (p0, p1, p2, p2, p2, p1, p0)[stage].at[k]
        await_bytes(amount, ar_recv.at[k, stage])
        await_bytes(amount, ar_send.at[k, stage])
        for a, order in enumerate(orders):
            if stage == 0:
                here = grads[k, a, ci].astype(F32)
                s1[k, a] = (here + p0[k, a].astype(F32)).astype(BF16)
            elif stage in (1, 2):
                size = QUARTER if stage == 1 else SHARD
                src, came, dst = (s1, p1, s2) if stage == 1 else (s2, p2, s3)
                at = aligned(coords[order[stage - 1]] * size, size, 16)
                here = src[k, a, at, :].astype(F32)
                for d in range(3):
                    here += came[k, a, d].astype(F32)
                dst[k, a] = here.astype(BF16)
            elif stage == 3:
                p3[k, a, coords[order[2]]] = s3[k, a]
                whole = p3[k, a, 0].astype(F32)
                for d in range(1, 4):
                    whole += p3[k, a, d].astype(F32)
                quarter = coords[order[0]] * QUARTER
                at = aligned(quarter + coords[order[1]] * SHARD, SHARD, 16)
                total[k, a, ci, at, :] = whole.astype(BF16)

    def ar_step(k, stage):
        ar_finish(k, stage)
        ar_start(k, stage + 1)

    def ar_leave(k):
        return pltpu.make_async_copy(total.at[k], grads_out.at[k], local_sem.at[3 if k else 6])

    turn_act(act_one, act_t)
    kernel_grad(act_t, x3_cot, 1)
    ar_start(1, 0)
    widen(gmid, x3_mid)
    halo_finish(gmid, 2, x3_mid)
    ar_step(1, 0)
    kernel_grad(zero_t, x3_mid, 0)
    ar_start(0, 0)

    def keep_gp(rows, acc):
        grad = tile4(gmid[rows]).astype(F32) + acc * tile4(bend[rows])
        gp[rows.start * COLS : rows.stop * COLS, :] = (
            grad * tile4(inv[rows])
        ).astype(BF16)

    conv(x3_mid, 0, keep_gp, flip=True, low=0, high=2)
    ar_step(1, 1)
    ar_step(0, 0)
    conv(x3_mid, 0, keep_gp, flip=True, low=2, high=4)

    esum[...] = jnp.zeros_like(esum)

    def vg_copy(j):
        sx, sy, sz = source(j)
        return remote(vg.at[j], relay.at[chip], vg_send, vg_recv, sz, sx * 8 + sy * 2 + ci)

    def gather(b):
        at = slice(b * 512, b * 512 + 512)
        chips = slice(b * 8, b * 8 + 8)
        hot = jnp.where(
            colb[at, :].astype(F32) == iota((512, COLS), 1).astype(F32), 1.0, 0.0
        ).astype(BF16)
        row_of = rowb[at, :]
        pieces = [
            jnp.where(row_of == jnp.array(r, BF16), hot, jnp.zeros_like(hot)) for r in range(ROWS)
        ]
        found = dot(jnp.concatenate(pieces, axis=1), gp[...])
        grad = (found * weight[at, :]).astype(BF16)
        vg[chips] = dot(grad, embed_t[...]).astype(BF16).reshape(8, 2, CAP, VALS)
        own = vals[chips].reshape(512, VALS)
        esum[...] += lax.dot_general(own, grad, TN, preferred_element_type=F32)
        for j in range(8 * b, 8 * b + 8):
            if j == 0:
                pltpu.make_async_copy(vg.at[0], relay.at[chip], vg_recv).start()
            else:
                vg_copy(j).start()

    gather(0)
    gather(1)
    ar_step(1, 2)
    gather(2)
    ar_step(0, 1)
    gather(3)
    ar_step(1, 3)
    gather(4)
    ar_step(0, 2)
    gather(5)
    ar_step(1, 4)
    gather(6)
    ar_step(0, 3)
    gather(7)
    ar_step(0, 4)

    member = yc
    column = xi * 4 + lat

    def embed_copies(stage):
        copies = []
        for d in range(1, 16 if stage == 1 else 8):
            if stage == 1:
                c = lax.rem(column + d, 16)
                tlat, tlon = lax.rem(c, 4), lax.div(c, 4) * 8 + member
                src, dst = esum.at[aligned(member * 16, 16, 16)], qe.at[column]
            else:
                m = lax.rem(member + d, 8)
                tlat, tlon = lat, xi * 8 + m
                if stage == 0:
                    src, dst = esum.at[aligned(m * 16, 16, 16)], pe.at[d - 1]
                else:
                    src = dst = etotal.at[aligned(member * 16, 16, 16)]
            copies.append(remote(src, dst, em_send.at[stage], em_recv.at[stage], tlat, tlon))
        return copies

    def embed_start(stage):
        for copy in embed_copies(stage):
            copy.start()

    def embed_wait(stage):
        amount = qe.at[pl.ds(0, 15)] if stage == 1 else pe
        await_bytes(amount, em_recv.at[stage])
        await_bytes(amount, em_send.at[stage])

    embed_start(0)
    widen(act_one, x3_act)
    halo_finish(act_one, 3, x3_act)

    def keep_enc(rows, acc):
        enc[rows] = grid4((tile4(mid[rows]).astype(F32) + acc).astype(BF16))

    conv(x3_act, 1, keep_enc, low=0, high=1)
    ar_step(1, 5)
    embed_wait(0)
    own_rows = aligned(member * 16, 16, 16)
    mine = esum[own_rows, :]
    for d in range(7):
        mine += pe[d]
    esum[own_rows, :] = mine
    embed_start(1)
    conv(x3_act, 1, keep_enc, low=1, high=2)
    ar_step(0, 5)
    conv(x3_act, 1, keep_enc, low=2, high=3)
    ar_finish(1, 6)
    ar_leave(1).start()
    embed_wait(1)
    qe[column] = esum[own_rows, :]
    whole = qe[0]
    for d in range(1, 16):
        whole += qe[d]
    etotal[own_rows, :] = whole
    embed_start(2)
    await_bytes(relay, vg_recv)
    vg_own = pltpu.make_async_copy(relay.at[:, ci], vg_out.at[:, ci], local_sem.at[5])
    vg_own.start()
    vg_other = remote(
        relay.at[:, 1 - ci], vg_out.at[:, ci], pair_send.at[1], pair_recv.at[1], lat, other_core
    )
    vg_other.start()
    conv(x3_act, 1, keep_enc, low=3, high=4)
    enc_copy = pltpu.make_async_copy(enc, enc_out, local_sem.at[2])
    enc_copy.start()
    ar_finish(0, 6)
    ar_leave(0).start()
    embed_wait(2)
    embed_out[...] = etotal[...] * (1.0 / 512.0)
    for g in range(4):
        await_bytes(vals.at[pl.ds(0, 15 if g == 0 else 16)], a2a_send.at[g])
    for stage in range(3):
        meta_sent(stage)
    await_bytes(vg.at[pl.ds(0, 63)], vg_send)
    vg_own.wait()
    vg_other.wait()
    enc_copy.wait()
    ar_leave(1).wait()
    ar_leave(0).wait()


def hand_over(
    enc_in, vg_in, grads_in, embed_in, enc_out, vg_out, grads_out, embed_out,
    enc, vg, embed, narrow, wide, in_sem, out_sem,
):
    steps = []
    for i in range(6):
        src, dst = slice(i % 3 * PART, (i % 3 + 1) * PART), slice(i * 3 * CH, (i + 1) * 3 * CH)
        k = i // 3
        steps.append(
            (grads_in.at[k, src], narrow.at[k, src], wide.at[dst], grads_out.at[dst], (k, src, dst))
        )
    steps.append((enc_in, enc, enc, enc_out, None))
    steps.append((vg_in, vg, vg, vg_out, None))
    steps.append((embed_in, embed, embed, embed_out, None))
    moves = [
        pltpu.make_async_copy(step[0], step[1], in_sem.at[i]) for i, step in enumerate(steps)
    ]
    for move in moves:
        move.start()
    results = []
    for i, (_, _, src, dst, at) in enumerate(steps):
        moves[i].wait()
        if at is not None:
            k, rows, to = at
            for n in range(6):
                half = slice(rows.start + n * CH, rows.start + n * CH + CH)
                into = slice(to.start + n // 2 * CH, to.start + (n // 2 + 1) * CH)
                lanes = slice(n % 2 * 128, n % 2 * 128 + 128)
                wide[into, lanes] = narrow[k, half, :].astype(F32) * (1.0 / 512.0)
        results.append(pltpu.make_async_copy(src, dst, out_sem.at[i]))
        results[i].start()
    for copy in results:
        copy.wait()


def on_device(
    obs_values, obs_cells, obs_subcell, slot_counts, sharpness, embed_weight, conv_weight, cotangent
):
    anywhere = pl.BlockSpec(memory_space=pl.ANY)
    vmem = pl.BlockSpec(memory_space=pltpu.VMEM)
    grid = (ROWS, COLS, CH)
    wide = (ROWS + 2, COLS, 3 * CH)
    dma = pltpu.SemaphoreType.DMA
    scratch = [
        pltpu.VMEM((64, 2, CAP, VALS), BF16),
        pltpu.VMEM((64, 2, CAP, VALS), BF16),
        pltpu.VMEM((64, 2, CAP, VALS), BF16),
        pltpu.VMEM((4, 32, 1, 128), F32),
        pltpu.VMEM((4, 4, 8, 1, 128), F32),
        pltpu.VMEM((4, 4, 4, 2, 1, 128), F32),
        pltpu.VMEM((8, 4, 4, 1, 128), F32),
        pltpu.VMEM((GROUP, 128), BF16),
        pltpu.VMEM((OBS, 128), BF16),
        pltpu.VMEM((OBS, 128), BF16),
        pltpu.VMEM((OBS, CH), F32),
        pltpu.VMEM((GROUP, CH), BF16),
        pltpu.VMEM((GROUP, 256), BF16),
        pltpu.VMEM((COLS, GROUP), BF16),
        pltpu.VMEM((16, GROUP), F32),
        pltpu.VMEM((CELLS, CH), F32),
        pltpu.VMEM((COLS, 256), F32),
        pltpu.VMEM(grid, F32),
        pltpu.VMEM(grid, BF16),
        pltpu.VMEM((2, 3, 3 * CH, CH), BF16),
        pltpu.VMEM((CH, VALS), BF16),
        pltpu.VMEM(grid, F32),
        pltpu.VMEM(grid, F32),
        pltpu.VMEM(grid, BF16),
        pltpu.VMEM(grid, BF16),
        pltpu.VMEM(grid, BF16),
        pltpu.VMEM(grid, BF16),
        pltpu.VMEM(grid, BF16),
        pltpu.VMEM((CELLS, CH), BF16),
        pltpu.VMEM((CH, CELLS), BF16),
        pltpu.VMEM((CH, CELLS), BF16),
        pltpu.VMEM(wide, BF16),
        pltpu.VMEM(wide, BF16),
        pltpu.VMEM(wide, BF16),
        pltpu.VMEM((4, 2 * COLS + 6 * 16, CH), BF16),
        pltpu.VMEM((4, 2, 16, CH), BF16),
        pltpu.VMEM((2, 16, CH), F32),
        pltpu.VMEM((64, 2, CAP, VALS), BF16),
        pltpu.VMEM((2, 3, 2, HALF, 128), BF16),
        pltpu.VMEM((2, 3, 2, HALF, 128), BF16),
        pltpu.VMEM((2, 3, HALF, 128), BF16),
        pltpu.VMEM((2, 3, HALF, 128), BF16),
        pltpu.VMEM((2, 3, 3, QUARTER, 128), BF16),
        pltpu.VMEM((2, 3, QUARTER, 128), BF16),
        pltpu.VMEM((2, 3, 3, SHARD, 128), BF16),
        pltpu.VMEM((2, 3, SHARD, 128), BF16),
        pltpu.VMEM((2, 3, 4, SHARD, 128), BF16),
        pltpu.VMEM((VALS, CH), F32),
        pltpu.VMEM((7, 16, CH), F32),
        pltpu.VMEM((16, 16, CH), F32),
        pltpu.VMEM((VALS, CH), F32),
        pltpu.VMEM(grid, BF16),
        dma((7,)),
        dma((2,)),
        dma((2,)),
        dma((4,)),
        dma((4,)),
        dma((3,)),
        dma((3,)),
        dma,
        dma,
        dma((4,)),
        dma((4,)),
        dma((2, 7)),
        dma((2, 7)),
        dma((3,)),
        dma((3,)),
    ]
    encoded, value_grads, grads, embed_total = pl.pallas_call(
        kernel,
        out_shape=(
            jax.ShapeDtypeStruct(grid, BF16),
            jax.ShapeDtypeStruct((64, 2, CAP, VALS), BF16),
            jax.ShapeDtypeStruct((2, 3, 2, HALF, 128), BF16),
            jax.ShapeDtypeStruct((VALS, CH), F32),
        ),
        in_specs=[anywhere, vmem, vmem, vmem, vmem, vmem, anywhere, anywhere],
        out_specs=(anywhere, anywhere, anywhere, vmem),
        scratch_shapes=scratch,
        compiler_params=pltpu.CompilerParams(
            collective_id=0, has_side_effects=True, vmem_limit_bytes=60 * 1024 * 1024
        ),
        cost_estimate=pl.CostEstimate(
            flops=30_000_000_000, bytes_accessed=20_000_000, transcendentals=4_000_000
        ),
    )(
        obs_values.reshape(64, 2, CAP, VALS),
        obs_cells.reshape(32, 128),
        obs_subcell.reshape(32, 128),
        slot_counts,
        sharpness.reshape(1, CH),
        embed_weight,
        conv_weight.reshape(2, 3, 3 * CH, CH),
        cotangent,
    )
    encoded, value_grads, conv_grads, embed_grads = pl.pallas_call(
        hand_over,
        out_shape=(
            jax.ShapeDtypeStruct(grid, BF16),
            jax.ShapeDtypeStruct((64, 2, CAP, VALS), BF16),
            jax.ShapeDtypeStruct((3 * PART, CH), F32),
            jax.ShapeDtypeStruct((VALS, CH), F32),
        ),
        in_specs=[anywhere] * 4,
        out_specs=(anywhere,) * 4,
        scratch_shapes=[
            pltpu.VMEM(grid, BF16),
            pltpu.VMEM((64, 2, CAP, VALS), BF16),
            pltpu.VMEM((VALS, CH), F32),
            pltpu.VMEM((2, 3 * PART, 128), BF16),
            pltpu.VMEM((3 * PART, CH), F32),
            dma((9,)),
            dma((9,)),
        ],
        compiler_params=pltpu.CompilerParams(vmem_limit_bytes=60 * 1024 * 1024),
    )(encoded, value_grads, grads.reshape(2, 3 * PART, 128), embed_total)
    return (
        encoded,
        value_grads.reshape(OBS, VALS),
        conv_grads.reshape(2, 3, 3, CH, CH),
        embed_grads,
    )


def solution(mesh):
    placed = (
        P(("lat", "lon"), None),
        P(("lat", "lon")),
        P(("lat", "lon")),
        P(("lat", "lon"), None),
        P(),
        P(),
        P(),
        P("lat", "lon", None),
    )
    return jax.shard_map(
        on_device,
        mesh=mesh,
        in_specs=placed,
        out_specs=(P("lat", "lon", None), P(("lat", "lon"), None), P(), P()),
        check_vma=False,
    )
```

```python
import jax
import jax.numpy as jnp
from jax import lax
from jax.experimental import pallas as pl
from jax.experimental.pallas import tpu as pltpu
from jax.sharding import PartitionSpec as P

F32 = jnp.float32
BF16 = jnp.bfloat16
N_LAT, N_LON = 4, 32
DEVICES = N_LAT * N_LON
CAP, VALS, CH = 32, 128, 256
ROWS, COLS = 16, 128
CELLS = ROWS * COLS
OBS = DEVICES * CAP
GROUP = 32 * CAP
PART, HALF, QUARTER, SHARD = 1536, 768, 192, 48
NT = (((1,), (1,)), ((), ()))
TN = (((0,), (0,)), ((), ()))


def dot(a, b):
    return jnp.dot(a, b, preferred_element_type=F32)


def iota(shape, axis):
    return lax.broadcasted_iota(jnp.int32, shape, axis)


def sigmoid(x):
    return 0.5 + 0.5 * jnp.tanh(0.5 * x)


def remote(src, dst, send, recv, lat, lon):
    return pltpu.make_async_remote_copy(
        src_ref=src,
        dst_ref=dst,
        send_sem=send,
        recv_sem=recv,
        device_id=(lat, lon),
        device_id_type=pl.DeviceIdType.MESH,
    )


def await_bytes(ref, sem):
    pltpu.make_async_copy(ref, ref, sem).wait()


def loop(low, high, body):
    def step(i, carry):
        body(i)
        return carry

    lax.fori_loop(low, high, step, 0)


def aligned(start, size, unit):
    return pl.ds(pl.multiple_of(start, unit), size)


def kernel(
    obs_in, cells, subs, live_counts, sharp, embed_w, conv_in, cot_in,
    enc_out, vg_out, grads_out, embed_out,
    vals, queue, relay, meta_own, meta_z, meta_x, meta, tmeta, colb, rowb, weight, ew, rk, colhot, rowl, placed, counts, inv,
    cot, conv_w, embed_t, back, bend, base, act_zero, mid, act_one, gmid, gp, act_t, zero_t,
    x3_act, x3_cot, x3_mid, halo, strip, stripf,
    vg, grads, total, p0, s1, p1, s2, p2, s3, p3, esum, pe, qe, etotal, enc,
    local_sem, pair_send, pair_recv, a2a_send, a2a_recv, meta_send, meta_recv, vg_send, vg_recv,
    halo_send, halo_recv, ar_send, ar_recv, em_send, em_recv,
):
    lat = lax.axis_index("lat")
    lon = lax.axis_index("lon")
    me = lat * N_LON + lon
    xi, yi, ci = lax.div(lon, 8), lax.rem(lax.div(lon, 2), 4), lax.rem(lon, 2)

    chip = lat * 16 + xi * 4 + yi
    yc = lax.rem(lon, 8)
    other_core = lon + 1 - 2 * ci

    to_x = [xi] + [lax.rem(xi + d, 4) for d in range(1, 4)]
    to_y = [yi] + [lax.rem(yi + d, 4) for d in range(1, 4)]
    to_z = [lat] + [lax.rem(lat + d, 4) for d in range(1, 4)]

    def offset(j):
        dx, dy = j // 4 % 4, j % 4
        return dx, dy, (j // 16 + 8 - dx - dy) % 4

    def source(j):
        dx, dy, dz = offset(j)
        return to_x[-dx % 4], to_y[-dy % 4], to_z[-dz % 4]

    barrier = pltpu.get_barrier_semaphore()

    cot_copy = pltpu.make_async_copy(cot_in, cot, local_sem.at[0])
    cot_copy.start()
    pair_own = pltpu.make_async_copy(obs_in.at[:, ci], queue.at[:, ci], local_sem.at[4])
    pair_own.start()
    pair_other = remote(
        obs_in.at[:, 1 - ci], queue.at[:, ci], pair_send.at[0], pair_recv.at[0], lat, other_core
    )

    def signal(tlat, tlon):
        pl.semaphore_signal(
            barrier, inc=1, device_id=(tlat, tlon), device_id_type=pl.DeviceIdType.MESH
        )

    for j in range(1, 64):
        signal(to_z[j // 4 % 4], to_x[j // 16] * 8 + to_y[j % 4] * 2 + ci)
    beside = lax.rem(lon + N_LON - 1 + 2 * ci, N_LON)
    for turn in (0, 1, 3):
        signal(to_z[turn], other_core)
        signal(to_z[turn], beside)
    for d in range(1, 4):
        signal(lat, xi * 8 + to_y[d] * 2 + 1 - ci)

    def meta_copies(stage):
        copies = []
        for d in range(1, 8 if stage == 2 else 4):
            if stage == 0:
                c = lax.rem(lat + d, 4)
                src, dst, target = meta_own.at[:, pl.ds(c * 8, 8)], meta_z.at[lat], (c, lon)
            elif stage == 1:
                c = lax.rem(xi + d, 4)
                src, dst = meta_z.at[:, :, pl.ds(c * 2, 2)], meta_x.at[xi]
                target = (lat, c * 8 + yc)
            else:
                c = lax.rem(yc + d, 8)
                src, dst = meta_x.at[:, :, lax.rem(c, 4), lax.div(c, 4)], meta.at[yc]
                target = (lat, xi * 8 + c)
            copies.append(remote(src, dst, meta_send.at[stage], meta_recv.at[stage], *target))
        own = (
            (meta_own.at[:, pl.ds(lat * 8, 8)], meta_z.at[lat]),
            (meta_z.at[:, :, pl.ds(xi * 2, 2)], meta_x.at[xi]),
            (meta_x.at[:, :, lax.rem(yc, 4), lax.div(yc, 4)], meta.at[yc]),
        )[stage]
        copies.append(pltpu.make_async_copy(*own, meta_recv.at[stage]))
        return copies

    def meta_start(stage):
        for copy in meta_copies(stage):
            copy.start()

    def meta_wait(stage):
        await_bytes((meta_z, meta_x, meta)[stage], meta_recv.at[stage])

    def meta_sent(stage):
        await_bytes((meta_z, meta_x, meta)[stage].at[pl.ds(0, (3, 3, 7)[stage])], meta_send.at[stage])

    conv_copy = pltpu.make_async_copy(conv_in, conv_w, local_sem.at[1])
    conv_copy.start()

    def send_slot(j):
        dx, dy, dz = offset(j)
        tx, ty, tz = to_x[dx], to_y[dy], to_z[dz]
        g = j // 16
        remote(
            queue.at[tz * 16 + tx * 4 + ty], vals.at[j], a2a_send.at[g], a2a_recv.at[g],
            tz, tx * 8 + ty * 2 + ci,
        ).start()

    north, south = lax.rem(lat + 3, N_LAT), lax.rem(lat + 1, N_LAT)
    west, east = lax.rem(lon + N_LON - 1, N_LON), lax.rem(lon + 1, N_LON)

    def halo_row(k, side):
        return halo.at[k, side * COLS : (side + 1) * COLS]

    def halo_col(k, side, turn):
        at = 2 * COLS + 16 * (3 * side + turn)
        return halo.at[k, at : at + 16]

    def halo_copies(src, k):
        pieces = [(src.at[ROWS - 1], halo_row(k, 0), south, lon)]
        pieces.append((src.at[0], halo_row(k, 1), north, lon))
        for side, column, target in ((0, 1, east), (1, 0, west)):
            for turn, tlat in enumerate((lat, south, north)):
                pieces.append((strip.at[k, column], halo_col(k, side, turn), tlat, target))
        return [remote(s, d, halo_send.at[k], halo_recv.at[k], a, b) for s, d, a, b in pieces]

    def halo_pack(src, k):
        for r in range(ROWS):
            stripf[0, r : r + 1, :] = src[r, 0:16, :].astype(F32)[0:1, :]
            stripf[1, r : r + 1, :] = src[r, COLS - 16 : COLS, :].astype(F32)[15:16, :]
        strip[k, 0] = stripf[0].astype(BF16)
        strip[k, 1] = stripf[1].astype(BF16)

    def halo_start(src, k):
        for copy in halo_copies(src, k):
            copy.start()

    def widen(src, x3, low=0, high=4):
        def body(b):
            for i in range(4):
                r = 4 * b + i
                row = src[r].astype(F32)
                x3[r + 1, :, 0:CH] = pltpu.roll(row, 1, 0).astype(BF16)
                x3[r + 1, :, CH : 2 * CH] = src[r]
                x3[r + 1, :, 2 * CH : 3 * CH] = pltpu.roll(row, COLS - 1, 0).astype(BF16)

        loop(low, high, body)

    def halo_finish(src, k, x3):
        await_bytes(halo.at[k], halo_recv.at[k])
        await_bytes(halo.at[k], halo_send.at[k])
        first = iota((16, CH), 0) == 0
        last = iota((16, CH), 0) == 15
        left = halo_col(k, 0, 0)[...].astype(F32)
        right = halo_col(k, 1, 0)[...].astype(F32)
        for r in range(ROWS):
            low = x3[r + 1, 0:16, 0:CH].astype(F32)
            x3[r + 1, 0:16, 0:CH] = jnp.where(first, left[r : r + 1, :], low).astype(BF16)
            high = x3[r + 1, COLS - 16 : COLS, 2 * CH : 3 * CH].astype(F32)
            x3[r + 1, COLS - 16 : COLS, 2 * CH : 3 * CH] = jnp.where(
                last, right[r : r + 1, :], high
            ).astype(BF16)
        spot = iota((COLS, CH), 0)
        for side, r, turn, pick, valid in (
            (0, 0, 1, ROWS - 1, lat > 0),
            (1, ROWS + 1, 2, 0, lat < N_LAT - 1),
        ):
            keep = jnp.where(valid, 1.0, 0.0).astype(F32)
            row = halo_row(k, side)[...].astype(F32) * keep
            lcorner = halo_col(k, 0, turn)[...].astype(F32)[pick : pick + 1, :] * keep
            rcorner = halo_col(k, 1, turn)[...].astype(F32)[pick : pick + 1, :] * keep
            x3[r, :, 0:CH] = jnp.where(spot == 0, lcorner, pltpu.roll(row, 1, 0)).astype(BF16)
            x3[r, :, CH : 2 * CH] = row.astype(BF16)
            x3[r, :, 2 * CH : 3 * CH] = jnp.where(
                spot == COLS - 1, rcorner, pltpu.roll(row, COLS - 1, 0)
            ).astype(BF16)

    def conv(x3, k, finish, flip=False, low=0, high=4):
        if flip:
            taps = [
                conv_w[k, 2 - p, (2 - q) * CH : (3 - q) * CH, :] for p in range(3) for q in range(3)
            ]
            taps = jnp.concatenate(taps, axis=1)
        else:
            taps = conv_w[k].reshape(9 * CH, CH)
        for b in range(low, high):
            near = [x3[4 * b + p : 4 * b + p + 4].reshape(4 * COLS, 3 * CH) for p in range(3)]
            near = jnp.concatenate(near, axis=1)
            if flip:
                acc = lax.dot_general(near, taps, NT, preferred_element_type=F32)
            else:
                acc = dot(near, taps)
            finish(slice(4 * b, 4 * b + 4), acc)

    def tile4(x):
        return x.reshape(4 * COLS, CH)

    def grid4(x):
        return x.reshape(4, COLS, CH)

    def turn_act(act, act_t):
        for r in range(ROWS):
            act_t[:, r * COLS : (r + 1) * COLS] = act[r].T

    def own_meta():
        line, lane = iota((32, 128), 0), iota((32, 128), 1)
        own_four = jnp.where(lax.div(lane, 4) == line, live_counts[...].astype(F32), 0.0).astype(BF16)
        to_slots = jnp.where(
            lax.rem(iota((128, 128), 0), 4) == lax.div(iota((128, 128), 1), 32), 1.0, 0.0
        ).astype(BF16)
        live = lax.rem(lane, 32).astype(F32) < dot(own_four, to_slots)
        cell, sub = cells[...], subs[...]
        u, v = sub >> 3, sub & 7
        u = jnp.where(u >= 4, u - 4, 3 - u)
        v = jnp.where(v >= 4, v - 4, 3 - v)
        row = cell >> 7
        fields = [
            jnp.where(live, (cell & 127).astype(F32), 255.0),
            (row * 16 + u * 4 + v).astype(F32),
            ((2 * u + 1) * (2 * u + 1) + (2 * v + 1) * (2 * v + 1)).astype(F32),
            row.astype(F32),
        ]
        for i in range(4):
            mixed = jnp.zeros((32, 128), F32)
            for f in range(4):
                shift = (f - i) * 32 % 128
                turned_field = pltpu.roll(fields[f], shift, 1) if shift else fields[f]
                mixed = jnp.where(lax.div(lane, 32) == f, turned_field, mixed)
            for r in range(32):
                meta_own[i, r] = mixed[r : r + 1, :]

    pl.semaphore_wait(barrier, 72)
    pair_other.start()
    own_meta()
    meta_start(0)
    cot_copy.wait()
    halo_pack(cot, 0)
    halo_start(cot, 0)
    meta_wait(0)
    meta_start(1)
    widen(cot, x3_cot, 0, 2)
    pair_own.wait()
    pair_other.wait()
    pltpu.make_async_copy(queue.at[chip], vals.at[0], a2a_recv.at[0]).start()
    for j in range(1, 16):
        send_slot(j)
    meta_wait(1)
    meta_start(2)
    for j in range(16, 64):
        send_slot(j)
    widen(cot, x3_cot, 2, 4)
    conv_copy.wait()
    embed_t[...] = embed_w[...].T
    halo_finish(cot, 0, x3_cot)

    def keep_back(rows, acc):
        back[rows] = grid4(acc)

    conv(x3_cot, 1, keep_back, flip=True)
    meta_wait(2)

    slot_mask = jnp.where(
        lax.rem(iota((CAP, 128), 1), 32) == iota((CAP, 128), 0), 1.0, 0.0
    ).astype(F32)
    spread = jnp.where(
        lax.div(iota((128, 512), 0), 32) == lax.div(iota((128, 512), 1), 128), 1.0, 0.0
    ).astype(BF16)
    lane, line = iota((COLS + 16, 128), 1), iota((COLS + 16, 128), 0)
    pick = jnp.where(lax.div(lane, 32) == jnp.where(line < COLS, 0, 3), 1.0, 0.0).astype(BF16)
    decay = sharp[...] * (-1.0 / 256.0)

    for g in range(4):
        for s in range(32):
            sx, sy, sz = source(g * 16 + s // 2)
            line = jnp.broadcast_to(meta[sy * 2 + s % 2, sx, sz], (CAP, 128)) * slot_mask
            tmeta[s * CAP : s * CAP + CAP, :] = line.astype(BF16)
        await_bytes(vals.at[pl.ds(g * 16, 16)], a2a_recv.at[g])

        for b in range(4):
            at = slice(b * 256, b * 256 + 256)
            of = slice(g * GROUP + b * 256, g * GROUP + b * 256 + 256)
            wide = dot(tmeta[at, :], spread)
            colb[of, :] = wide[:, 0:128].astype(BF16)
            rowb[of, :] = wide[:, 384:512].astype(BF16)
            rk_of = jnp.concatenate([wide[:, 128:256]] * 2, axis=1)
            radius = jnp.concatenate([wide[:, 256:384]] * 2, axis=1)
            rk[at, :] = jnp.where(
                rk_of == iota((256, 256), 1).astype(F32), 1.0, 0.0
            ).astype(BF16)
            w = jnp.exp(radius * decay)
            weight[of, :] = w
            ew[at, :] = (dot(vals[g * 16 + 4 * b : g * 16 + 4 * b + 4].reshape(256, VALS), embed_w[...]) * w).astype(BF16)

        both = lax.dot_general(pick, tmeta[...], NT, preferred_element_type=F32)
        colhot[...] = jnp.where(
            both[0:COLS] == iota((COLS, GROUP), 0).astype(F32), 1.0, 0.0
        ).astype(BF16)
        rowl[...] = both[COLS : COLS + 16]
        tally = dot(colhot[...], rk[...])
        counts[...] = tally if g == 0 else counts[...] + tally

        hot = colhot[...].reshape(8, 16, GROUP)
        for b in range(4):
            rows = []
            for r in range(4 * b, 4 * b + 4):
                mask = jnp.where(rowl[...] == float(r), 1.0, 0.0).astype(BF16)
                rows.append((hot * mask[None]).reshape(COLS, GROUP))
            at = slice(b * 512, b * 512 + 512)
            here = dot(jnp.concatenate(rows, axis=0), ew[...])
            placed[at, :] = here if g == 0 else placed[at, :] + here

    kind = lax.rem(iota((256, CH), 0), 16)
    half_u, half_v = 2 * lax.div(kind, 4) + 1, 2 * lax.rem(kind, 4) + 1
    table = jnp.exp((half_u * half_u + half_v * half_v).astype(F32) * decay)
    table_hi = table.astype(BF16)
    table_lo = (table - table_hi.astype(F32)).astype(BF16)
    tables = jnp.concatenate([table_hi, table_lo], axis=0)
    row_of_lane = lax.div(iota((COLS, 256), 1), 16)
    for b in range(4):
        rows = []
        for r in range(4 * b, 4 * b + 4):
            rows.append(jnp.where(row_of_lane == r, counts[...], 0.0).astype(BF16))
        tally = jnp.concatenate(rows, axis=0)
        recip = 1.0 / (dot(jnp.concatenate([tally, tally], axis=1), tables) + 1.0)
        at = slice(4 * b, 4 * b + 4)
        inv[at] = grid4(recip)
        value = (placed[b * 512 : b * 512 + 512, :] * recip).astype(BF16)
        base[at] = grid4(value)
        x = value.astype(F32)
        s = sigmoid(x)
        act_zero[at] = grid4((x * s).astype(BF16))
        bend[at] = grid4(s * (1.0 + x * (1.0 - s)))

    halo_pack(act_zero, 1)
    halo_start(act_zero, 1)
    widen(act_zero, x3_act)
    turn_act(act_zero, zero_t)
    halo_finish(act_zero, 1, x3_act)

    def keep_mid(rows, acc):
        value = (tile4(base[rows]).astype(F32) + acc).astype(BF16)
        mid[rows] = grid4(value)
        x = value.astype(F32)
        s = sigmoid(x)
        act_one[rows] = grid4((x * s).astype(BF16))
        slope = s * (1.0 + x * (1.0 - s))
        grad = tile4(cot[rows]).astype(F32) + tile4(back[rows]) * slope
        gmid[rows] = grid4(grad.astype(BF16))

    conv(x3_act, 0, keep_mid)
    halo_pack(gmid, 2)
    halo_start(gmid, 2)
    halo_pack(act_one, 3)
    halo_start(act_one, 3)

    def kernel_grad(act_t, x3, k):
        for p in range(3):
            block = dot(act_t[...], x3[2 - p : 2 - p + ROWS].reshape(CELLS, 3 * CH))
            for q in range(3):
                for h in range(2):
                    n, lanes = 6 * p + 2 * q + h, (2 - q) * CH + h * 128
                    at = n % 3 * CH
                    grads[k, n // 6, n // 3 % 2, at : at + CH, :] = block[
                        :, lanes : lanes + 128
                    ].astype(BF16)

    coords = {"x": xi, "y": yi, "z": lat}
    orders = (("x", "y", "z"), ("y", "z", "x"), ("z", "x", "y"))

    def along(axis, c):
        cx, cy, cz = [c if axis == n else coords[n] for n in ("x", "y", "z")]
        return cz, cx * 8 + cy * 2 + ci

    def turned(axis, d):
        return {"x": to_x, "y": to_y, "z": to_z}[axis][d]

    def part_copies(k, stage):
        sems = (ar_send.at[k, stage], ar_recv.at[k, stage])
        if stage == 0:
            return [remote(grads.at[k, :, 1 - ci], p0.at[k], *sems, lat, other_core)]
        if stage == 6:
            half = total.at[k, :, ci]
            return [remote(half, half, *sems, lat, other_core)]
        copies = []
        for a, order in enumerate(orders):
            quarter = coords[order[0]] * QUARTER
            shard = quarter + coords[order[1]] * SHARD
            axis = order[{1: 0, 2: 1, 3: 2, 4: 1, 5: 0}[stage]]
            for d in (1, 3, 2):
                c = turned(axis, d)
                if stage == 1:
                    src, dst = s1.at[k, a, aligned(c * QUARTER, QUARTER, 16)], p1.at[k, a, d - 1]
                elif stage == 2:
                    src, dst = s2.at[k, a, aligned(c * SHARD, SHARD, 16)], p2.at[k, a, d - 1]
                elif stage == 3:
                    src, dst = s3.at[k, a], p3.at[k, a, coords[axis]]
                elif stage == 4:
                    src = dst = total.at[k, a, ci, aligned(shard, SHARD, 16)]
                else:
                    src = dst = total.at[k, a, ci, aligned(quarter, QUARTER, 16)]
                copies.append(remote(src, dst, *sems, *along(axis, c)))
        return copies

    def ar_start(k, stage):
        for copy in part_copies(k, stage):
            copy.start()

    def ar_finish(k, stage):
        amount = (p0, p1, p2, p2, p2, p1, p0)[stage].at[k]
        await_bytes(amount, ar_recv.at[k, stage])
        await_bytes(amount, ar_send.at[k, stage])
        for a, order in enumerate(orders):
            if stage == 0:
                here = grads[k, a, ci].astype(F32)
                s1[k, a] = (here + p0[k, a].astype(F32)).astype(BF16)
            elif stage in (1, 2):
                size = QUARTER if stage == 1 else SHARD
                src, came, dst = (s1, p1, s2) if stage == 1 else (s2, p2, s3)
                at = aligned(coords[order[stage - 1]] * size, size, 16)
                here = src[k, a, at, :].astype(F32)
                for d in range(3):
                    here += came[k, a, d].astype(F32)
                dst[k, a] = here.astype(BF16)
            elif stage == 3:
                p3[k, a, coords[order[2]]] = s3[k, a]
                whole = p3[k, a, 0].astype(F32)
                for d in range(1, 4):
                    whole += p3[k, a, d].astype(F32)
                quarter = coords[order[0]] * QUARTER
                at = aligned(quarter + coords[order[1]] * SHARD, SHARD, 16)
                total[k, a, ci, at, :] = whole.astype(BF16)

    def ar_step(k, stage):
        ar_finish(k, stage)
        ar_start(k, stage + 1)

    def ar_leave(k):
        return pltpu.make_async_copy(total.at[k], grads_out.at[k], local_sem.at[3 if k else 6])

    turn_act(act_one, act_t)
    kernel_grad(act_t, x3_cot, 1)
    ar_start(1, 0)
    widen(gmid, x3_mid)
    halo_finish(gmid, 2, x3_mid)
    ar_step(1, 0)
    kernel_grad(zero_t, x3_mid, 0)
    ar_start(0, 0)

    def keep_gp(rows, acc):
        grad = tile4(gmid[rows]).astype(F32) + acc * tile4(bend[rows])
        gp[rows.start * COLS : rows.stop * COLS, :] = (
            grad * tile4(inv[rows])
        ).astype(BF16)

    conv(x3_mid, 0, keep_gp, flip=True, low=0, high=2)
    ar_step(1, 1)
    ar_step(0, 0)
    conv(x3_mid, 0, keep_gp, flip=True, low=2, high=4)

    esum[...] = jnp.zeros_like(esum)

    def vg_copy(j):
        sx, sy, sz = source(j)
        return remote(vg.at[j], relay.at[chip], vg_send, vg_recv, sz, sx * 8 + sy * 2 + ci)

    def gather(b):
        at = slice(b * 512, b * 512 + 512)
        chips = slice(b * 8, b * 8 + 8)
        hot = jnp.where(
            colb[at, :].astype(F32) == iota((512, COLS), 1).astype(F32), 1.0, 0.0
        ).astype(BF16)
        row_of = rowb[at, :]
        pieces = [
            jnp.where(row_of == jnp.array(r, BF16), hot, jnp.zeros_like(hot)) for r in range(ROWS)
        ]
        found = dot(jnp.concatenate(pieces, axis=1), gp[...])
        grad = (found * weight[at, :]).astype(BF16)
        vg[chips] = dot(grad, embed_t[...]).astype(BF16).reshape(8, 2, CAP, VALS)
        own = vals[chips].reshape(512, VALS)
        esum[...] += lax.dot_general(own, grad, TN, preferred_element_type=F32)
        for j in range(8 * b, 8 * b + 8):
            if j == 0:
                pltpu.make_async_copy(vg.at[0], relay.at[chip], vg_recv).start()
            else:
                vg_copy(j).start()

    gather(0)
    gather(1)
    ar_step(1, 2)
    gather(2)
    ar_step(0, 1)
    gather(3)
    ar_step(1, 3)
    gather(4)
    ar_step(0, 2)
    gather(5)
    ar_step(1, 4)
    gather(6)
    ar_step(0, 3)
    gather(7)
    ar_step(0, 4)

    member = yc
    column = xi * 4 + lat

    def embed_copies(stage):
        copies = []
        for d in range(1, 16 if stage == 1 else 8):
            if stage == 1:
                c = lax.rem(column + d, 16)
                tlat, tlon = lax.rem(c, 4), lax.div(c, 4) * 8 + member
                src, dst = esum.at[aligned(member * 16, 16, 16)], qe.at[column]
            else:
                m = lax.rem(member + d, 8)
                tlat, tlon = lat, xi * 8 + m
                if stage == 0:
                    src, dst = esum.at[aligned(m * 16, 16, 16)], pe.at[d - 1]
                else:
                    src = dst = etotal.at[aligned(member * 16, 16, 16)]
            copies.append(remote(src, dst, em_send.at[stage], em_recv.at[stage], tlat, tlon))
        return copies

    def embed_start(stage):
        for copy in embed_copies(stage):
            copy.start()

    def embed_wait(stage):
        amount = qe.at[pl.ds(0, 15)] if stage == 1 else pe
        await_bytes(amount, em_recv.at[stage])
        await_bytes(amount, em_send.at[stage])

    embed_start(0)
    widen(act_one, x3_act)
    halo_finish(act_one, 3, x3_act)

    def keep_enc(rows, acc):
        enc[rows] = grid4((tile4(mid[rows]).astype(F32) + acc).astype(BF16))

    conv(x3_act, 1, keep_enc, low=0, high=1)
    ar_step(1, 5)
    embed_wait(0)
    own_rows = aligned(member * 16, 16, 16)
    mine = esum[own_rows, :]
    for d in range(7):
        mine += pe[d]
    esum[own_rows, :] = mine
    embed_start(1)
    conv(x3_act, 1, keep_enc, low=1, high=2)
    ar_step(0, 5)
    conv(x3_act, 1, keep_enc, low=2, high=3)
    ar_finish(1, 6)
    ar_leave(1).start()
    embed_wait(1)
    qe[column] = esum[own_rows, :]
    whole = qe[0]
    for d in range(1, 16):
        whole += qe[d]
    etotal[own_rows, :] = whole
    embed_start(2)
    await_bytes(relay, vg_recv)
    vg_own = pltpu.make_async_copy(relay.at[:, ci], vg_out.at[:, ci], local_sem.at[5])
    vg_own.start()
    vg_other = remote(
        relay.at[:, 1 - ci], vg_out.at[:, ci], pair_send.at[1], pair_recv.at[1], lat, other_core
    )
    vg_other.start()
    conv(x3_act, 1, keep_enc, low=3, high=4)
    enc_copy = pltpu.make_async_copy(enc, enc_out, local_sem.at[2])
    enc_copy.start()
    ar_finish(0, 6)
    ar_leave(0).start()
    embed_wait(2)
    embed_out[...] = etotal[...] * (1.0 / 512.0)
    for g in range(4):
        await_bytes(vals.at[pl.ds(0, 15 if g == 0 else 16)], a2a_send.at[g])
    for stage in range(3):
        meta_sent(stage)
    await_bytes(vg.at[pl.ds(0, 63)], vg_send)
    vg_own.wait()
    vg_other.wait()
    enc_copy.wait()
    ar_leave(1).wait()
    ar_leave(0).wait()


def hand_over(
    enc_in, vg_in, grads_in, embed_in, enc_out, vg_out, grads_out, embed_out,
    enc, vg, embed, narrow, wide, in_sem, out_sem,
):
    steps = []
    for i in range(6):
        src, dst = slice(i % 3 * PART, (i % 3 + 1) * PART), slice(i * 3 * CH, (i + 1) * 3 * CH)
        k = i // 3
        steps.append(
            (grads_in.at[k, src], narrow.at[k, src], wide.at[dst], grads_out.at[dst], (k, src, dst))
        )
    steps.append((enc_in, enc, enc, enc_out, None))
    steps.append((vg_in, vg, vg, vg_out, None))
    steps.append((embed_in, embed, embed, embed_out, None))
    moves = [
        pltpu.make_async_copy(step[0], step[1], in_sem.at[i]) for i, step in enumerate(steps)
    ]
    for move in moves:
        move.start()
    results = []
    for i, (_, _, src, dst, at) in enumerate(steps):
        moves[i].wait()
        if at is not None:
            k, rows, to = at
            for n in range(6):
                half = slice(rows.start + n * CH, rows.start + n * CH + CH)
                into = slice(to.start + n // 2 * CH, to.start + (n // 2 + 1) * CH)
                lanes = slice(n % 2 * 128, n % 2 * 128 + 128)
                wide[into, lanes] = narrow[k, half, :].astype(F32) * (1.0 / 512.0)
        results.append(pltpu.make_async_copy(src, dst, out_sem.at[i]))
        results[i].start()
    for copy in results:
        copy.wait()


def on_device(
    obs_values, obs_cells, obs_subcell, slot_counts, sharpness, embed_weight, conv_weight, cotangent
):
    anywhere = pl.BlockSpec(memory_space=pl.ANY)
    vmem = pl.BlockSpec(memory_space=pltpu.VMEM)
    grid = (ROWS, COLS, CH)
    wide = (ROWS + 2, COLS, 3 * CH)
    dma = pltpu.SemaphoreType.DMA
    scratch = [
        pltpu.VMEM((64, 2, CAP, VALS), BF16),
        pltpu.VMEM((64, 2, CAP, VALS), BF16),
        pltpu.VMEM((64, 2, CAP, VALS), BF16),
        pltpu.VMEM((4, 32, 1, 128), F32),
        pltpu.VMEM((4, 4, 8, 1, 128), F32),
        pltpu.VMEM((4, 4, 4, 2, 1, 128), F32),
        pltpu.VMEM((8, 4, 4, 1, 128), F32),
        pltpu.VMEM((GROUP, 128), BF16),
        pltpu.VMEM((OBS, 128), BF16),
        pltpu.VMEM((OBS, 128), BF16),
        pltpu.VMEM((OBS, CH), F32),
        pltpu.VMEM((GROUP, CH), BF16),
        pltpu.VMEM((GROUP, 256), BF16),
        pltpu.VMEM((COLS, GROUP), BF16),
        pltpu.VMEM((16, GROUP), F32),
        pltpu.VMEM((CELLS, CH), F32),
        pltpu.VMEM((COLS, 256), F32),
        pltpu.VMEM(grid, F32),
        pltpu.VMEM(grid, BF16),
        pltpu.VMEM((2, 3, 3 * CH, CH), BF16),
        pltpu.VMEM((CH, VALS), BF16),
        pltpu.VMEM(grid, F32),
        pltpu.VMEM(grid, F32),
        pltpu.VMEM(grid, BF16),
        pltpu.VMEM(grid, BF16),
        pltpu.VMEM(grid, BF16),
        pltpu.VMEM(grid, BF16),
        pltpu.VMEM(grid, BF16),
        pltpu.VMEM((CELLS, CH), BF16),
        pltpu.VMEM((CH, CELLS), BF16),
        pltpu.VMEM((CH, CELLS), BF16),
        pltpu.VMEM(wide, BF16),
        pltpu.VMEM(wide, BF16),
        pltpu.VMEM(wide, BF16),
        pltpu.VMEM((4, 2 * COLS + 6 * 16, CH), BF16),
        pltpu.VMEM((4, 2, 16, CH), BF16),
        pltpu.VMEM((2, 16, CH), F32),
        pltpu.VMEM((64, 2, CAP, VALS), BF16),
        pltpu.VMEM((2, 3, 2, HALF, 128), BF16),
        pltpu.VMEM((2, 3, 2, HALF, 128), BF16),
        pltpu.VMEM((2, 3, HALF, 128), BF16),
        pltpu.VMEM((2, 3, HALF, 128), BF16),
        pltpu.VMEM((2, 3, 3, QUARTER, 128), BF16),
        pltpu.VMEM((2, 3, QUARTER, 128), BF16),
        pltpu.VMEM((2, 3, 3, SHARD, 128), BF16),
        pltpu.VMEM((2, 3, SHARD, 128), BF16),
        pltpu.VMEM((2, 3, 4, SHARD, 128), BF16),
        pltpu.VMEM((VALS, CH), F32),
        pltpu.VMEM((7, 16, CH), F32),
        pltpu.VMEM((16, 16, CH), F32),
        pltpu.VMEM((VALS, CH), F32),
        pltpu.VMEM(grid, BF16),
        dma((7,)),
        dma((2,)),
        dma((2,)),
        dma((4,)),
        dma((4,)),
        dma((3,)),
        dma((3,)),
        dma,
        dma,
        dma((4,)),
        dma((4,)),
        dma((2, 7)),
        dma((2, 7)),
        dma((3,)),
        dma((3,)),
    ]
    encoded, value_grads, grads, embed_total = pl.pallas_call(
        kernel,
        out_shape=(
            jax.ShapeDtypeStruct(grid, BF16),
            jax.ShapeDtypeStruct((64, 2, CAP, VALS), BF16),
            jax.ShapeDtypeStruct((2, 3, 2, HALF, 128), BF16),
            jax.ShapeDtypeStruct((VALS, CH), F32),
        ),
        in_specs=[anywhere, vmem, vmem, vmem, vmem, vmem, anywhere, anywhere],
        out_specs=(anywhere, anywhere, anywhere, vmem),
        scratch_shapes=scratch,
        compiler_params=pltpu.CompilerParams(
            collective_id=0, has_side_effects=True, vmem_limit_bytes=60 * 1024 * 1024
        ),
        cost_estimate=pl.CostEstimate(
            flops=30_000_000_000, bytes_accessed=20_000_000, transcendentals=4_000_000
        ),
    )(
        obs_values.reshape(64, 2, CAP, VALS),
        obs_cells.reshape(32, 128),
        obs_subcell.reshape(32, 128),
        slot_counts,
        sharpness.reshape(1, CH),
        embed_weight,
        conv_weight.reshape(2, 3, 3 * CH, CH),
        cotangent,
    )
    encoded, value_grads, conv_grads, embed_grads = pl.pallas_call(
        hand_over,
        out_shape=(
            jax.ShapeDtypeStruct(grid, BF16),
            jax.ShapeDtypeStruct((64, 2, CAP, VALS), BF16),
            jax.ShapeDtypeStruct((3 * PART, CH), F32),
            jax.ShapeDtypeStruct((VALS, CH), F32),
        ),
        in_specs=[anywhere] * 4,
        out_specs=(anywhere,) * 4,
        scratch_shapes=[
            pltpu.VMEM(grid, BF16),
            pltpu.VMEM((64, 2, CAP, VALS), BF16),
            pltpu.VMEM((VALS, CH), F32),
            pltpu.VMEM((2, 3 * PART, 128), BF16),
            pltpu.VMEM((3 * PART, CH), F32),
            dma((9,)),
            dma((9,)),
        ],
        compiler_params=pltpu.CompilerParams(vmem_limit_bytes=60 * 1024 * 1024),
    )(encoded, value_grads, grads.reshape(2, 3 * PART, 128), embed_total)
    return (
        encoded,
        value_grads.reshape(OBS, VALS),
        conv_grads.reshape(2, 3, 3, CH, CH),
        embed_grads,
    )


def solution(mesh):
    placed = (
        P(("lat", "lon"), None),
        P(("lat", "lon")),
        P(("lat", "lon")),
        P(("lat", "lon"), None),
        P(),
        P(),
        P(),
        P("lat", "lon", None),
    )
    return jax.shard_map(
        on_device,
        mesh=mesh,
        in_specs=placed,
        out_specs=(P("lat", "lon", None), P(("lat", "lon"), None), P(), P()),
        check_vma=False,
    )
```
